32 devices in a mesh: seq: 8 (over y, x, core), batch: 4 (over z).
Axes of the slice: x: 2, y: 2, z: 4, core: 2. Of those that a mesh axis runs over, the one named last changes fastest.
Arguments:
- tokens: bfloat16 [16, 1024, 768], P('batch', 'seq'), may hold values from -6 to 6
- first_gain: float32 [768], replicated, may hold values from 0.25 to 1.75
- first_shift: float32 [768], replicated, may hold values from -1.75 to 1.75
- mixer_input: bfloat16 [768, 2304], replicated, may hold values from -0.21875 to 0.21875
- conv_kernel: bfloat16 [256, 768], replicated, may hold values from -0.375 to 0.375
- mixer_output: bfloat16 [768, 768], replicated, may hold values from -0.375 to 0.375
- second_gain: float32 [768], replicated, may hold values from 0.25 to 1.75
- second_shift: float32 [768], replicated, may hold values from -1.75 to 1.75
- widen_weight: bfloat16 [768, 3072], replicated, may hold values from -0.21875 to 0.21875
- narrow_weight: bfloat16 [3072, 768], replicated, may hold values from -0.15625 to 0.15625
- cotangent: bfloat16 [16, 1024, 768], P('batch', 'seq'), may hold values from -6 to 6
Outputs:
- block_output: bfloat16 [16, 1024, 768], P('batch', 'seq')
- grad_tokens: bfloat16 [16, 1024, 768], P('batch', 'seq')
- grad_first_gain: float32 [768], P('seq')
- grad_first_shift: float32 [768], P('seq')
- grad_mixer_input: float32 [768, 2304], P('seq')
- grad_conv_kernel: float32 [256, 768], P('seq')
- grad_mixer_output: float32 [768, 768], P('seq')
- grad_second_gain: float32 [768], P('seq')
- grad_second_shift: float32 [768], P('seq')
- grad_widen: float32 [768, 3072], P('seq')
- grad_narrow: float32 [3072, 768], P('seq')
The draws below stay inside these ranges and needn't reach their ends.
All inputs are finite; a program needn't handle non-finite values.
Results may differ from the reference program's by a relative error of at most 0.0085.
Values sent between devices are 32-bit elements; how exact they have to be, the bound alone decides.
No kernel may reach another device: no remote copies, remote signals or barrier semaphores. Data moves between devices by JAX's collectives and lax.ppermute only.
A program may use at most 192 MiB of HBM per device.

```python
import math
import jax
import jax.numpy as jnp
from jax import lax

D = 768
FF = 3072
L = 1024
KT = 256
SEQS = 16


def strengthened(result, own_key, source, target, parts, factor):
    owner, partner = [(jnp.arange(result.shape[axis_at]) // (result.shape[axis_at] // parts)).reshape([-1 if axis == axis_at else 1 for axis in range(result.ndim)]) for axis_at in (source, target)]
    chosen = jax.random.permutation(own_key, parts)[partner]
    strong = (owner == chosen) | (owner == (partner + parts // 2) % parts)
    return jnp.where(strong, factor * result, result)


def levels(rng, dims, cuts, low, largest):
    gain, own = 1.0, jax.random.fold_in(rng, 6)
    for axis_at, parts in cuts:
        steps = jnp.exp(jax.random.uniform(jax.random.fold_in(own, axis_at), (parts,), jnp.float32, low / len(cuts), largest / len(cuts)))
        gain = gain * jnp.repeat(steps, dims[axis_at] // parts).reshape([-1 if axis == axis_at else 1 for axis in range(len(dims))])
    return gain


def scatter_about(rng, extent, deviation, reach, shards=(), dtype=jnp.bfloat16):
    gain = levels(rng, extent, shards, -0.22, 0.18) if shards else 1.0
    values = jax.random.normal(rng, extent, jnp.float32) * deviation * gain
    return jnp.minimum(jnp.maximum(values, -reach), reach).astype(dtype)


def noise_with(own_key, shape, width, bound, cuts, heavy, held_as=jnp.bfloat16):
    array = width * jax.random.normal(own_key, shape, jnp.float32)
    if cuts:
        array = array * levels(own_key, shape, cuts, -0.22, 0.18)
    return jnp.clip(strengthened(array, jax.random.fold_in(own_key, 3), *heavy), -bound, bound).astype(held_as)


def setup_inputs(seed: int = 0) -> dict:
    seeds = jax.random.split(jax.random.key(seed), 12)
    return {
        "tokens": noise_with(seeds[0], (SEQS, L, D), 1.0, 6.0, ((0, 4), (1, 8)), (1, 2, 8, 2.0)),
        "first_gain": jnp.clip(1.0 + 0.15 * jax.random.normal(seeds[1], (D,), jnp.float32), 0.25, 1.75),
        "first_shift": scatter_about(seeds[2], (D,), 0.3, 1.75, (), jnp.float32),
        "mixer_input": scatter_about(seeds[3], (D, 3 * D), D ** -0.5, 0.21875),
        "conv_kernel": scatter_about(seeds[4], (KT, D), KT ** -0.5, 0.375),
        "mixer_output": scatter_about(seeds[5], (D, D), (D // 3) ** -0.5, 0.375),
        "second_gain": jnp.clip(1.0 + 0.15 * jax.random.normal(seeds[6], (D,), jnp.float32), 0.25, 1.75),
        "second_shift": scatter_about(seeds[7], (D,), 0.3, 1.75, (), jnp.float32),
        "widen_weight": scatter_about(seeds[8], (D, FF), D ** -0.5, 0.21875),
        "narrow_weight": scatter_about(seeds[9], (FF, D), (FF // 2) ** -0.5, 0.15625),
        "cotangent": scatter_about(seeds[10], (SEQS, L, D), 1.0, 6.0, ((0, 4), (1, 8))),
    }


norm_epsilon = 1e-05
shrink_level = 0.003
highest = lax.Precision.HIGHEST

@jax.custom_vjp
def low(v):
    return lax.optimization_barrier(v.astype(jnp.bfloat16)).astype(jnp.float32)

@jax.custom_vjp
def low_back(v):
    return v

def low_keep(v):
    return (low(v), None)

def low_pass(kept, grad):
    return (grad,)

def back_keep(v):
    return (v, None)

def back_low(kept, grad):
    return (low(grad),)
low.defvjp(low_keep, low_pass)
low_back.defvjp(back_keep, back_low)

def norm_apply(values, scale_row, shift_row):
    centered = values - lax.optimization_barrier(jnp.mean(values, axis=-1, keepdims=True))
    inverse = lax.rsqrt(lax.optimization_barrier(jnp.mean(centered * centered, axis=-1, keepdims=True)) + norm_epsilon)
    return centered * inverse * scale_row + shift_row

def shape_kernel(raw_kernel):
    shrunk = raw_kernel - shrink_level * jnp.tanh(raw_kernel / shrink_level)
    padded = jnp.pad(shrunk, ((1, 1), (0, 0)))
    return (padded[:-2] + padded[1:-1] + padded[2:]) / 3.0

def exact_gelu(values):
    return 0.5 * values * (1.0 + lax.erf(values / math.sqrt(2.0)))

def causal_convolve(signal, kernel_taps):
    length = signal.shape[0]
    spectrum = jnp.fft.rfft(signal, n=2 * length, axis=0) * jnp.fft.rfft(kernel_taps, n=2 * length, axis=0)
    return jnp.fft.irfft(spectrum, n=2 * length, axis=0)[:length]

def block_forward(tokens_row, first_gain, first_shift, mixer_input, conv_kernel, mixer_output, second_gain, second_shift, widen_weight, narrow_weight):
    normed = low(norm_apply(tokens_row, first_gain, first_shift))
    mixed_rows = low_back(jnp.dot(normed, mixer_input, precision=highest))
    query_rows = mixed_rows[:, :D]
    key_rows = mixed_rows[:, D:2 * D]
    value_rows = mixed_rows[:, 2 * D:]
    convolved = causal_convolve(key_rows * value_rows, shape_kernel(conv_kernel))
    gated = low(query_rows * convolved)
    middle = tokens_row + low_back(jnp.dot(gated, mixer_output, precision=highest))
    second = low(norm_apply(middle, second_gain, second_shift))
    hidden = low_back(jnp.dot(second, widen_weight, precision=highest))
    active = low(exact_gelu(hidden))
    return middle + low_back(jnp.dot(active, narrow_weight, precision=highest))

def reference(tokens, first_gain, first_shift, mixer_input, conv_kernel, mixer_output, second_gain, second_shift, widen_weight, narrow_weight, cotangent):
    weights = (first_gain.astype(jnp.float32), first_shift.astype(jnp.float32), mixer_input.astype(jnp.float32), conv_kernel.astype(jnp.float32), mixer_output.astype(jnp.float32), second_gain.astype(jnp.float32), second_shift.astype(jnp.float32), widen_weight.astype(jnp.float32), narrow_weight.astype(jnp.float32))

    def one_sequence(totals, seq_pair):
        seq_tokens, seq_cot = seq_pair
        output, pullback = jax.vjp(block_forward, seq_tokens.astype(jnp.float32), *weights)
        gradients = pullback(seq_cot.astype(jnp.float32))
        totals = tuple((total + extra for total, extra in zip(totals, gradients[1:])))
        return (totals, (output.astype(jnp.bfloat16), gradients[0].astype(jnp.bfloat16)))
    start = tuple((jnp.zeros(weight.shape, jnp.float32) for weight in weights))
    totals, (outputs, input_grads) = lax.scan(one_sequence, start, (tokens, cotangent))
    return (outputs, input_grads, totals[0], totals[1], totals[2], totals[3], totals[4], totals[5], totals[6], totals[7], totals[8])
```

```python
import functools
import math

import jax
import jax.numpy as jnp
import numpy as np
from jax import lax
from jax.experimental import pallas as pl
from jax.experimental.pallas import tpu as pltpu
from jax.sharding import PartitionSpec as P

norm_epsilon = 1e-05
shrink_level = 0.003
highest = lax.Precision.HIGHEST
low_type = jnp.bfloat16


def split_low(table):
    high = table.astype(np.float32).astype(jnp.bfloat16)
    rest = (table - high.astype(np.float64)).astype(np.float32).astype(jnp.bfloat16)
    return high, rest


@functools.lru_cache(maxsize=None)
def half_tables(block):
    order = np.concatenate([np.arange(0, block, 2), np.arange(1, block, 2)])
    theta = np.pi * (2 * order + 1) / (2 * block)
    place = np.arange(block)
    early = theta[:, None] * place[None, :]
    late = theta[None, :] * (block + place[:, None])
    forward = np.concatenate([np.cos(early), -np.sin(early)], axis=0)
    inverse = np.concatenate([np.cos(late), -np.sin(late)], axis=1) / block
    return forward, inverse


def stacked_pair(table):
    high, rest = split_low(table)
    return np.concatenate([high, rest], axis=1)


def turn(spectrum, block):
    half = block // 2
    real, imag = spectrum[:block], spectrum[block:]
    return jnp.concatenate([imag[:half], -imag[half:], -real[:half], real[half:]], axis=0)


def turn_back(spectrum, block):
    half = block // 2
    first, last = spectrum[:block], spectrum[block:]
    return jnp.concatenate([-last[:half], last[half:], first[:half], -first[half:]], axis=0)


def twice(values):
    rounded = values.astype(low_type)
    return jnp.concatenate([rounded, rounded], axis=0)


def low_dot(left, right):
    return jnp.dot(left, right, preferred_element_type=jnp.float32)


def convolve_kernel(count, block, table_ref, high_ref, rest_ref, filter_ref, query_ref, *refs):
    block_refs, (convolved_ref, gated_ref) = refs[:count], refs[count:]
    real, imag = 0.0, 0.0
    for place in range(count):
        spectrum = low_dot(table_ref[...], twice(block_refs[place][0]))
        own_real, own_imag = spectrum[:block], spectrum[block:]
        filter_real = filter_ref[place, :block, :]
        filter_imag = filter_ref[place, block:, :]
        real += own_real * filter_real - own_imag * filter_imag
        imag += own_real * filter_imag + own_imag * filter_real
    total = jnp.concatenate([real, imag], axis=0).astype(low_type)
    convolved = low_dot(high_ref[...], total) + low_dot(rest_ref[...], total)
    convolved_ref[0] = convolved
    gated_ref[0] = (query_ref[0] * convolved).astype(low_type)


def pull_kernel(count, block, table_ref, high_ref, rest_ref, filter_ref, key_ref, value_ref, *refs):
    block_refs, (key_out_ref, value_out_ref) = refs[:count], refs[count:]
    real, imag = 0.0, 0.0
    for place in range(count):
        spectrum = low_dot(table_ref[...], twice(block_refs[place][0]))
        own_real, own_imag = spectrum[:block], spectrum[block:]
        filter_real = filter_ref[place, :block, :]
        filter_imag = filter_ref[place, block:, :]
        real += own_real * filter_real + own_imag * filter_imag
        imag += own_imag * filter_real - own_real * filter_imag
    total = jnp.concatenate([real, imag], axis=0).astype(low_type)
    pulled = low_dot(high_ref[...], total) + low_dot(rest_ref[...], total)
    key_out_ref[0] = (pulled * value_ref[0]).astype(low_type)
    value_out_ref[0] = (pulled * key_ref[0]).astype(low_type)


def filter_grad_kernel(count, block, table_ref, pull_table_ref, grad_ref, *refs):
    block_refs, out_ref = refs[:count], refs[count]

    @pl.when(pl.program_id(1) == 0)
    def _():
        out_ref[...] = jnp.zeros_like(out_ref)

    grad = low_dot(pull_table_ref[...], twice(grad_ref[0]))
    grad_real, grad_imag = grad[:block], grad[block:]
    for place in range(count):
        spectrum = low_dot(table_ref[...], twice(block_refs[place][0]))
        own_real, own_imag = spectrum[:block], spectrum[block:]
        out_ref[place, :block, :] += grad_real * own_real + grad_imag * own_imag
        out_ref[place, block:, :] += grad_imag * own_real - grad_real * own_imag


def full_spec(shape):
    return pl.BlockSpec(shape, lambda *place: (0,) * len(shape))


def convolve_call(body, blocks, tables, spectrum, extras, out_types):
    seqs, block, features = blocks[0].shape
    count = len(blocks)
    width = 256
    tile = pl.BlockSpec((1, block, width), lambda column, seq: (seq, 0, column))
    in_specs = [full_spec(table.shape) for table in tables]
    operands = list(tables)
    if spectrum is not None:
        in_specs.append(pl.BlockSpec((count, 2 * block, width), lambda column, seq: (0, 0, column)))
        operands.append(spectrum)
    in_specs += [tile] * (len(extras) + count)
    operands += list(extras) + list(blocks)
    if out_types is None:
        out_shape = jax.ShapeDtypeStruct((count, 2 * block, features), jnp.float32)
        out_specs = pl.BlockSpec((count, 2 * block, width), lambda column, seq: (0, 0, column))
    else:
        out_shape = [jax.ShapeDtypeStruct((seqs, block, features), kind) for kind in out_types]
        out_specs = [tile] * len(out_types)
    return pl.pallas_call(
        functools.partial(body, count, block),
        grid=(features // width, seqs),
        in_specs=in_specs,
        out_specs=out_specs,
        out_shape=out_shape,
        compiler_params=pltpu.CompilerParams(vmem_limit_bytes=48 * 2**20),
    )(*operands)


def partner_pairs(size, step):
    return [(place, place ^ step) for place in range(size)]


def swap(values, axis, step):
    return lax.ppermute(values, axis, partner_pairs(lax.axis_size(axis), step))


def gather_blocks(own, count, sign):
    size = lax.axis_size("seq")
    parity = lax.axis_index("seq") % 2
    blocks = {0: own}
    for pair in range(1, (count + 1) // 2 + 1):
        step = sign * 2 * pair
        pairs = [(a, a + step) for a in range(size) if 0 <= a + step < size]
        blocks[2 * pair] = lax.ppermute(own, "seq", pairs)
    evens = [(a, a ^ 1) for a in range(0, size, 2)]
    odds = [(a, a ^ 1) for a in range(1, size, 2)]
    near, far = (evens, odds) if sign > 0 else (odds, evens)
    for pair in range(1, (count + 1) // 2 + 1):
        blocks[2 * pair - 1] = lax.ppermute(blocks[2 * pair - 2], "seq", near) + lax.ppermute(
            blocks[2 * pair], "seq", far
        )
    return [blocks[place] for place in range(count + 1)]


def pick(values, dim, place):
    return lax.dynamic_index_in_dim(values, place, dim, keepdims=False)


def halve(values, dim, axis, bit):
    mine = (lax.axis_index(axis) >> bit) & 1
    moved = swap(pick(values, dim, 1 - mine), axis, 1 << bit)
    return pick(values, dim, mine) + moved


def seq_shares(values):
    size = lax.axis_size("seq")
    rows, width = values.shape
    bits = size.bit_length() - 1
    cells = values.reshape([2] * bits + [rows // size, width])
    cells = halve(cells, bits - 1, "seq", 0)
    middle = width // 2 // 128 * 128
    parts = []
    for part, order in (
        (cells[..., :middle], list(range(1, bits))),
        (cells[..., middle:], list(range(bits - 1, 0, -1))),
    ):
        left = sorted(order, reverse=True)
        for bit in order:
            part = halve(part, left.index(bit), "seq", bit)
            left.remove(bit)
        parts.append(part)
    return jnp.concatenate(parts, axis=-1)


def batch_total(values):
    size = lax.axis_size("batch")
    bits = size.bit_length() - 1
    rows, width = values.shape
    for bit in range(bits):
        values = halve(values.reshape(2, -1, width), 0, "batch", bit)
    for bit in reversed(range(bits)):
        mine = (lax.axis_index("batch") >> bit) & 1
        moved = swap(values, "batch", 1 << bit)
        first = jnp.where(mine == 0, values, moved)
        last = jnp.where(mine == 0, moved, values)
        values = jnp.concatenate([first, last], axis=0)
    return values


def reduce_all(values):
    return batch_total(seq_shares(values))


def norm_parts(values):
    centered = values - jnp.mean(values, axis=-1, keepdims=True)
    inverse = lax.rsqrt(jnp.mean(centered * centered, axis=-1, keepdims=True) + norm_epsilon)
    return centered * inverse, inverse


def norm_pull(grad, unit, inverse, gain):
    scaled = grad * gain
    return inverse * (
        scaled
        - jnp.mean(scaled, axis=-1, keepdims=True)
        - unit * jnp.mean(scaled * unit, axis=-1, keepdims=True)
    )


def shape_kernel(raw_kernel):
    shrunk = raw_kernel - shrink_level * jnp.tanh(raw_kernel / shrink_level)
    padded = jnp.pad(shrunk, ((1, 1), (0, 0)))
    return (padded[:-2] + padded[1:-1] + padded[2:]) / 3.0


def wide_dot(left, right):
    return jnp.dot(left, right, preferred_element_type=jnp.float32)


def token_dot(left, right):
    return lax.dot_general(left, right, (((0,), (0,)), ((), ())), preferred_element_type=jnp.float32)


def weight_dot(left, right):
    return lax.dot_general(left, right, (((1,), (1,)), ((), ())), preferred_element_type=jnp.float32)


def on_device(
    tokens,
    first_gain,
    first_shift,
    mixer_input,
    conv_kernel,
    mixer_output,
    second_gain,
    second_shift,
    widen_weight,
    narrow_weight,
    cotangent,
):
    axis_count = lax.axis_size("seq")
    seqs_here, local_len, features = tokens.shape
    row_total = seqs_here * local_len
    tap_count = conv_kernel.shape[0]
    reach = -(-tap_count // local_len)
    block_shape = tokens.shape

    forward, inverse = half_tables(local_len)
    forward_pair = jnp.asarray(stacked_pair(forward))
    inverse_high, inverse_rest = (jnp.asarray(part) for part in split_low(inverse))
    pull_pair = jnp.asarray(stacked_pair(inverse.T))
    push_high, push_rest = (jnp.asarray(part) for part in split_low(forward.T))

    flat_tokens = tokens.reshape(row_total, features).astype(jnp.float32)
    flat_cot = cotangent.reshape(row_total, features)
    unit, scale = norm_parts(flat_tokens)
    normed_low = (unit * first_gain + first_shift).astype(low_type)
    key_value = wide_dot(normed_low, mixer_input[:, features:])
    key_rows = key_value[:, :features].reshape(block_shape)
    value_rows = key_value[:, features:].reshape(block_shape)
    product = key_rows * value_rows
    product_blocks = gather_blocks(product, reach, 1)

    query_rows = wide_dot(normed_low, mixer_input[:, :features])
    raw_kernel = conv_kernel.astype(jnp.float32)
    kernel_taps = shape_kernel(raw_kernel)
    tap_blocks = jnp.pad(kernel_taps, ((0, reach * local_len - tap_count), (0, 0))).reshape(
        reach, local_len, features
    )
    table = jnp.asarray(forward.astype(np.float32))
    tap_spectra = [jnp.dot(table, tap_blocks[place], precision=highest) for place in range(reach)]
    spectra = []
    for place in range(reach + 1):
        parts = []
        if place > 0:
            parts.append(tap_spectra[place - 1])
        if place < reach:
            parts.append(turn(tap_spectra[place], local_len))
        spectra.append(sum(parts))
    spectrum = jnp.stack(spectra)

    convolved, gated_low = convolve_call(
        convolve_kernel,
        product_blocks,
        (forward_pair, inverse_high, inverse_rest),
        spectrum,
        (query_rows.reshape(block_shape),),
        (jnp.float32, low_type),
    )
    gated_low = gated_low.reshape(row_total, features)
    middle = flat_tokens + wide_dot(gated_low, mixer_output)
    unit2, scale2 = norm_parts(middle)
    second_low = (unit2 * second_gain + second_shift).astype(low_type)
    hidden = wide_dot(second_low, widen_weight)
    spread = 0.5 * (1.0 + lax.erf(hidden / math.sqrt(2.0)))
    active_low = (hidden * spread).astype(low_type)
    block_output = (middle + wide_dot(active_low, narrow_weight)).astype(low_type)
    grad_active = weight_dot(flat_cot, narrow_weight)
    slope = spread + hidden * jnp.exp(-0.5 * hidden * hidden) * (1.0 / math.sqrt(2.0 * math.pi))
    grad_hidden = (grad_active * slope).astype(low_type)
    grad_second = weight_dot(grad_hidden, widen_weight)
    grad_second_gain = jnp.sum(grad_second * unit2, axis=0)
    grad_second_shift = jnp.sum(grad_second, axis=0)
    grad_middle = flat_cot.astype(jnp.float32) + norm_pull(grad_second, unit2, scale2, second_gain)
    grad_branch = grad_middle.astype(low_type)
    grad_gated = weight_dot(grad_branch, mixer_output)
    grad_conv = (grad_gated * query_rows).reshape(block_shape)
    grad_blocks = gather_blocks(grad_conv, reach, -1)

    grad_narrow = reduce_all(token_dot(active_low, flat_cot))
    grad_widen = reduce_all(token_dot(second_low, grad_hidden))

    grad_spectrum = convolve_call(
        filter_grad_kernel, product_blocks, (forward_pair, pull_pair), None, (grad_conv,), None
    )
    back_table = jnp.asarray(forward.T.astype(np.float32))
    grad_taps = jnp.concatenate(
        [
            jnp.dot(
                back_table,
                grad_spectrum[place + 1] + turn_back(grad_spectrum[place], local_len),
                precision=highest,
            )
            for place in range(reach)
        ]
    )[:tap_count]
    padded = jnp.pad(grad_taps, ((1, 1), (0, 0)))
    grad_kernel = (
        (padded[:-2] + padded[1:-1] + padded[2:]) / 3.0 * jnp.tanh(raw_kernel / shrink_level) ** 2
    )
    lanes = 128
    kernel_width = tap_count * features // features
    second_sums = jnp.stack([grad_second_gain, grad_second_shift], axis=1)
    mixed_group = jnp.concatenate(
        [
            token_dot(gated_low, grad_branch),
            grad_kernel.reshape(features, kernel_width),
            jnp.pad(second_sums, ((0, 0), (0, lanes - 2))),
        ],
        axis=1,
    )
    output_sum = reduce_all(mixed_group)

    grad_key, grad_value = convolve_call(
        pull_kernel,
        grad_blocks,
        (pull_pair, push_high, push_rest),
        spectrum,
        (key_rows, value_rows),
        (low_type, low_type),
    )
    grad_query = (grad_gated * convolved.reshape(row_total, features)).astype(low_type)
    grad_mixed = jnp.concatenate(
        [
            grad_query,
            grad_key.reshape(row_total, features),
            grad_value.reshape(row_total, features),
        ],
        axis=1,
    )
    grad_normed = weight_dot(grad_mixed, mixer_input)
    first_sums = jnp.stack([jnp.sum(grad_normed * unit, axis=0), jnp.sum(grad_normed, axis=0)], axis=1)
    input_group = jnp.concatenate(
        [token_dot(normed_low, grad_mixed), jnp.pad(first_sums, ((0, 0), (0, lanes - 2)))], axis=1
    )
    input_sum = reduce_all(input_group)
    grad_tokens = (grad_middle + norm_pull(grad_normed, unit, scale, first_gain)).astype(low_type)

    side = 3 * features
    edge = features + kernel_width
    return (
        block_output.reshape(block_shape),
        grad_tokens.reshape(block_shape),
        input_sum[:, side],
        input_sum[:, side + 1],
        input_sum[:, :side],
        output_sum[:, features:edge].reshape(tap_count // axis_count, features),
        output_sum[:, :features],
        output_sum[:, edge],
        output_sum[:, edge + 1],
        grad_widen,
        grad_narrow,
    )


def solution(mesh):
    in_specs = (
        P("batch", "seq", None),
        P(),
        P(),
        P(),
        P(),
        P(),
        P(),
        P(),
        P(),
        P(),
        P("batch", "seq", None),
    )
    out_specs = (
        P("batch", "seq", None),
        P("batch", "seq", None),
        P("seq"),
        P("seq"),
        P("seq", None),
        P("seq", None),
        P("seq", None),
        P("seq"),
        P("seq"),
        P("seq", None),
        P("seq", None),
    )
    return jax.shard_map(
        on_device, mesh=mesh, in_specs=in_specs, out_specs=out_specs, check_vma=False
    )
```

```python
import functools
import math

import jax
import jax.numpy as jnp
import numpy as np
from jax import lax
from jax.experimental import pallas as pl
from jax.experimental.pallas import tpu as pltpu
from jax.sharding import PartitionSpec as P

norm_epsilon = 1e-05
shrink_level = 0.003
highest = lax.Precision.HIGHEST
low_type = jnp.bfloat16


def split_low(table):
    high = table.astype(np.float32).astype(jnp.bfloat16)
    rest = (table - high.astype(np.float64)).astype(np.float32).astype(jnp.bfloat16)
    return high, rest


@functools.lru_cache(maxsize=None)
def half_tables(block):
    order = np.concatenate([np.arange(0, block, 2), np.arange(1, block, 2)])
    theta = np.pi * (2 * order + 1) / (2 * block)
    place = np.arange(block)
    early = theta[:, None] * place[None, :]
    late = theta[None, :] * (block + place[:, None])
    forward = np.concatenate([np.cos(early), -np.sin(early)], axis=0)
    inverse = np.concatenate([np.cos(late), -np.sin(late)], axis=1) / block
    return forward, inverse


def stacked_pair(table):
    high, rest = split_low(table)
    return np.concatenate([high, rest], axis=1)


def turn(spectrum, block):
    half = block // 2
    real, imag = spectrum[:block], spectrum[block:]
    return jnp.concatenate([imag[:half], -imag[half:], -real[:half], real[half:]], axis=0)


def turn_back(spectrum, block):
    half = block // 2
    first, last = spectrum[:block], spectrum[block:]
    return jnp.concatenate([-last[:half], last[half:], first[:half], -first[half:]], axis=0)


def twice(values):
    rounded = values.astype(low_type)
    return jnp.concatenate([rounded, rounded], axis=0)


def low_dot(left, right):
    return jnp.dot(left, right, preferred_element_type=jnp.float32)


def filtered(block_refs, block, table_ref, filter_ref, conjugate):
    real, imag = 0.0, 0.0
    for place, block_ref in enumerate(block_refs):
        spectrum = low_dot(table_ref[...], twice(block_ref[0]))
        own_real, own_imag = spectrum[:block], spectrum[block:]
        filter_real = filter_ref[place, :block, :]
        filter_imag = filter_ref[place, block:, :]
        if conjugate:
            real += own_real * filter_real + own_imag * filter_imag
            imag += own_imag * filter_real - own_real * filter_imag
        else:
            real += own_real * filter_real - own_imag * filter_imag
            imag += own_real * filter_imag + own_imag * filter_real
    return jnp.concatenate([real, imag], axis=0).astype(low_type)


def convolve_kernel(count, block, table_ref, high_ref, rest_ref, filter_ref, query_ref, *refs):
    convolved_ref, gated_ref = refs[-2:]
    total = filtered(refs[:count], block, table_ref, filter_ref, False)
    convolved = low_dot(high_ref[...], total) + low_dot(rest_ref[...], total)
    convolved_ref[0] = convolved
    gated_ref[0] = (query_ref[0] * convolved).astype(low_type)


def pull_kernel(count, block, table_ref, high_ref, rest_ref, filter_ref, key_ref, value_ref, *refs):
    key_out_ref, value_out_ref = refs[-2:]
    total = filtered(refs[:count], block, table_ref, filter_ref, True)
    pulled = low_dot(high_ref[...], total) + low_dot(rest_ref[...], total)
    key_out_ref[0] = (pulled * value_ref[0]).astype(low_type)
    value_out_ref[0] = (pulled * key_ref[0]).astype(low_type)


def filter_grad_kernel(count, block, table_ref, pull_table_ref, grad_ref, *refs):
    out_ref = refs[-1]

    @pl.when(pl.program_id(1) == 0)
    def _():
        out_ref[...] = jnp.zeros_like(out_ref)

    grad = low_dot(pull_table_ref[...], twice(grad_ref[0]))
    grad_real, grad_imag = grad[:block], grad[block:]
    for place in range(count):
        spectrum = low_dot(table_ref[...], twice(refs[place][0]))
        own_real, own_imag = spectrum[:block], spectrum[block:]
        out_ref[place, :block, :] += grad_real * own_real + grad_imag * own_imag
        out_ref[place, block:, :] += grad_imag * own_real - grad_real * own_imag


def full_spec(shape):
    return pl.BlockSpec(shape, lambda *place: (0,) * len(shape), pipeline_mode=pl.Buffered(1))


def out_spec(shape):
    return pl.BlockSpec(shape, lambda *place: (0,) * len(shape))


def room(megabytes):
    return pltpu.CompilerParams(vmem_limit_bytes=megabytes * 2**20)


def convolve_call(body, blocks, tables, spectrum, extras, out_types, part, whole=None, earlier=None):
    seqs, block, features = blocks[0].shape
    count = len(blocks)
    width = features if count < 8 else 256
    base = part * seqs

    def tile(array_seqs):
        first = 0 if array_seqs == seqs else base
        return pl.BlockSpec((1, block, width), lambda column, seq: (first + seq, 0, column))

    in_specs = [full_spec(table.shape) for table in tables]
    operands = list(tables)
    filter_spec = pl.BlockSpec((count, 2 * block, width), lambda column, seq: (0, 0, column))
    if spectrum is not None:
        in_specs.append(filter_spec)
        operands.append(spectrum)
    arrays = list(extras) + list(blocks)
    in_specs += [tile(array.shape[0]) for array in arrays]
    operands += arrays
    aliases = {}
    if earlier is not None:
        aliases = {len(operands) + at: at for at in range(len(earlier))}
        in_specs += [pl.BlockSpec(memory_space=pl.ANY)] * len(earlier)
        operands += list(earlier)
    if out_types is None:
        out_shape = jax.ShapeDtypeStruct((count, 2 * block, features), jnp.float32)
        out_specs = filter_spec
    else:
        held = seqs if whole is None else whole
        out_shape = [jax.ShapeDtypeStruct((held, block, features), kind) for kind in out_types]
        out_specs = [tile(held)] * len(out_types)
    return pl.pallas_call(
        functools.partial(body, count, block),
        grid=(features // width, seqs),
        in_specs=in_specs,
        out_specs=out_specs,
        out_shape=out_shape,
        input_output_aliases=aliases,
        compiler_params=room(24 if count < 8 else 48),
    )(*operands)


def pull_dot(left, right):
    return lax.dot_general(left, right, (((1,), (1,)), ((), ())), preferred_element_type=jnp.float32)


def first_kernel(tokens_ref, gain_ref, shift_ref, key_weight_ref, value_weight_ref, *refs):
    normed_ref, key_ref, value_ref = refs[:3]
    at = pl.program_id(0)

    @pl.when(at == 0)
    def _():
        unit, _ = norm_parts(tokens_ref[...].astype(jnp.float32))
        normed_ref[...] = (unit * gain_ref[...] + shift_ref[...]).astype(low_type)

    normed = normed_ref[...]
    key = low_dot(normed, key_weight_ref[...])
    value = low_dot(normed, value_weight_ref[...])
    key_ref[...] = key
    value_ref[...] = value
    product = key * value
    rows = refs[3].shape[0]
    for part, product_ref in enumerate(refs[3:]):
        product_ref[...] = product[part * rows : (part + 1) * rows]


def first_call(tokens, gain, shift, weight, parts):
    rows, features = tokens.shape
    columns = 2
    width = features // columns
    row = full_spec((1, features))
    wide = jax.ShapeDtypeStruct((rows, features), jnp.float32)
    block = pl.BlockSpec((rows, width), lambda at: (0, at))
    return pl.pallas_call(
        first_kernel,
        grid=(columns,),
        in_specs=[
            full_spec((rows, features)),
            row,
            row,
            pl.BlockSpec((features, width), lambda at: (0, columns + at)),
            pl.BlockSpec((features, width), lambda at: (0, 2 * columns + at)),
        ],
        out_specs=[out_spec((rows, features)), block, block]
        + [pl.BlockSpec((rows // parts, width), lambda at: (0, at))] * parts,
        out_shape=[jax.ShapeDtypeStruct((rows, features), low_type), wide, wide]
        + [jax.ShapeDtypeStruct((rows // parts, features), jnp.float32)] * parts,
        compiler_params=room(24),
    )(tokens, gain[None], shift[None], weight, weight)


def middle_kernel(last, *refs):
    tokens_ref, cot_ref, mixer_ref, gain_ref, shift_ref, widen_ref, narrow_ref, query_ref = refs[:8]
    gated_ref, convolved_ref = refs[8:10]
    second_columns_ref, gated_columns_ref, active_ref, hidden_out_ref, block_ref = refs[-16:-11]
    grad_middle_ref, branch_ref, grad_query_ref, grad_conv_ref, sums_ref = refs[-11:-6]
    second_ref, middle_ref, unit_ref, inverse_ref, grad_ref, feed_ref = refs[-6:]
    at = pl.program_id(0)

    @pl.when(at == 0)
    def _():
        gated = gated_ref[...]
        middle = tokens_ref[...].astype(jnp.float32) + low_dot(gated, mixer_ref[...])
        unit, inverse = norm_parts(middle)
        middle_ref[...] = middle
        unit_ref[...] = unit
        inverse_ref[...] = inverse
        second = (unit * gain_ref[...] + shift_ref[...]).astype(low_type)
        second_ref[...] = second
        second_columns_ref[...] = second.T
        gated_columns_ref[...] = gated.T
        grad_ref[...] = jnp.zeros_like(grad_ref)
        feed_ref[...] = jnp.zeros_like(feed_ref)

    hidden = low_dot(second_ref[...], widen_ref[...])
    grad_active = pull_dot(cot_ref[...], narrow_ref[...])
    spread = 0.5 + 0.5 * lax.erf(hidden * (1.0 / math.sqrt(2.0)))
    active = (hidden * spread).astype(low_type)
    slope = spread + hidden * (jnp.exp(-0.5 * hidden * hidden) * (1.0 / math.sqrt(2.0 * math.pi)))
    grad_hidden = (grad_active * slope).astype(low_type)
    active_ref[...] = active
    hidden_out_ref[...] = grad_hidden
    grad_ref[...] += pull_dot(grad_hidden, widen_ref[...])
    feed_ref[...] += low_dot(active, narrow_ref[...])

    @pl.when(at == last)
    def _():
        grad, unit = grad_ref[...], unit_ref[...]
        sums_ref[0:1, :] = jnp.sum(grad * unit, axis=0, keepdims=True)
        sums_ref[1:2, :] = jnp.sum(grad, axis=0, keepdims=True)
        sums_ref[2:, :] = jnp.zeros_like(sums_ref[2:, :])
        block_ref[...] = (middle_ref[...] + feed_ref[...]).astype(low_type)
        grad_middle = cot_ref[...].astype(jnp.float32) + norm_pull(
            grad, unit, inverse_ref[...], gain_ref[...]
        )
        grad_middle_ref[...] = grad_middle
        branch = grad_middle.astype(low_type)
        branch_ref[...] = branch
        grad_gated = pull_dot(branch, mixer_ref[...])
        grad_conv_ref[...] = grad_gated * query_ref[...]
        grad_query_ref[...] = (grad_gated * convolved_ref[...]).astype(low_type)


def middle_call(tokens, cot, mixer, gain, shift, widen, narrow, query, gated, convolved, part, earlier=None):
    total, features = tokens.shape
    rows = gated.shape[0]
    hidden_size = widen.shape[1]
    tile = 768 if hidden_size % 768 == 0 else hidden_size
    steps = hidden_size // tile
    single = pl.Buffered(1)
    here = pl.BlockSpec((rows, features), lambda at: (part, 0), pipeline_mode=single)
    alone = full_spec((rows, features))
    row = full_spec((1, features))
    out_here = pl.BlockSpec((rows, features), lambda at: (part, 0))
    columns = pl.BlockSpec((features, rows), lambda at: (0, part))
    hidden_tile = pl.BlockSpec((rows, tile), lambda at: (part, at))
    wide, tall = (total, features), (features, total)
    operands = [tokens, cot, mixer, gain[None], shift[None], widen, narrow, query, gated, convolved]
    in_specs = [
        here,
        here,
        full_spec((features, features)),
        row,
        row,
        pl.BlockSpec((features, tile), lambda at: (0, at)),
        pl.BlockSpec((tile, features), lambda at: (at, 0)),
        here,
        alone,
        alone,
    ]
    aliases = {}
    if earlier is not None:
        aliases = {len(operands) + at: at for at in range(len(earlier))}
        in_specs += [pl.BlockSpec(memory_space=pl.ANY)] * len(earlier)
        operands += list(earlier)
    return pl.pallas_call(
        functools.partial(middle_kernel, steps - 1),
        grid=(steps,),
        in_specs=in_specs,
        out_specs=[columns, columns, hidden_tile, hidden_tile, out_here, out_here, out_here, out_here]
        + [out_spec((rows, features)), out_spec((8, features))],
        out_shape=[
            jax.ShapeDtypeStruct(tall, low_type),
            jax.ShapeDtypeStruct(tall, low_type),
            jax.ShapeDtypeStruct((total, hidden_size), low_type),
            jax.ShapeDtypeStruct((total, hidden_size), low_type),
            jax.ShapeDtypeStruct(wide, low_type),
            jax.ShapeDtypeStruct(wide, jnp.float32),
            jax.ShapeDtypeStruct(wide, low_type),
            jax.ShapeDtypeStruct(wide, low_type),
            jax.ShapeDtypeStruct((rows, features), jnp.float32),
            jax.ShapeDtypeStruct((8, features), jnp.float32),
        ],
        scratch_shapes=[
            pltpu.VMEM((rows, features), low_type),
            pltpu.VMEM((rows, features), jnp.float32),
            pltpu.VMEM((rows, features), jnp.float32),
            pltpu.VMEM((rows, 1), jnp.float32),
            pltpu.VMEM((rows, features), jnp.float32),
            pltpu.VMEM((rows, features), jnp.float32),
        ],
        input_output_aliases=aliases,
        compiler_params=room(32),
    )(*operands)


def last_kernel(chunks, width, tokens_ref, grad_middle_ref, gain_ref, weight_ref, query_ref, *refs):
    key_refs, value_refs = refs[:chunks], refs[chunks : 2 * chunks]
    out_ref, sums_ref, grad_ref = refs[2 * chunks :]
    at = pl.program_id(0)

    @pl.when(at == 0)
    def _():
        grad_ref[...] = pull_dot(query_ref[...], weight_ref[...])

    for place, part_refs in ((1, key_refs), (2, value_refs)):

        @pl.when(at == place)
        def _(part_refs=part_refs):
            total = grad_ref[...]
            for chunk, part_ref in enumerate(part_refs):
                total += pull_dot(part_ref[...], weight_ref[:, chunk * width : (chunk + 1) * width])
            grad_ref[...] = total

    @pl.when(at == 2)
    def _():
        grad = grad_ref[...]
        unit, inverse = norm_parts(tokens_ref[...].astype(jnp.float32))
        sums_ref[0:1, :] = jnp.sum(grad * unit, axis=0, keepdims=True)
        sums_ref[1:2, :] = jnp.sum(grad, axis=0, keepdims=True)
        sums_ref[2:, :] = jnp.zeros_like(sums_ref[2:, :])
        out_ref[...] = (grad_middle_ref[...] + norm_pull(grad, unit, inverse, gain_ref[...])).astype(low_type)


def last_call(tokens, grad_middle, gain, weight, query, keys, values):
    rows, features = tokens.shape
    chunks = len(keys)
    width = features // chunks
    full = full_spec((rows, features))
    return pl.pallas_call(
        functools.partial(last_kernel, chunks, width),
        grid=(3,),
        in_specs=[
            full,
            full,
            full_spec((1, features)),
            pl.BlockSpec((features, features), lambda at: (0, at)),
            full,
        ]
        + [full_spec((rows, width))] * (2 * chunks),
        out_specs=[out_spec((rows, features)), out_spec((8, features))],
        out_shape=[
            jax.ShapeDtypeStruct((rows, features), low_type),
            jax.ShapeDtypeStruct((8, features), jnp.float32),
        ],
        scratch_shapes=[pltpu.VMEM((rows, features), jnp.float32)],
        compiler_params=room(24),
    )(tokens, grad_middle, gain[None], weight, query, *keys, *values)


def columns_kernel(layout, left_count, right_count, split, *refs):
    left_refs, refs = refs[:left_count], refs[left_count:]
    right_refs, refs = refs[:right_count], refs[right_count:]
    for place, (left, right, column) in enumerate(layout):

        @pl.when(pl.program_id(0) == place)
        def _(left=left, right=right, column=column):
            width = refs[-1].shape[1]
            values = right_refs[right][:, column * width : (column + 1) * width]
            result = values if left is None else low_dot(left_refs[left][...], values)
            if split:
                half = result.shape[0] // 2
                result = result + refs[0][...]
                refs[1][...] = result[:half]
                refs[2][...] = result[half:]
            else:
                refs[-1][...] = result


def columns_call(lefts, rights, layout, width, moved=None, kind=jax.ShapeDtypeStruct):
    rows = lefts[0].shape[0]
    total = width * len(layout)
    split = moved is not None
    block = pl.BlockSpec((rows, width), lambda at: (0, at))
    if split:
        out_specs = [pl.BlockSpec((rows // 2, width), lambda at: (0, at))] * 2
        out_shape = [kind((rows // 2, total), jnp.float32)] * 2
    else:
        out_specs, out_shape = block, kind((rows, total), jnp.float32)
    in_specs = [full_spec(left.shape) for left in lefts]
    base = layout[0][2]
    if len(layout) > 1 and layout == [(0, 0, base + at) for at in range(len(layout))]:
        in_specs.append(pl.BlockSpec((rights[0].shape[0], width), lambda at: (0, base + at)))
        layout = [(0, 0, 0)] * len(layout)
    else:
        in_specs += [full_spec(right.shape) for right in rights]
    operands = [*lefts, *rights]
    if split:
        in_specs.append(block)
        operands.append(moved)
    return pl.pallas_call(
        functools.partial(columns_kernel, layout, len(lefts), len(rights), split),
        grid=(len(layout),),
        in_specs=in_specs,
        out_specs=out_specs,
        out_shape=out_shape,
        compiler_params=room(16),
    )(*operands)


def narrow_kernel(count, owner_ref, left_ref, right_ref, *refs):
    result = low_dot(left_ref[...], right_ref[...])
    if len(refs) == 1:
        refs[0][0] = result
        return
    result = result + refs[0][0]
    half = result.shape[0] // 2
    first = pl.program_id(0) < count // 2

    @pl.when(first)
    def _():
        refs[2][0] = result[:half]
        refs[4][0] = result[half:]

    @pl.when(jnp.logical_not(first))
    def _():
        refs[1][0] = result[:half]
        refs[3][0] = result[half:]


def narrow_grad(left, right, order, core, moved=None):
    size = lax.axis_size("seq")
    rows, depth = left.shape
    columns = right.shape[1] // size
    count = size // 2
    held = rows // 2
    if columns % 128:
        chosen = choose(right, 1, order, core).reshape(depth, count, columns)
        result = jnp.einsum("mt,tcp->cmp", left, chosen, preferred_element_type=jnp.float32)
        if moved is None:
            return result
        result = result + moved
        return [part for at in range(2) for part in cut(result[:, at * held : (at + 1) * held], 0)]
    owners = jnp.stack(owner_list(order, core)).astype(jnp.int32)
    half = count // 2

    def turned(at):
        return lax.rem(at + half, count) if moved is not None else at

    in_specs = [
        pl.BlockSpec((rows, depth), lambda at, owner: (0, 0), pipeline_mode=pl.Buffered(1)),
        pl.BlockSpec((depth, columns), lambda at, owner: (0, owner[turned(at)])),
    ]
    if moved is None:
        operands = []
        out_specs = pl.BlockSpec((1, rows, columns), lambda at, owner: (at, 0, 0))
        out_shape = pltpu.HBM((count, rows, columns), jnp.float32)
    else:
        operands = [moved]
        in_specs.append(pl.BlockSpec((1, rows, columns), lambda at, owner: (turned(at), 0, 0)))
        out_specs = [
            pl.BlockSpec((1, held, columns), lambda at, owner: (jnp.maximum(at - half, 0), 0, 0)),
            pl.BlockSpec((1, held, columns), lambda at, owner: (jnp.minimum(at, half - 1), 0, 0)),
        ] * 2
        out_shape = [pltpu.HBM((half, held, columns), jnp.float32)] * 4
    return pl.pallas_call(
        functools.partial(narrow_kernel, count),
        grid_spec=pltpu.PrefetchScalarGridSpec(
            num_scalar_prefetch=1, grid=(count,), in_specs=in_specs, out_specs=out_specs
        ),
        out_shape=out_shape,
        compiler_params=room(16),
    )(owners, left, right, *operands)


def turn_kernel(*refs):
    rows = refs[0].shape[0]
    for at, ref in enumerate(refs[:-1]):
        refs[-1][:, at * rows : (at + 1) * rows] = ref[...].T


def turned_rows(parts):
    rows, columns = parts[0].shape
    shape = (columns, rows * len(parts))
    if columns % 128:
        return jnp.concatenate(parts, axis=0).T
    return pl.pallas_call(
        turn_kernel, out_shape=jax.ShapeDtypeStruct(shape, jnp.float32), compiler_params=room(16)
    )(*parts)


def partner_pairs(size, step):
    return [(place, place ^ step) for place in range(size)]


def swap(values, axis, step):
    return lax.ppermute(values, axis, partner_pairs(lax.axis_size(axis), step))


def start_blocks(own, count, sign):
    size = lax.axis_size("seq")
    blocks = [own]
    for pair in range(1, (count + 1) // 2 + 1):
        step = sign * 2 * pair
        pairs = [(a, a + step) for a in range(size) if 0 <= a + step < size]
        blocks.append(lax.ppermute(own, "seq", pairs))
    return blocks


def fill_blocks(evens, count, sign):
    core = lax.axis_index("seq") & 1
    blocks = [evens[0]]
    for near, far in zip(evens[:-1], evens[1:]):
        sent = jnp.where((core == 0) == (sign > 0), near, far)
        blocks += [swap(sent, "seq", 1), far]
    return blocks[: count + 1]


def core_swap(values):
    size = lax.axis_size("seq")
    groups = [[place, place + 1] for place in range(0, size, 2)]
    return lax.all_to_all(values, "seq", 0, 0, axis_index_groups=groups)


def swap_blocks(evens, count, sign):
    core = lax.axis_index("seq") & 1
    blocks = [evens[0]]
    for near, far in zip(evens[:-1], evens[1:]):
        moved = core_swap(jnp.stack([far, near] if sign > 0 else [near, far]))
        blocks += [lax.dynamic_index_in_dim(moved, 1 - core, 0, keepdims=False), far]
    return blocks[: count + 1]


def region(work, *values):
    shapes = jax.eval_shape(work, *values)

    def idle(*values):
        return jax.tree.map(lambda shape: jnp.zeros(shape.shape, shape.dtype), shapes)

    always = lax.axis_index("seq") < lax.axis_size("seq")
    return lax.cond(always, work, idle, *values)


class Order:
    def __init__(self):
        self.last = None

    def step(self, work, *values):
        if self.last is not None:
            values, _ = lax.optimization_barrier((values, self.last))
        result = work(*values)
        self.last = result
        return result


def owner_list(order, core):
    chip = lax.axis_index("seq") >> 1
    count = len(order)
    owners = []
    for place in range(1 << count):
        relative = sum(((place >> (count - 1 - at)) & 1) << (bit - 1) for at, bit in enumerate(order))
        owners.append(((chip ^ relative) << 1) | core)
    return owners


def choose(values, dim, order, core):
    size = lax.axis_size("seq")
    part = values.shape[dim] // size
    return jnp.concatenate(
        [
            lax.dynamic_slice_in_dim(values, owner * part, part, dim)
            for owner in owner_list(order, core)
        ],
        axis=dim,
    )


def cut(values, dim):
    half = values.shape[dim] // 2
    return lax.slice_in_dim(values, 0, half, axis=dim), lax.slice_in_dim(values, half, 2 * half, axis=dim)


class Piece:
    def __init__(self, kept, moved, dim, order):
        self.kept, self.dim, self.order = kept, dim, order
        self.arriving = swap(moved, "seq", 1 << order[0])
        self.done = 1

    def advance(self, steps):
        bit = self.order[self.done]
        self.done += 1

        def work(kept, arriving):
            keep, move = cut(kept, self.dim)
            arrived_keep, arrived_move = cut(arriving, self.dim)
            return keep + arrived_keep, move + arrived_move

        self.kept, moved = steps.step(work, self.kept, self.arriving)
        self.arriving = swap(moved, "seq", 1 << bit)

    def finish(self, steps):
        while self.done < len(self.order):
            self.advance(steps)
        return steps.step(lambda kept, arriving: kept + arriving, self.kept, self.arriving)


class BatchSum:
    def __init__(self, values):
        self.size = lax.axis_size("batch")
        self.values = values
        self.stage = 0
        if self.size == 4:
            self.arriving = lax.ppermute(values, "batch", [(0, 1), (3, 2)])
        else:
            self.arriving = None

    def advance(self, steps):
        if self.size != 4:
            if self.stage == 0:
                self.values = lax.psum(self.values, "batch")
        elif self.stage < 2:
            self.values = steps.step(lambda values, arriving: values + arriving, self.values, self.arriving)
            pairs = [(1, 2), (2, 1)] if self.stage == 0 else [(1, 0), (2, 3)]
            self.arriving = lax.ppermute(self.values, "batch", pairs)
        else:
            place = lax.axis_index("batch")
            middle = (place == 1) | (place == 2)
            self.values = steps.step(
                lambda values, arriving: jnp.where(middle, values, arriving), self.values, self.arriving
            )
        self.stage += 1


def norm_parts(values):
    centered = values - jnp.mean(values, axis=-1, keepdims=True)
    inverse = lax.rsqrt(jnp.mean(centered * centered, axis=-1, keepdims=True) + norm_epsilon)
    return centered * inverse, inverse


def norm_pull(grad, unit, inverse, gain):
    scaled = grad * gain
    return inverse * (
        scaled
        - jnp.mean(scaled, axis=-1, keepdims=True)
        - unit * jnp.mean(scaled * unit, axis=-1, keepdims=True)
    )


def shape_kernel(raw_kernel):
    shrunk = raw_kernel - shrink_level * jnp.tanh(raw_kernel / shrink_level)
    padded = jnp.pad(shrunk, ((1, 1), (0, 0)))
    return (padded[:-2] + padded[1:-1] + padded[2:]) / 3.0


def tap_rows(values):
    size = lax.axis_size("seq")
    taps, features = values.shape
    if features % taps:
        return values.reshape(features, taps)
    cells = values.reshape(size, taps // size, features // taps, taps)
    return jnp.swapaxes(cells, 1, 2).reshape(features, taps)


def tap_share(values):
    size = lax.axis_size("seq")
    rows, taps = values.shape
    features = rows * size
    if features % taps:
        return values.reshape(taps // size, features)
    cells = values.reshape(features // taps, taps // size, taps)
    return jnp.swapaxes(cells, 0, 1).reshape(taps // size, features)


def wide_dot(left, right):
    return jnp.dot(left, right, preferred_element_type=jnp.float32)


def token_dot(left, right):
    return lax.dot_general(left, right, (((0,), (0,)), ((), ())), preferred_element_type=jnp.float32)


def weight_dot(left, right):
    return lax.dot_general(left, right, (((1,), (1,)), ((), ())), preferred_element_type=jnp.float32)


def on_device(
    tokens,
    first_gain,
    first_shift,
    mixer_input,
    conv_kernel,
    mixer_output,
    second_gain,
    second_shift,
    widen_weight,
    narrow_weight,
    cotangent,
):
    axis_count = lax.axis_size("seq")
    core = lax.axis_index("seq") & 1
    other = 1 - core
    seqs_here, local_len, features = tokens.shape
    row_total = seqs_here * local_len
    tap_count = conv_kernel.shape[0]
    reach = -(-tap_count // local_len)
    block_shape = tokens.shape
    parts = 2 if seqs_here % 2 == 0 else 1
    part_shape = (seqs_here // parts, local_len, features)
    part_rows = row_total // parts
    bits = axis_count.bit_length() - 1
    down_order = list(range(bits - 1, 0, -1))
    up_order = list(range(1, bits))
    steps = Order()

    forward, inverse = half_tables(local_len)
    forward_pair = jnp.asarray(stacked_pair(forward))
    inverse_high, inverse_rest = (jnp.asarray(part) for part in split_low(inverse))
    pull_pair = jnp.asarray(stacked_pair(inverse.T))
    push_high, push_rest = (jnp.asarray(part) for part in split_low(forward.T))

    flat_tokens = tokens.reshape(row_total, features)
    flat_cot = cotangent.reshape(row_total, features)

    normed_low, key_rows, value_rows, *products = steps.step(
        lambda values: first_call(values, first_gain, first_shift, mixer_input, parts), flat_tokens
    )
    key_rows = key_rows.reshape(block_shape)
    value_rows = value_rows.reshape(block_shape)
    product_evens = [start_blocks(products[0].reshape(part_shape), reach, 1)]

    raw_kernel = conv_kernel.astype(jnp.float32)

    def filter_step(raw_kernel):
        kernel_taps = shape_kernel(raw_kernel)
        tap_blocks = jnp.pad(kernel_taps, ((0, reach * local_len - tap_count), (0, 0))).reshape(
            reach, local_len, features
        )
        table = jnp.asarray(forward.astype(np.float32))
        tap_spectra = [jnp.dot(table, tap_blocks[place], precision=highest) for place in range(reach)]
        spectra = []
        for place in range(reach + 1):
            terms = []
            if place > 0:
                terms.append(tap_spectra[place - 1])
            if place < reach:
                terms.append(turn(tap_spectra[place], local_len))
            spectra.append(sum(terms))
        return jnp.stack(spectra)

    cot_columns = steps.step(jnp.transpose, flat_cot)
    normed_columns = steps.step(jnp.transpose, normed_low)
    for part in products[1:]:
        part, _ = lax.optimization_barrier((part, steps.last))
        product_evens.append(start_blocks(part.reshape(part_shape), reach, 1))
    query_rows = steps.step(
        lambda rows, weight: wide_dot(rows, weight), normed_low, mixer_input[:, :features]
    )
    spectrum = steps.step(filter_step, raw_kernel)

    def convolve_part(at, query, spectrum, blocks):
        result = convolve_call(
            convolve_kernel,
            blocks,
            (forward_pair, inverse_high, inverse_rest),
            spectrum,
            (query,),
            (jnp.float32, low_type),
            at,
        )
        return [values.reshape(part_rows, features) for values in result]

    middle_parts, product_blocks, grad_conv, grad_evens, second_sums = None, [], [], [], []
    for at in range(parts):
        blocks = steps.step(lambda evens: swap_blocks(evens, reach, 1), product_evens[at])
        convolved, gated = steps.step(
            functools.partial(convolve_part, at), query_rows.reshape(block_shape), spectrum, blocks
        )
        product_blocks.append(blocks)
        *middle_parts, grad, sums = steps.step(
            lambda query, gated, convolved, earlier, at=at: middle_call(
                flat_tokens,
                flat_cot,
                mixer_output,
                second_gain,
                second_shift,
                widen_weight,
                narrow_weight,
                query,
                gated,
                convolved,
                at,
                earlier,
            ),
            query_rows,
            gated,
            convolved,
            middle_parts,
        )
        grad_conv.append(grad.reshape(part_shape))
        grad_evens.append(start_blocks(grad_conv[at], reach, -1))
        second_sums.append(sums)
    (
        second_columns,
        gated_columns,
        active_low,
        grad_hidden,
        block_output,
        grad_middle,
        grad_branch,
        grad_query,
    ) = middle_parts

    tiles = grad_hidden.shape[1] // 2 // features
    half_layouts = [[(0, 0, half * tiles + at) for at in range(tiles)] for half in range(2)]
    output_layout = [(0, 0, 0), (1, 1, 0)]
    both = (other, core)

    def dots(lefts, rights, layout, moved=None, width=features):
        return columns_call(lefts, rights, layout, width, moved, kind=pltpu.HBM)

    def widen_work(second_columns, grad_hidden):
        inner = Order()
        lefts = inner.step(
            lambda v: [choose(v, 0, order, each) for each in both for order in widen_orders], second_columns
        )
        moved = [
            swap(inner.step(lambda *pair, half=half: dots(pair[:1], pair[1:], half), left, grad_hidden), "seq", 1)
            for half, left in zip(half_layouts, lefts[:2])
        ]
        return [
            inner.step(
                lambda left, right, moved, half=half: dots([left], [right], half, moved), left, grad_hidden, part
            )
            for half, left, part in zip(half_layouts, lefts[2:], moved)
        ]

    def narrow_work(cot_columns, active, gated, normed, branch, query):
        inner = Order()
        moved = swap(
            inner.step(lambda *pair: narrow_grad(*pair, down_order, other), cot_columns, active), "seq", 1
        )
        lefts = inner.step(
            lambda *pair: [choose(values, 0, up_order, each) for each in both for values in pair],
            gated,
            normed,
        )
        moved_output = swap(
            inner.step(
                lambda lefts, *rights: dots(lefts, rights, output_layout), lefts[:2], branch, query
            ),
            "seq",
            1,
        )
        narrow = inner.step(
            lambda left, right, moved: narrow_grad(left, right, down_order, core, moved),
            cot_columns,
            active,
            moved,
        )
        output = inner.step(
            lambda lefts, branch, query, moved: dots(lefts, [branch, query], output_layout, moved),
            lefts[2:],
            branch,
            query,
            moved_output,
        )
        return narrow[:2], narrow[2:], output

    starts, flows = {}, {}

    def run(plan):
        for name in plan.split():
            if name[0] == "+":
                (kept, moved), order = starts[name[1:]]
                moved, _ = lax.optimization_barrier((moved, steps.last))
                flows[name[1:]] = Piece(kept, moved, 0, order)
                continue
            flow = flows[name]
            if isinstance(flow, BatchSum):
                flow.advance(steps)
            elif flow.done < len(flow.order):
                flow.advance(steps)
            else:
                flows[name] = BatchSum(flow.finish(steps))

    widen_orders = (up_order, down_order)
    second_columns, grad_evens[0] = lax.optimization_barrier((second_columns, grad_evens[0]))
    pairs = steps.step(lambda *values: region(widen_work, *values), second_columns, grad_hidden)
    pairs, grad_evens = lax.optimization_barrier((pairs, grad_evens))
    starts["w0"], starts["w1"] = zip(pairs, widen_orders)
    run("+w0 +w1")
    pairs = steps.step(
        lambda *values: region(narrow_work, *values),
        cot_columns,
        active_low,
        gated_columns,
        normed_columns,
        grad_branch,
        grad_query,
    )
    starts["n0"], starts["n1"], starts["o"] = zip(pairs, (down_order, down_order, up_order))
    run("w0 w1 +n0 +o +n1")

    grad_spectrum = [
        steps.step(
            lambda grad, blocks, at=at: convolve_call(
                filter_grad_kernel, blocks, (forward_pair, pull_pair), None, (grad,), None, at
            ),
            grad_conv[at],
            product_blocks[at],
        )
        for at in range(parts)
    ]

    def taps_step(raw_kernel, *terms):
        grad_spectrum = sum(terms)
        back_table = jnp.asarray(forward.T.astype(np.float32))
        grad_taps = jnp.concatenate(
            [
                jnp.dot(
                    back_table,
                    grad_spectrum[place + 1] + turn_back(grad_spectrum[place], local_len),
                    precision=highest,
                )
                for place in range(reach)
            ]
        )[:tap_count]
        padded = jnp.pad(grad_taps, ((1, 1), (0, 0)))
        return (
            (padded[:-2] + padded[1:-1] + padded[2:]) / 3.0 * jnp.tanh(raw_kernel / shrink_level) ** 2
        )

    kernel_rows = steps.step(
        lambda *values: tap_rows(taps_step(*values)), raw_kernel, *grad_spectrum
    )

    width = features // 2
    tail_width = -(-(tap_count + 4) // width) * width
    input_layout = [(0, side, at) for side in range(2) for at in range(2)]
    input_layout += [(None, 2, at) for at in range(tail_width // width)]

    def pull_work(evens, spectrum, key, value):
        inner = Order()
        blocks = [fill_blocks(part, reach, -1) for part in evens]
        pulled = None
        for at in range(parts):
            pulled = inner.step(
                lambda spectrum, key, value, blocks, earlier, at=at: convolve_call(
                    pull_kernel,
                    blocks,
                    (pull_pair, push_high, push_rest),
                    spectrum,
                    (key, value),
                    (low_type, low_type),
                    at,
                    seqs_here,
                    earlier,
                ),
                spectrum,
                key,
                value,
                blocks[at],
                pulled,
            )
        return pulled

    pulled = steps.step(
        lambda *values: region(pull_work, *values), grad_evens, spectrum, key_rows, value_rows
    )
    keys, values = (part.reshape(row_total, features) for part in pulled)

    def mixer_work(keys, values, normed, query, grad_middle, kernel_rows, second_sums):
        inner = Order()
        lefts = inner.step(lambda v: [choose(v, 0, down_order, each) for each in both], normed)
        grad_tokens, first_sums = inner.step(
            lambda grad_middle, query, keys, values: last_call(
                flat_tokens, grad_middle, first_gain, mixer_input, query, [keys], [values]
            ),
            grad_middle,
            query,
            keys,
            values,
        )

        def tail_step(kernel_rows, first_sums, second_sums):
            rows = jnp.concatenate([first_sums[:2], second_sums[:2]], axis=0)
            tail = jnp.concatenate(
                [kernel_rows, jnp.pad(rows.T, ((0, 0), (0, tail_width - tap_count - 4)))], axis=1
            )
            return [choose(tail, 0, down_order, each) for each in both]

        tails = inner.step(tail_step, kernel_rows, first_sums, second_sums)
        moved = swap(
            inner.step(
                lambda left, *rights: dots([left], rights, input_layout, None, width),
                lefts[0],
                keys,
                values,
                tails[0],
            ),
            "seq",
            1,
        )
        pair = inner.step(
            lambda left, keys, values, tail, moved: dots(
                [left], [keys, values, tail], input_layout, moved, width
            ),
            lefts[1],
            keys,
            values,
            tails[1],
            moved,
        )
        return pair, grad_tokens

    pair, grad_tokens = steps.step(
        lambda *values: region(mixer_work, *values),
        keys,
        values,
        normed_columns,
        grad_query,
        grad_middle,
        kernel_rows,
        sum(second_sums),
    )
    starts["i"] = pair, down_order
    run("w0 w1 n0 o n1 +i w0 n0 o w1 n1 w0 n0 i w1 w0 o n0 n1 w1 i o n0 n1 i o n1 i i")

    output_total, input_total = flows["o"].values, flows["i"].values
    side = 2 * features
    edge = side + tap_count
    return (
        block_output.reshape(block_shape),
        grad_tokens.reshape(block_shape),
        input_total[:, edge],
        input_total[:, edge + 1],
        jnp.concatenate([output_total[:, features:side], input_total[:, :side]], axis=1),
        tap_share(input_total[:, side:edge]),
        output_total[:, :features],
        input_total[:, edge + 2],
        input_total[:, edge + 3],
        jnp.concatenate([flows["w0"].values, flows["w1"].values], axis=1),
        turned_rows([flows["n0"].values[0], flows["n1"].values[0]]),
    )


def solution(mesh):
    in_specs = (
        P("batch", "seq", None),
        P(),
        P(),
        P(),
        P(),
        P(),
        P(),
        P(),
        P(),
        P(),
        P("batch", "seq", None),
    )
    out_specs = (
        P("batch", "seq", None),
        P("batch", "seq", None),
        P("seq"),
        P("seq"),
        P("seq", None),
        P("seq", None),
        P("seq", None),
        P("seq"),
        P("seq"),
        P("seq", None),
        P("seq", None),
    )
    return jax.shard_map(
        on_device, mesh=mesh, in_specs=in_specs, out_specs=out_specs, check_vma=False
    )
```

```python
import functools
import math

import jax
import jax.numpy as jnp
import numpy as np
from jax import lax
from jax.experimental import pallas as pl
from jax.experimental.pallas import tpu as pltpu
from jax.sharding import PartitionSpec as P

norm_epsilon = 1e-05
shrink_level = 0.003
highest = lax.Precision.HIGHEST
low_type = jnp.bfloat16


def split_low(table):
    high = table.astype(np.float32).astype(jnp.bfloat16)
    rest = (table - high.astype(np.float64)).astype(np.float32).astype(jnp.bfloat16)
    return high, rest


@functools.lru_cache(maxsize=None)
def half_tables(block):
    order = np.concatenate([np.arange(0, block, 2), np.arange(1, block, 2)])
    theta = np.pi * (2 * order + 1) / (2 * block)
    place = np.arange(block)
    early = theta[:, None] * place[None, :]
    late = theta[None, :] * (block + place[:, None])
    forward = np.concatenate([np.cos(early), -np.sin(early)], axis=0)
    inverse = np.concatenate([np.cos(late), -np.sin(late)], axis=1) / block
    return forward, inverse


def stacked_pair(table):
    high, rest = split_low(table)
    return np.concatenate([high, rest], axis=1)


def turn(spectrum, block):
    half = block // 2
    real, imag = spectrum[:block], spectrum[block:]
    return jnp.concatenate([imag[:half], -imag[half:], -real[:half], real[half:]], axis=0)


def turn_back(spectrum, block):
    half = block // 2
    first, last = spectrum[:block], spectrum[block:]
    return jnp.concatenate([-last[:half], last[half:], first[:half], -first[half:]], axis=0)


def twice(values):
    rounded = values.astype(low_type)
    return jnp.concatenate([rounded, rounded], axis=0)


def low_dot(left, right):
    return jnp.dot(left, right, preferred_element_type=jnp.float32)


def filtered(block_refs, block, table_ref, filter_ref, conjugate):
    real, imag = 0.0, 0.0
    for place, block_ref in enumerate(block_refs):
        spectrum = low_dot(table_ref[...], twice(block_ref[0]))
        own_real, own_imag = spectrum[:block], spectrum[block:]
        filter_real = filter_ref[place, :block, :]
        filter_imag = filter_ref[place, block:, :]
        if conjugate:
            real += own_real * filter_real + own_imag * filter_imag
            imag += own_imag * filter_real - own_real * filter_imag
        else:
            real += own_real * filter_real - own_imag * filter_imag
            imag += own_real * filter_imag + own_imag * filter_real
    return jnp.concatenate([real, imag], axis=0).astype(low_type)


def convolve_kernel(count, block, table_ref, high_ref, rest_ref, filter_ref, query_ref, *refs):
    convolved_ref, gated_ref = refs[-2:]
    total = filtered(refs[:count], block, table_ref, filter_ref, False)
    convolved = low_dot(high_ref[...], total) + low_dot(rest_ref[...], total)
    convolved_ref[0] = convolved
    gated_ref[0] = (query_ref[0] * convolved).astype(low_type)


def pull_kernel(count, block, table_ref, high_ref, rest_ref, filter_ref, key_ref, value_ref, *refs):
    key_out_ref, value_out_ref = refs[-2:]
    total = filtered(refs[:count], block, table_ref, filter_ref, True)
    pulled = low_dot(high_ref[...], total) + low_dot(rest_ref[...], total)
    key_out_ref[0] = (pulled * value_ref[0]).astype(low_type)
    value_out_ref[0] = (pulled * key_ref[0]).astype(low_type)


def filter_grad_kernel(count, block, table_ref, pull_table_ref, grad_ref, *refs):
    out_ref = refs[-1]

    @pl.when(pl.program_id(1) == 0)
    def _():
        out_ref[...] = jnp.zeros_like(out_ref)

    grad = low_dot(pull_table_ref[...], twice(grad_ref[0]))
    grad_real, grad_imag = grad[:block], grad[block:]
    for place in range(count):
        spectrum = low_dot(table_ref[...], twice(refs[place][0]))
        own_real, own_imag = spectrum[:block], spectrum[block:]
        out_ref[place, :block, :] += grad_real * own_real + grad_imag * own_imag
        out_ref[place, block:, :] += grad_imag * own_real - grad_real * own_imag


def full_spec(shape):
    return pl.BlockSpec(shape, lambda *place: (0,) * len(shape), pipeline_mode=pl.Buffered(1))


def out_spec(shape):
    return pl.BlockSpec(shape, lambda *place: (0,) * len(shape))


def room(megabytes):
    return pltpu.CompilerParams(vmem_limit_bytes=megabytes * 2**20)


def convolve_call(body, blocks, tables, spectrum, extras, out_types, part, whole=None, earlier=None):
    seqs, block, features = blocks[0].shape
    count = len(blocks)
    width = features if count < 8 else 256
    base = part * seqs

    def tile(array_seqs):
        first = 0 if array_seqs == seqs else base
        return pl.BlockSpec((1, block, width), lambda column, seq: (first + seq, 0, column))

    in_specs = [full_spec(table.shape) for table in tables]
    operands = list(tables)
    filter_spec = pl.BlockSpec((count, 2 * block, width), lambda column, seq: (0, 0, column))
    if spectrum is not None:
        in_specs.append(filter_spec)
        operands.append(spectrum)
    arrays = list(extras) + list(blocks)
    in_specs += [tile(array.shape[0]) for array in arrays]
    operands += arrays
    aliases = {}
    if earlier is not None:
        aliases = {len(operands) + at: at for at in range(len(earlier))}
        in_specs += [pl.BlockSpec(memory_space=pl.ANY)] * len(earlier)
        operands += list(earlier)
    if out_types is None:
        out_shape = jax.ShapeDtypeStruct((count, 2 * block, features), jnp.float32)
        out_specs = filter_spec
    else:
        held = seqs if whole is None else whole
        out_shape = [jax.ShapeDtypeStruct((held, block, features), kind) for kind in out_types]
        out_specs = [tile(held)] * len(out_types)
    return pl.pallas_call(
        functools.partial(body, count, block),
        grid=(features // width, seqs),
        in_specs=in_specs,
        out_specs=out_specs,
        out_shape=out_shape,
        input_output_aliases=aliases,
        compiler_params=room(24 if count < 8 else 48),
    )(*operands)


def pull_dot(left, right):
    return lax.dot_general(left, right, (((1,), (1,)), ((), ())), preferred_element_type=jnp.float32)


def first_kernel(tokens_ref, gain_ref, shift_ref, key_weight_ref, value_weight_ref, *refs):
    normed_ref, key_ref, value_ref = refs[:3]
    at = pl.program_id(0)

    @pl.when(at == 0)
    def _():
        unit, _ = norm_parts(tokens_ref[...].astype(jnp.float32))
        normed_ref[...] = (unit * gain_ref[...] + shift_ref[...]).astype(low_type)

    normed = normed_ref[...]
    key = low_dot(normed, key_weight_ref[...])
    value = low_dot(normed, value_weight_ref[...])
    key_ref[...] = key
    value_ref[...] = value
    product = key * value
    rows = refs[3].shape[0]
    for part, product_ref in enumerate(refs[3:]):
        product_ref[...] = product[part * rows : (part + 1) * rows]


def first_call(tokens, gain, shift, weight, parts):
    rows, features = tokens.shape
    columns = 2
    width = features // columns
    row = full_spec((1, features))
    wide = jax.ShapeDtypeStruct((rows, features), jnp.float32)
    block = pl.BlockSpec((rows, width), lambda at: (0, at))
    return pl.pallas_call(
        first_kernel,
        grid=(columns,),
        in_specs=[
            full_spec((rows, features)),
            row,
            row,
            pl.BlockSpec((features, width), lambda at: (0, columns + at)),
            pl.BlockSpec((features, width), lambda at: (0, 2 * columns + at)),
        ],
        out_specs=[out_spec((rows, features)), block, block]
        + [pl.BlockSpec((rows // parts, width), lambda at: (0, at))] * parts,
        out_shape=[jax.ShapeDtypeStruct((rows, features), low_type), wide, wide]
        + [jax.ShapeDtypeStruct((rows // parts, features), jnp.float32)] * parts,
        compiler_params=room(24),
    )(tokens, gain[None], shift[None], weight, weight)


def middle_kernel(last, *refs):
    tokens_ref, cot_ref, mixer_ref, gain_ref, shift_ref, widen_ref, narrow_ref, query_ref = refs[:8]
    gated_ref, convolved_ref = refs[8:10]
    second_columns_ref, gated_columns_ref, active_ref, hidden_out_ref, block_ref = refs[-16:-11]
    grad_middle_ref, branch_ref, grad_query_ref, grad_conv_ref, sums_ref = refs[-11:-6]
    second_ref, middle_ref, unit_ref, inverse_ref, grad_ref, feed_ref = refs[-6:]
    at = pl.program_id(0)

    @pl.when(at == 0)
    def _():
        gated = gated_ref[...]
        middle = tokens_ref[...].astype(jnp.float32) + low_dot(gated, mixer_ref[...])
        unit, inverse = norm_parts(middle)
        middle_ref[...] = middle
        unit_ref[...] = unit
        inverse_ref[...] = inverse
        second = (unit * gain_ref[...] + shift_ref[...]).astype(low_type)
        second_ref[...] = second
        second_columns_ref[...] = second.T
        gated_columns_ref[...] = gated.T
        grad_ref[...] = jnp.zeros_like(grad_ref)
        feed_ref[...] = jnp.zeros_like(feed_ref)

    hidden = low_dot(second_ref[...], widen_ref[...])
    grad_active = pull_dot(cot_ref[...], narrow_ref[...])
    spread = 0.5 + 0.5 * lax.erf(hidden * (1.0 / math.sqrt(2.0)))
    active = (hidden * spread).astype(low_type)
    slope = spread + hidden * (jnp.exp(-0.5 * hidden * hidden) * (1.0 / math.sqrt(2.0 * math.pi)))
    grad_hidden = (grad_active * slope).astype(low_type)
    active_ref[...] = active
    hidden_out_ref[...] = grad_hidden
    grad_ref[...] += pull_dot(grad_hidden, widen_ref[...])
    feed_ref[...] += low_dot(active, narrow_ref[...])

    @pl.when(at == last)
    def _():
        grad, unit = grad_ref[...], unit_ref[...]
        sums_ref[0:1, :] = jnp.sum(grad * unit, axis=0, keepdims=True)
        sums_ref[1:2, :] = jnp.sum(grad, axis=0, keepdims=True)
        sums_ref[2:, :] = jnp.zeros_like(sums_ref[2:, :])
        block_ref[...] = (middle_ref[...] + feed_ref[...]).astype(low_type)
        grad_middle = cot_ref[...].astype(jnp.float32) + norm_pull(
            grad, unit, inverse_ref[...], gain_ref[...]
        )
        grad_middle_ref[...] = grad_middle
        branch = grad_middle.astype(low_type)
        branch_ref[...] = branch
        grad_gated = pull_dot(branch, mixer_ref[...])
        grad_conv_ref[...] = grad_gated * query_ref[...]
        grad_query_ref[...] = (grad_gated * convolved_ref[...]).astype(low_type)


def middle_call(tokens, cot, mixer, gain, shift, widen, narrow, query, gated, convolved, part, earlier=None):
    total, features = tokens.shape
    rows = gated.shape[0]
    hidden_size = widen.shape[1]
    tile = 768 if hidden_size % 768 == 0 else hidden_size
    steps = hidden_size // tile
    single = pl.Buffered(1)
    here = pl.BlockSpec((rows, features), lambda at: (part, 0), pipeline_mode=single)
    alone = full_spec((rows, features))
    row = full_spec((1, features))
    out_here = pl.BlockSpec((rows, features), lambda at: (part, 0))
    columns = pl.BlockSpec((features, rows), lambda at: (0, part))
    hidden_tile = pl.BlockSpec((rows, tile), lambda at: (part, at))
    wide, tall = (total, features), (features, total)
    operands = [tokens, cot, mixer, gain[None], shift[None], widen, narrow, query, gated, convolved]
    in_specs = [
        here,
        here,
        full_spec((features, features)),
        row,
        row,
        pl.BlockSpec((features, tile), lambda at: (0, at)),
        pl.BlockSpec((tile, features), lambda at: (at, 0)),
        here,
        alone,
        alone,
    ]
    aliases = {}
    if earlier is not None:
        aliases = {len(operands) + at: at for at in range(len(earlier))}
        in_specs += [pl.BlockSpec(memory_space=pl.ANY)] * len(earlier)
        operands += list(earlier)
    return pl.pallas_call(
        functools.partial(middle_kernel, steps - 1),
        grid=(steps,),
        in_specs=in_specs,
        out_specs=[columns, columns, hidden_tile, hidden_tile, out_here, out_here, out_here, out_here]
        + [out_spec((rows, features)), out_spec((8, features))],
        out_shape=[
            jax.ShapeDtypeStruct(tall, low_type),
            jax.ShapeDtypeStruct(tall, low_type),
            pltpu.HBM((total, hidden_size), low_type),
            pltpu.HBM((total, hidden_size), low_type),
            jax.ShapeDtypeStruct(wide, low_type),
            jax.ShapeDtypeStruct(wide, jnp.float32),
            jax.ShapeDtypeStruct(wide, low_type),
            jax.ShapeDtypeStruct(wide, low_type),
            jax.ShapeDtypeStruct((rows, features), jnp.float32),
            jax.ShapeDtypeStruct((8, features), jnp.float32),
        ],
        scratch_shapes=[
            pltpu.VMEM((rows, features), low_type),
            pltpu.VMEM((rows, features), jnp.float32),
            pltpu.VMEM((rows, features), jnp.float32),
            pltpu.VMEM((rows, 1), jnp.float32),
            pltpu.VMEM((rows, features), jnp.float32),
            pltpu.VMEM((rows, features), jnp.float32),
        ],
        input_output_aliases=aliases,
        compiler_params=room(32),
    )(*operands)


def last_kernel(chunks, width, tokens_ref, grad_middle_ref, gain_ref, weight_ref, query_ref, *refs):
    key_refs, value_refs = refs[:chunks], refs[chunks : 2 * chunks]
    out_ref, sums_ref, grad_ref = refs[2 * chunks :]
    at = pl.program_id(0)

    @pl.when(at == 0)
    def _():
        grad_ref[...] = pull_dot(query_ref[...], weight_ref[...])

    for place, part_refs in ((1, key_refs), (2, value_refs)):

        @pl.when(at == place)
        def _(part_refs=part_refs):
            total = grad_ref[...]
            for chunk, part_ref in enumerate(part_refs):
                total += pull_dot(part_ref[...], weight_ref[:, chunk * width : (chunk + 1) * width])
            grad_ref[...] = total

    @pl.when(at == 2)
    def _():
        grad = grad_ref[...]
        unit, inverse = norm_parts(tokens_ref[...].astype(jnp.float32))
        sums_ref[0:1, :] = jnp.sum(grad * unit, axis=0, keepdims=True)
        sums_ref[1:2, :] = jnp.sum(grad, axis=0, keepdims=True)
        sums_ref[2:, :] = jnp.zeros_like(sums_ref[2:, :])
        out_ref[...] = (grad_middle_ref[...] + norm_pull(grad, unit, inverse, gain_ref[...])).astype(low_type)


def last_call(tokens, grad_middle, gain, weight, query, keys, values):
    rows, features = tokens.shape
    chunks = len(keys)
    width = features // chunks
    full = full_spec((rows, features))
    return pl.pallas_call(
        functools.partial(last_kernel, chunks, width),
        grid=(3,),
        in_specs=[
            full,
            full,
            full_spec((1, features)),
            pl.BlockSpec((features, features), lambda at: (0, at)),
            full,
        ]
        + [full_spec((rows, width))] * (2 * chunks),
        out_specs=[out_spec((rows, features)), out_spec((8, features))],
        out_shape=[
            jax.ShapeDtypeStruct((rows, features), low_type),
            jax.ShapeDtypeStruct((8, features), jnp.float32),
        ],
        scratch_shapes=[pltpu.VMEM((rows, features), jnp.float32)],
        compiler_params=room(24),
    )(tokens, grad_middle, gain[None], weight, query, *keys, *values)


def columns_kernel(layout, left_count, right_count, split, *refs):
    left_refs, refs = refs[:left_count], refs[left_count:]
    right_refs, refs = refs[:right_count], refs[right_count:]
    for place, (left, right, column) in enumerate(layout):

        @pl.when(pl.program_id(0) == place)
        def _(left=left, right=right, column=column):
            width = refs[-1].shape[1]
            values = right_refs[right][:, column * width : (column + 1) * width]
            result = values if left is None else low_dot(left_refs[left][...], values)
            if split:
                half = result.shape[0] // 2
                result = result + refs[0][...]
                refs[1][...] = result[:half]
                refs[2][...] = result[half:]
            else:
                refs[-1][...] = result


def columns_call(lefts, rights, layout, width, moved=None, kind=jax.ShapeDtypeStruct):
    rows = lefts[0].shape[0]
    total = width * len(layout)
    split = moved is not None
    block = pl.BlockSpec((rows, width), lambda at: (0, at))
    if split:
        out_specs = [pl.BlockSpec((rows // 2, width), lambda at: (0, at))] * 2
        out_shape = [kind((rows // 2, total), jnp.float32)] * 2
    else:
        out_specs, out_shape = block, kind((rows, total), jnp.float32)
    in_specs = [full_spec(left.shape) for left in lefts]
    base = layout[0][2]
    if len(layout) > 1 and layout == [(0, 0, base + at) for at in range(len(layout))]:
        in_specs.append(pl.BlockSpec((rights[0].shape[0], width), lambda at: (0, base + at)))
        layout = [(0, 0, 0)] * len(layout)
    else:
        in_specs += [full_spec(right.shape) for right in rights]
    operands = [*lefts, *rights]
    if split:
        in_specs.append(block)
        operands.append(moved)
    return pl.pallas_call(
        functools.partial(columns_kernel, layout, len(lefts), len(rights), split),
        grid=(len(layout),),
        in_specs=in_specs,
        out_specs=out_specs,
        out_shape=out_shape,
        compiler_params=room(16),
    )(*operands)


def narrow_kernel(count, owner_ref, left_ref, right_ref, *refs):
    result = low_dot(left_ref[...], right_ref[...])
    if len(refs) == 1:
        refs[0][0] = result
        return
    result = result + refs[0][0]
    half = result.shape[0] // 2
    first = pl.program_id(0) < count // 2

    @pl.when(first)
    def _():
        refs[2][0] = result[:half]
        refs[4][0] = result[half:]

    @pl.when(jnp.logical_not(first))
    def _():
        refs[1][0] = result[:half]
        refs[3][0] = result[half:]


def narrow_grad(left, right, order, core, moved=None):
    size = lax.axis_size("seq")
    rows, depth = left.shape
    columns = right.shape[1] // size
    count = size // 2
    held = rows // 2
    if columns % 128:
        chosen = choose(right, 1, order, core).reshape(depth, count, columns)
        result = jnp.einsum("mt,tcp->cmp", left, chosen, preferred_element_type=jnp.float32)
        if moved is None:
            return result
        result = result + moved
        return [part for at in range(2) for part in cut(result[:, at * held : (at + 1) * held], 0)]
    owners = jnp.stack(owner_list(order, core)).astype(jnp.int32)
    half = count // 2

    def turned(at):
        return lax.rem(at + half, count) if moved is not None else at

    in_specs = [
        pl.BlockSpec((rows, depth), lambda at, owner: (0, 0), pipeline_mode=pl.Buffered(1)),
        pl.BlockSpec((depth, columns), lambda at, owner: (0, owner[turned(at)])),
    ]
    if moved is None:
        operands = []
        out_specs = pl.BlockSpec((1, rows, columns), lambda at, owner: (at, 0, 0))
        out_shape = pltpu.HBM((count, rows, columns), jnp.float32)
    else:
        operands = [moved]
        in_specs.append(pl.BlockSpec((1, rows, columns), lambda at, owner: (turned(at), 0, 0)))
        out_specs = [
            pl.BlockSpec((1, held, columns), lambda at, owner: (jnp.maximum(at - half, 0), 0, 0)),
            pl.BlockSpec((1, held, columns), lambda at, owner: (jnp.minimum(at, half - 1), 0, 0)),
        ] * 2
        out_shape = [pltpu.HBM((half, held, columns), jnp.float32)] * 4
    return pl.pallas_call(
        functools.partial(narrow_kernel, count),
        grid_spec=pltpu.PrefetchScalarGridSpec(
            num_scalar_prefetch=1, grid=(count,), in_specs=in_specs, out_specs=out_specs
        ),
        out_shape=out_shape,
        compiler_params=room(16),
    )(owners, left, right, *operands)


def turn_kernel(*refs):
    rows = refs[0].shape[0]
    for at, ref in enumerate(refs[:-1]):
        refs[-1][:, at * rows : (at + 1) * rows] = ref[...].T


def turned_rows(parts):
    rows, columns = parts[0].shape
    shape = (columns, rows * len(parts))
    if columns % 128:
        return jnp.concatenate(parts, axis=0).T
    return pl.pallas_call(
        turn_kernel, out_shape=jax.ShapeDtypeStruct(shape, jnp.float32), compiler_params=room(16)
    )(*parts)


def partner_pairs(size, step):
    return [(place, place ^ step) for place in range(size)]


def swap(values, axis, step):
    return lax.ppermute(values, axis, partner_pairs(lax.axis_size(axis), step))


def start_blocks(own, count, sign):
    size = lax.axis_size("seq")
    blocks = [own]
    for pair in range(1, (count + 1) // 2 + 1):
        step = sign * 2 * pair
        pairs = [(a, a + step) for a in range(size) if 0 <= a + step < size]
        blocks.append(lax.ppermute(own, "seq", pairs))
    return blocks


def fill_blocks(evens, count, sign):
    core = lax.axis_index("seq") & 1
    blocks = [evens[0]]
    for near, far in zip(evens[:-1], evens[1:]):
        sent = jnp.where((core == 0) == (sign > 0), near, far)
        blocks += [swap(sent, "seq", 1), far]
    return blocks[: count + 1]


def core_swap(values):
    size = lax.axis_size("seq")
    groups = [[place, place + 1] for place in range(0, size, 2)]
    return lax.all_to_all(values, "seq", 0, 0, axis_index_groups=groups)


def swap_blocks(evens, count, sign):
    core = lax.axis_index("seq") & 1
    blocks = [evens[0]]
    for near, far in zip(evens[:-1], evens[1:]):
        moved = core_swap(jnp.stack([far, near] if sign > 0 else [near, far]))
        blocks += [lax.dynamic_index_in_dim(moved, 1 - core, 0, keepdims=False), far]
    return blocks[: count + 1]


def later(ready, values):
    first = jax.tree.leaves(ready)[0]
    small = lax.slice(first, (0,) * first.ndim, (1,) * (first.ndim - 2) + (8, 128))
    tied, values, _ = lax.optimization_barrier((ready, values, swap(small, "seq", 1)))
    return tied, values


def region(work, *values):
    shapes = jax.eval_shape(work, *values)

    def idle(*values):
        return jax.tree.map(lambda shape: jnp.zeros(shape.shape, shape.dtype), shapes)

    always = lax.axis_index("seq") < lax.axis_size("seq")
    return lax.cond(always, work, idle, *values)


class Order:
    def __init__(self):
        self.last = None

    def step(self, work, *values):
        if self.last is not None:
            values, _ = lax.optimization_barrier((values, self.last))
        result = work(*values)
        self.last = result
        return result


def owner_list(order, core):
    chip = lax.axis_index("seq") >> 1
    count = len(order)
    owners = []
    for place in range(1 << count):
        relative = sum(((place >> (count - 1 - at)) & 1) << (bit - 1) for at, bit in enumerate(order))
        owners.append(((chip ^ relative) << 1) | core)
    return owners


def choose(values, dim, order, core):
    size = lax.axis_size("seq")
    part = values.shape[dim] // size
    return jnp.concatenate(
        [
            lax.dynamic_slice_in_dim(values, owner * part, part, dim)
            for owner in owner_list(order, core)
        ],
        axis=dim,
    )


def cut(values, dim):
    half = values.shape[dim] // 2
    return lax.slice_in_dim(values, 0, half, axis=dim), lax.slice_in_dim(values, half, 2 * half, axis=dim)


class Piece:
    def __init__(self, kept, moved, dim, order):
        self.kept, self.dim, self.order = kept, dim, order
        self.arriving = swap(moved, "seq", 1 << order[0])
        self.done = 1

    def advance(self, steps):
        bit = self.order[self.done]
        self.done += 1

        def work(kept, arriving):
            keep, move = cut(kept, self.dim)
            arrived_keep, arrived_move = cut(arriving, self.dim)
            return keep + arrived_keep, move + arrived_move

        self.kept, moved = steps.step(work, self.kept, self.arriving)
        self.arriving = swap(moved, "seq", 1 << bit)

    def finish(self, steps):
        while self.done < len(self.order):
            self.advance(steps)
        return steps.step(lambda kept, arriving: kept + arriving, self.kept, self.arriving)


class BatchSum:
    def __init__(self, values):
        self.size = lax.axis_size("batch")
        self.values = values
        self.stage = 0
        if self.size == 4:
            self.arriving = lax.ppermute(values, "batch", [(0, 1), (3, 2)])
        else:
            self.arriving = None

    def advance(self, steps):
        if self.size != 4:
            if self.stage == 0:
                self.values = lax.psum(self.values, "batch")
        elif self.stage < 2:
            self.values = steps.step(lambda values, arriving: values + arriving, self.values, self.arriving)
            pairs = [(1, 2), (2, 1)] if self.stage == 0 else [(1, 0), (2, 3)]
            self.arriving = lax.ppermute(self.values, "batch", pairs)
        else:
            place = lax.axis_index("batch")
            middle = (place == 1) | (place == 2)
            self.values = steps.step(
                lambda values, arriving: jnp.where(middle, values, arriving), self.values, self.arriving
            )
        self.stage += 1


def norm_parts(values):
    centered = values - jnp.mean(values, axis=-1, keepdims=True)
    inverse = lax.rsqrt(jnp.mean(centered * centered, axis=-1, keepdims=True) + norm_epsilon)
    return centered * inverse, inverse


def norm_pull(grad, unit, inverse, gain):
    scaled = grad * gain
    return inverse * (
        scaled
        - jnp.mean(scaled, axis=-1, keepdims=True)
        - unit * jnp.mean(scaled * unit, axis=-1, keepdims=True)
    )


def shape_kernel(raw_kernel):
    shrunk = raw_kernel - shrink_level * jnp.tanh(raw_kernel / shrink_level)
    padded = jnp.pad(shrunk, ((1, 1), (0, 0)))
    return (padded[:-2] + padded[1:-1] + padded[2:]) / 3.0


def tap_rows(values):
    size = lax.axis_size("seq")
    taps, features = values.shape
    if features % taps:
        return values.reshape(features, taps)
    cells = values.reshape(size, taps // size, features // taps, taps)
    return jnp.swapaxes(cells, 1, 2).reshape(features, taps)


def tap_share(values):
    size = lax.axis_size("seq")
    rows, taps = values.shape
    features = rows * size
    if features % taps:
        return values.reshape(taps // size, features)
    cells = values.reshape(features // taps, taps // size, taps)
    return jnp.swapaxes(cells, 0, 1).reshape(taps // size, features)


def wide_dot(left, right):
    return jnp.dot(left, right, preferred_element_type=jnp.float32)


def token_dot(left, right):
    return lax.dot_general(left, right, (((0,), (0,)), ((), ())), preferred_element_type=jnp.float32)


def weight_dot(left, right):
    return lax.dot_general(left, right, (((1,), (1,)), ((), ())), preferred_element_type=jnp.float32)


def on_device(
    tokens,
    first_gain,
    first_shift,
    mixer_input,
    conv_kernel,
    mixer_output,
    second_gain,
    second_shift,
    widen_weight,
    narrow_weight,
    cotangent,
):
    axis_count = lax.axis_size("seq")
    core = lax.axis_index("seq") & 1
    other = 1 - core
    seqs_here, local_len, features = tokens.shape
    row_total = seqs_here * local_len
    tap_count = conv_kernel.shape[0]
    reach = -(-tap_count // local_len)
    block_shape = tokens.shape
    parts = 2 if seqs_here % 2 == 0 else 1
    part_shape = (seqs_here // parts, local_len, features)
    part_rows = row_total // parts
    bits = axis_count.bit_length() - 1
    down_order = list(range(bits - 1, 0, -1))
    up_order = list(range(1, bits))
    steps = Order()

    forward, inverse = half_tables(local_len)
    forward_pair = jnp.asarray(stacked_pair(forward))
    inverse_high, inverse_rest = (jnp.asarray(part) for part in split_low(inverse))
    pull_pair = jnp.asarray(stacked_pair(inverse.T))
    push_high, push_rest = (jnp.asarray(part) for part in split_low(forward.T))

    flat_tokens = tokens.reshape(row_total, features)
    flat_cot = cotangent.reshape(row_total, features)

    normed_low, key_rows, value_rows, *products = steps.step(
        lambda values: first_call(values, first_gain, first_shift, mixer_input, parts), flat_tokens
    )
    key_rows = key_rows.reshape(block_shape)
    value_rows = value_rows.reshape(block_shape)
    product_evens = [start_blocks(products[0].reshape(part_shape), reach, 1)]

    raw_kernel = conv_kernel.astype(jnp.float32)

    def filter_step(raw_kernel):
        kernel_taps = shape_kernel(raw_kernel)
        tap_blocks = jnp.pad(kernel_taps, ((0, reach * local_len - tap_count), (0, 0))).reshape(
            reach, local_len, features
        )
        table = jnp.asarray(forward.astype(np.float32))
        tap_spectra = [jnp.dot(table, tap_blocks[place], precision=highest) for place in range(reach)]
        spectra = []
        for place in range(reach + 1):
            terms = []
            if place > 0:
                terms.append(tap_spectra[place - 1])
            if place < reach:
                terms.append(turn(tap_spectra[place], local_len))
            spectra.append(sum(terms))
        return jnp.stack(spectra)

    cot_columns = steps.step(jnp.transpose, flat_cot)
    normed_columns = steps.step(jnp.transpose, normed_low)
    query_rows = steps.step(
        lambda rows, weight: wide_dot(rows, weight), normed_low, mixer_input[:, :features]
    )
    spectrum = steps.step(filter_step, raw_kernel)
    for part in products[1:]:
        part, _ = lax.optimization_barrier((part, steps.last))
        product_evens.append(start_blocks(part.reshape(part_shape), reach, 1))

    def convolve_part(at, query, spectrum, blocks):
        result = convolve_call(
            convolve_kernel,
            blocks,
            (forward_pair, inverse_high, inverse_rest),
            spectrum,
            (query,),
            (jnp.float32, low_type),
            at,
        )
        return [values.reshape(part_rows, features) for values in result]

    middle_parts, product_blocks, grad_conv, grad_evens, second_sums = None, [], [], [], []
    for at in range(parts):
        blocks = steps.step(lambda evens: swap_blocks(evens, reach, 1), product_evens[at])
        convolved, gated = steps.step(
            functools.partial(convolve_part, at), query_rows.reshape(block_shape), spectrum, blocks
        )
        product_blocks.append(blocks)
        *middle_parts, grad, sums = steps.step(
            lambda query, gated, convolved, earlier, at=at: middle_call(
                flat_tokens,
                flat_cot,
                mixer_output,
                second_gain,
                second_shift,
                widen_weight,
                narrow_weight,
                query,
                gated,
                convolved,
                at,
                earlier,
            ),
            query_rows,
            gated,
            convolved,
            middle_parts,
        )
        grad_conv.append(grad.reshape(part_shape))
        grad_evens.append(start_blocks(grad_conv[at], reach, -1))
        second_sums.append(sums)
    (
        second_columns,
        gated_columns,
        active_low,
        grad_hidden,
        block_output,
        grad_middle,
        grad_branch,
        grad_query,
    ) = middle_parts

    tiles = grad_hidden.shape[1] // 2 // features
    half_layouts = [[(0, 0, half * tiles + at) for at in range(tiles)] for half in range(2)]
    output_layout = [(0, 0, 0), (1, 1, 0)]
    both = (other, core)

    def dots(lefts, rights, layout, moved=None, width=features):
        return columns_call(lefts, rights, layout, width, moved, kind=pltpu.HBM)

    def widen_work(second_columns, grad_hidden):
        inner = Order()
        lefts = inner.step(
            lambda v: [choose(v, 0, order, each) for each in both for order in widen_orders], second_columns
        )
        moved = [
            swap(inner.step(lambda *pair, half=half: dots(pair[:1], pair[1:], half), left, grad_hidden), "seq", 1)
            for half, left in zip(half_layouts, lefts[:2])
        ]
        return [
            inner.step(
                lambda left, right, moved, half=half: dots([left], [right], half, moved), left, grad_hidden, part
            )
            for half, left, part in zip(half_layouts, lefts[2:], moved)
        ]

    def narrow_work(cot_columns, active, gated, normed, branch, query):
        inner = Order()
        moved = swap(
            inner.step(lambda *pair: narrow_grad(*pair, down_order, other), cot_columns, active), "seq", 1
        )
        lefts = inner.step(
            lambda *pair: [choose(values, 0, up_order, each) for each in both for values in pair],
            gated,
            normed,
        )
        moved_output = swap(
            inner.step(
                lambda lefts, *rights: dots(lefts, rights, output_layout), lefts[:2], branch, query
            ),
            "seq",
            1,
        )
        narrow = inner.step(
            lambda left, right, moved: narrow_grad(left, right, down_order, core, moved),
            cot_columns,
            active,
            moved,
        )
        output = inner.step(
            lambda lefts, branch, query, moved: dots(lefts, [branch, query], output_layout, moved),
            lefts[2:],
            branch,
            query,
            moved_output,
        )
        return narrow[:2], narrow[2:], output

    starts, flows = {}, {}

    def run(*plan):
        for name in plan:
            if name[0] == "+":
                (kept, moved), order = starts[name[1:]]
                moved, _ = lax.optimization_barrier((moved, steps.last))
                flows[name[1:]] = Piece(kept, moved, 0, order)
                continue
            flow = flows[name]
            if isinstance(flow, BatchSum):
                flow.advance(steps)
            elif flow.done < len(flow.order):
                flow.advance(steps)
            else:
                flows[name] = BatchSum(flow.finish(steps))

    widen_orders = (up_order, down_order)
    second_columns, grad_evens[0] = lax.optimization_barrier((second_columns, grad_evens[0]))
    pairs = steps.step(lambda *values: region(widen_work, *values), second_columns, grad_hidden)
    pairs, grad_evens = lax.optimization_barrier((pairs, grad_evens))
    starts["w0"], starts["w1"] = zip(pairs, widen_orders)
    run("+w0", "+w1")
    grad_evens, cot_columns = later(grad_evens, cot_columns)
    pairs = steps.step(
        lambda *values: region(narrow_work, *values),
        cot_columns,
        active_low,
        gated_columns,
        normed_columns,
        grad_branch,
        grad_query,
    )
    starts["n0"], starts["n1"], starts["o"] = zip(pairs, (down_order, down_order, up_order))
    run("+n0", "+o", "w0", "w1", "+n1")

    grad_spectrum = [
        steps.step(
            lambda grad, blocks, at=at: convolve_call(
                filter_grad_kernel, blocks, (forward_pair, pull_pair), None, (grad,), None, at
            ),
            grad_conv[at],
            product_blocks[at],
        )
        for at in range(parts)
    ]

    def taps_step(raw_kernel, *terms):
        grad_spectrum = sum(terms)
        back_table = jnp.asarray(forward.T.astype(np.float32))
        grad_taps = jnp.concatenate(
            [
                jnp.dot(
                    back_table,
                    grad_spectrum[place + 1] + turn_back(grad_spectrum[place], local_len),
                    precision=highest,
                )
                for place in range(reach)
            ]
        )[:tap_count]
        padded = jnp.pad(grad_taps, ((1, 1), (0, 0)))
        return (
            (padded[:-2] + padded[1:-1] + padded[2:]) / 3.0 * jnp.tanh(raw_kernel / shrink_level) ** 2
        )

    kernel_rows = steps.step(
        lambda *values: tap_rows(taps_step(*values)), raw_kernel, *grad_spectrum
    )

    width = features // 2
    tail_width = -(-(tap_count + 4) // width) * width
    value_layout = [(0, 0, 0)]
    key_layout = [(0, 0, at) for at in range(2)] + [(None, 1, at) for at in range(tail_width // width)]

    def pull_work(evens, spectrum, key, value):
        inner = Order()
        blocks = [fill_blocks(part, reach, -1) for part in evens]
        pulled = None
        for at in range(parts):
            pulled = inner.step(
                lambda spectrum, key, value, blocks, earlier, at=at: convolve_call(
                    pull_kernel,
                    blocks,
                    (pull_pair, push_high, push_rest),
                    spectrum,
                    (key, value),
                    (low_type, low_type),
                    at,
                    seqs_here,
                    earlier,
                ),
                spectrum,
                key,
                value,
                blocks[at],
                pulled,
            )
        return [part.reshape(row_total, features) for part in pulled]

    keys, values = steps.step(
        lambda *values: region(pull_work, *values), grad_evens, spectrum, key_rows, value_rows
    )
    run("w0", "w1", "n0", "o")

    def mixer_work(keys, values, normed, query, grad_middle, kernel_rows, second_sums):
        inner = Order()
        lefts = inner.step(
            lambda v: [choose(v, 0, order, each) for each in both for order in (up_order, down_order)], normed
        )
        grad_tokens, first_sums = inner.step(
            lambda grad_middle, query, keys, values: last_call(
                flat_tokens, grad_middle, first_gain, mixer_input, query, [keys], [values]
            ),
            grad_middle,
            query,
            keys,
            values,
        )

        def tail_step(kernel_rows, first_sums, second_sums):
            rows = jnp.concatenate([first_sums[:2], second_sums[:2]], axis=0)
            tail = jnp.concatenate(
                [kernel_rows, jnp.pad(rows.T, ((0, 0), (0, tail_width - tap_count - 4)))], axis=1
            )
            return [choose(tail, 0, up_order, each) for each in both]

        tails = inner.step(tail_step, kernel_rows, first_sums, second_sums)
        moved_values = swap(
            inner.step(lambda *pair: dots(pair[:1], pair[1:], value_layout), lefts[1], values), "seq", 1
        )
        moved_keys = swap(
            inner.step(
                lambda left, *rights: dots([left], rights, key_layout, None, width), lefts[0], keys, tails[0]
            ),
            "seq",
            1,
        )
        value_pair = inner.step(
            lambda left, values, moved: dots([left], [values], value_layout, moved),
            lefts[3],
            values,
            moved_values,
        )
        key_pair = inner.step(
            lambda left, keys, tail, moved: dots([left], [keys, tail], key_layout, moved, width),
            lefts[2],
            keys,
            tails[1],
            moved_keys,
        )
        return key_pair, value_pair, grad_tokens

    key_pair, value_pair, grad_tokens = steps.step(
        lambda *values: region(mixer_work, *values),
        keys,
        values,
        normed_columns,
        grad_query,
        grad_middle,
        kernel_rows,
        sum(second_sums),
    )
    starts["k"], starts["v"] = (key_pair, up_order), (value_pair, down_order)
    run("w0", "+k", "+v", "n0", "n1", "w0", "w1", "o", "v", "n0", "w0", "w1", "n1", "k")
    run("v", "o", "n0", "w1", "k", "n1", "v", "o", "n0", "k", "n1", "v", "o", "k")
    run("n1", "v", "k")

    output_total, key_total, value_total = (flows[name].values for name in "okv")
    edge = features + tap_count
    return (
        block_output.reshape(block_shape),
        grad_tokens.reshape(block_shape),
        key_total[:, edge],
        key_total[:, edge + 1],
        jnp.concatenate([output_total[:, features:], key_total[:, :features], value_total], axis=1),
        tap_share(key_total[:, features:edge]),
        output_total[:, :features],
        key_total[:, edge + 2],
        key_total[:, edge + 3],
        jnp.concatenate([flows["w0"].values, flows["w1"].values], axis=1),
        turned_rows([flows["n0"].values[0], flows["n1"].values[0]]),
    )


def solution(mesh):
    in_specs = (
        P("batch", "seq", None),
        P(),
        P(),
        P(),
        P(),
        P(),
        P(),
        P(),
        P(),
        P(),
        P("batch", "seq", None),
    )
    out_specs = (
        P("batch", "seq", None),
        P("batch", "seq", None),
        P("seq"),
        P("seq"),
        P("seq", None),
        P("seq", None),
        P("seq", None),
        P("seq"),
        P("seq"),
        P("seq", None),
        P("seq", None),
    )
    return jax.shard_map(
        on_device, mesh=mesh, in_specs=in_specs, out_specs=out_specs, check_vma=False
    )
```

```python
import functools
import math

import jax
import jax.numpy as jnp
import numpy as np
from jax import lax
from jax.experimental import pallas as pl
from jax.experimental.pallas import tpu as pltpu
from jax.sharding import PartitionSpec as P

norm_epsilon = 1e-05
shrink_level = 0.003
highest = lax.Precision.HIGHEST
low_type = jnp.bfloat16


def split_low(table):
    high = table.astype(np.float32).astype(jnp.bfloat16)
    rest = (table - high.astype(np.float64)).astype(np.float32).astype(jnp.bfloat16)
    return high, rest


@functools.lru_cache(maxsize=None)
def half_tables(block):
    order = np.concatenate([np.arange(0, block, 2), np.arange(1, block, 2)])
    theta = np.pi * (2 * order + 1) / (2 * block)
    place = np.arange(block)
    early = theta[:, None] * place[None, :]
    late = theta[None, :] * (block + place[:, None])
    forward = np.concatenate([np.cos(early), -np.sin(early)], axis=0)
    inverse = np.concatenate([np.cos(late), -np.sin(late)], axis=1) / block
    return forward, inverse


def stacked_pair(table):
    high, rest = split_low(table)
    return np.concatenate([high, rest], axis=1)


def turn(spectrum, block):
    half = block // 2
    real, imag = spectrum[:block], spectrum[block:]
    return jnp.concatenate([imag[:half], -imag[half:], -real[:half], real[half:]], axis=0)


def turn_back(spectrum, block):
    half = block // 2
    first, last = spectrum[:block], spectrum[block:]
    return jnp.concatenate([-last[:half], last[half:], first[:half], -first[half:]], axis=0)


def twice(values):
    rounded = values.astype(low_type)
    return jnp.concatenate([rounded, rounded], axis=0)


def low_dot(left, right):
    return jnp.dot(left, right, preferred_element_type=jnp.float32)


def filtered(block_refs, block, table_ref, filter_ref, conjugate):
    real, imag = 0.0, 0.0
    for place, block_ref in enumerate(block_refs):
        spectrum = low_dot(table_ref[...], twice(block_ref[0]))
        own_real, own_imag = spectrum[:block], spectrum[block:]
        filter_real = filter_ref[place, :block, :]
        filter_imag = filter_ref[place, block:, :]
        if conjugate:
            real += own_real * filter_real + own_imag * filter_imag
            imag += own_imag * filter_real - own_real * filter_imag
        else:
            real += own_real * filter_real - own_imag * filter_imag
            imag += own_real * filter_imag + own_imag * filter_real
    return jnp.concatenate([real, imag], axis=0).astype(low_type)


def convolve_kernel(count, block, table_ref, high_ref, rest_ref, filter_ref, query_ref, *refs):
    convolved_ref, gated_ref = refs[-2:]
    total = filtered(refs[:count], block, table_ref, filter_ref, False)
    convolved = low_dot(high_ref[...], total) + low_dot(rest_ref[...], total)
    convolved_ref[0] = convolved
    gated_ref[0] = (query_ref[0] * convolved).astype(low_type)


def pull_kernel(count, block, table_ref, high_ref, rest_ref, filter_ref, key_ref, value_ref, *refs):
    key_out_ref, value_out_ref = refs[-2:]
    total = filtered(refs[:count], block, table_ref, filter_ref, True)
    pulled = low_dot(high_ref[...], total) + low_dot(rest_ref[...], total)
    key_out_ref[0] = (pulled * value_ref[0]).astype(low_type)
    value_out_ref[0] = (pulled * key_ref[0]).astype(low_type)


def filter_grad_kernel(count, block, table_ref, pull_table_ref, grad_ref, *refs):
    out_ref = refs[-1]

    @pl.when(pl.program_id(1) == 0)
    def _():
        out_ref[...] = jnp.zeros_like(out_ref)

    grad = low_dot(pull_table_ref[...], twice(grad_ref[0]))
    grad_real, grad_imag = grad[:block], grad[block:]
    for place in range(count):
        spectrum = low_dot(table_ref[...], twice(refs[place][0]))
        own_real, own_imag = spectrum[:block], spectrum[block:]
        out_ref[place, :block, :] += grad_real * own_real + grad_imag * own_imag
        out_ref[place, block:, :] += grad_imag * own_real - grad_real * own_imag


def full_spec(shape):
    return pl.BlockSpec(shape, lambda *place: (0,) * len(shape), pipeline_mode=pl.Buffered(1))


def out_spec(shape):
    return pl.BlockSpec(shape, lambda *place: (0,) * len(shape))


def room(megabytes):
    return pltpu.CompilerParams(vmem_limit_bytes=megabytes * 2**20)


def convolve_call(body, blocks, tables, spectrum, extras, out_types, part, whole=None, earlier=None):
    seqs, block, features = blocks[0].shape
    count = len(blocks)
    width = features if count < 8 else 256
    base = part * seqs

    def tile(array_seqs):
        first = 0 if array_seqs == seqs else base
        return pl.BlockSpec((1, block, width), lambda column, seq: (first + seq, 0, column))

    in_specs = [full_spec(table.shape) for table in tables]
    operands = list(tables)
    filter_spec = pl.BlockSpec((count, 2 * block, width), lambda column, seq: (0, 0, column))
    if spectrum is not None:
        in_specs.append(filter_spec)
        operands.append(spectrum)
    arrays = list(extras) + list(blocks)
    in_specs += [tile(array.shape[0]) for array in arrays]
    operands += arrays
    aliases = {}
    if earlier is not None:
        aliases = {len(operands) + at: at for at in range(len(earlier))}
        in_specs += [pl.BlockSpec(memory_space=pl.ANY)] * len(earlier)
        operands += list(earlier)
    if out_types is None:
        out_shape = jax.ShapeDtypeStruct((count, 2 * block, features), jnp.float32)
        out_specs = filter_spec
    else:
        held = seqs if whole is None else whole
        out_shape = [jax.ShapeDtypeStruct((held, block, features), kind) for kind in out_types]
        out_specs = [tile(held)] * len(out_types)
    return pl.pallas_call(
        functools.partial(body, count, block),
        grid=(features // width, seqs),
        in_specs=in_specs,
        out_specs=out_specs,
        out_shape=out_shape,
        input_output_aliases=aliases,
        compiler_params=room(24 if count < 8 else 48),
    )(*operands)


def pull_dot(left, right):
    return lax.dot_general(left, right, (((1,), (1,)), ((), ())), preferred_element_type=jnp.float32)


def first_kernel(tokens_ref, gain_ref, shift_ref, key_weight_ref, value_weight_ref, *refs):
    normed_ref, key_ref, value_ref = refs[:3]
    at = pl.program_id(0)

    @pl.when(at == 0)
    def _():
        unit, _ = norm_parts(tokens_ref[...].astype(jnp.float32))
        normed_ref[...] = (unit * gain_ref[...] + shift_ref[...]).astype(low_type)

    normed = normed_ref[...]
    key = low_dot(normed, key_weight_ref[...])
    value = low_dot(normed, value_weight_ref[...])
    key_ref[...] = key
    value_ref[...] = value
    product = key * value
    rows = refs[3].shape[0]
    for part, product_ref in enumerate(refs[3:]):
        product_ref[...] = product[part * rows : (part + 1) * rows]


def first_call(tokens, gain, shift, weight, parts):
    rows, features = tokens.shape
    columns = 2
    width = features // columns
    row = full_spec((1, features))
    wide = jax.ShapeDtypeStruct((rows, features), jnp.float32)
    block = pl.BlockSpec((rows, width), lambda at: (0, at))
    return pl.pallas_call(
        first_kernel,
        grid=(columns,),
        in_specs=[
            full_spec((rows, features)),
            row,
            row,
            pl.BlockSpec((features, width), lambda at: (0, columns + at)),
            pl.BlockSpec((features, width), lambda at: (0, 2 * columns + at)),
        ],
        out_specs=[out_spec((rows, features)), block, block]
        + [pl.BlockSpec((rows // parts, width), lambda at: (0, at))] * parts,
        out_shape=[jax.ShapeDtypeStruct((rows, features), low_type), wide, wide]
        + [jax.ShapeDtypeStruct((rows // parts, features), jnp.float32)] * parts,
        compiler_params=room(24),
    )(tokens, gain[None], shift[None], weight, weight)


def middle_kernel(last, *refs):
    tokens_ref, cot_ref, mixer_ref, gain_ref, shift_ref, widen_ref, narrow_ref, query_ref = refs[:8]
    gated_ref, convolved_ref = refs[8:10]
    second_columns_ref, gated_columns_ref, active_ref, hidden_out_ref, block_ref = refs[-16:-11]
    grad_middle_ref, branch_ref, grad_query_ref, grad_conv_ref, sums_ref = refs[-11:-6]
    second_ref, middle_ref, unit_ref, inverse_ref, grad_ref, feed_ref = refs[-6:]
    at = pl.program_id(0)

    @pl.when(at == 0)
    def _():
        gated = gated_ref[...]
        middle = tokens_ref[...].astype(jnp.float32) + low_dot(gated, mixer_ref[...])
        unit, inverse = norm_parts(middle)
        middle_ref[...] = middle
        unit_ref[...] = unit
        inverse_ref[...] = inverse
        second = (unit * gain_ref[...] + shift_ref[...]).astype(low_type)
        second_ref[...] = second
        second_columns_ref[...] = second.T
        gated_columns_ref[...] = gated.T
        grad_ref[...] = jnp.zeros_like(grad_ref)
        feed_ref[...] = jnp.zeros_like(feed_ref)

    hidden = low_dot(second_ref[...], widen_ref[...])
    grad_active = pull_dot(cot_ref[...], narrow_ref[...])
    spread = 0.5 + 0.5 * lax.erf(hidden * (1.0 / math.sqrt(2.0)))
    active = (hidden * spread).astype(low_type)
    slope = spread + hidden * (jnp.exp(-0.5 * hidden * hidden) * (1.0 / math.sqrt(2.0 * math.pi)))
    grad_hidden = (grad_active * slope).astype(low_type)
    active_ref[...] = active
    hidden_out_ref[...] = grad_hidden
    grad_ref[...] += pull_dot(grad_hidden, widen_ref[...])
    feed_ref[...] += low_dot(active, narrow_ref[...])

    @pl.when(at == last)
    def _():
        grad, unit = grad_ref[...], unit_ref[...]
        sums_ref[0:1, :] = jnp.sum(grad * unit, axis=0, keepdims=True)
        sums_ref[1:2, :] = jnp.sum(grad, axis=0, keepdims=True)
        sums_ref[2:, :] = jnp.zeros_like(sums_ref[2:, :])
        block_ref[...] = (middle_ref[...] + feed_ref[...]).astype(low_type)
        grad_middle = cot_ref[...].astype(jnp.float32) + norm_pull(
            grad, unit, inverse_ref[...], gain_ref[...]
        )
        grad_middle_ref[...] = grad_middle
        branch = grad_middle.astype(low_type)
        branch_ref[...] = branch
        grad_gated = pull_dot(branch, mixer_ref[...])
        grad_conv_ref[...] = grad_gated * query_ref[...]
        grad_query_ref[...] = (grad_gated * convolved_ref[...]).astype(low_type)


def middle_call(tokens, cot, mixer, gain, shift, widen, narrow, query, gated, convolved, part, earlier=None):
    total, features = tokens.shape
    rows = gated.shape[0]
    hidden_size = widen.shape[1]
    tile = 768 if hidden_size % 768 == 0 else hidden_size
    steps = hidden_size // tile
    single = pl.Buffered(1)
    here = pl.BlockSpec((rows, features), lambda at: (part, 0), pipeline_mode=single)
    alone = full_spec((rows, features))
    row = full_spec((1, features))
    out_here = pl.BlockSpec((rows, features), lambda at: (part, 0))
    columns = pl.BlockSpec((features, rows), lambda at: (0, part))
    hidden_tile = pl.BlockSpec((rows, tile), lambda at: (part, at))
    wide, tall = (total, features), (features, total)
    operands = [tokens, cot, mixer, gain[None], shift[None], widen, narrow, query, gated, convolved]
    in_specs = [
        here,
        here,
        full_spec((features, features)),
        row,
        row,
        pl.BlockSpec((features, tile), lambda at: (0, at)),
        pl.BlockSpec((tile, features), lambda at: (at, 0)),
        here,
        alone,
        alone,
    ]
    aliases = {}
    if earlier is not None:
        aliases = {len(operands) + at: at for at in range(len(earlier))}
        in_specs += [pl.BlockSpec(memory_space=pl.ANY)] * len(earlier)
        operands += list(earlier)
    return pl.pallas_call(
        functools.partial(middle_kernel, steps - 1),
        grid=(steps,),
        in_specs=in_specs,
        out_specs=[columns, columns, hidden_tile, hidden_tile, out_here, out_here, out_here, out_here]
        + [out_spec((rows, features)), out_spec((8, features))],
        out_shape=[
            jax.ShapeDtypeStruct(tall, low_type),
            jax.ShapeDtypeStruct(tall, low_type),
            pltpu.HBM((total, hidden_size), low_type),
            pltpu.HBM((total, hidden_size), low_type),
            jax.ShapeDtypeStruct(wide, low_type),
            jax.ShapeDtypeStruct(wide, jnp.float32),
            jax.ShapeDtypeStruct(wide, low_type),
            jax.ShapeDtypeStruct(wide, low_type),
            jax.ShapeDtypeStruct((rows, features), jnp.float32),
            jax.ShapeDtypeStruct((8, features), jnp.float32),
        ],
        scratch_shapes=[
            pltpu.VMEM((rows, features), low_type),
            pltpu.VMEM((rows, features), jnp.float32),
            pltpu.VMEM((rows, features), jnp.float32),
            pltpu.VMEM((rows, 1), jnp.float32),
            pltpu.VMEM((rows, features), jnp.float32),
            pltpu.VMEM((rows, features), jnp.float32),
        ],
        input_output_aliases=aliases,
        compiler_params=room(32),
    )(*operands)


def last_kernel(chunks, width, tokens_ref, grad_middle_ref, gain_ref, weight_ref, query_ref, *refs):
    key_refs, value_refs = refs[:chunks], refs[chunks : 2 * chunks]
    out_ref, sums_ref, grad_ref = refs[2 * chunks :]
    at = pl.program_id(0)

    @pl.when(at == 0)
    def _():
        grad_ref[...] = pull_dot(query_ref[...], weight_ref[...])

    for place, part_refs in ((1, key_refs), (2, value_refs)):

        @pl.when(at == place)
        def _(part_refs=part_refs):
            total = grad_ref[...]
            for chunk, part_ref in enumerate(part_refs):
                total += pull_dot(part_ref[...], weight_ref[:, chunk * width : (chunk + 1) * width])
            grad_ref[...] = total

    @pl.when(at == 2)
    def _():
        grad = grad_ref[...]
        unit, inverse = norm_parts(tokens_ref[...].astype(jnp.float32))
        sums_ref[0:1, :] = jnp.sum(grad * unit, axis=0, keepdims=True)
        sums_ref[1:2, :] = jnp.sum(grad, axis=0, keepdims=True)
        sums_ref[2:, :] = jnp.zeros_like(sums_ref[2:, :])
        out_ref[...] = (grad_middle_ref[...] + norm_pull(grad, unit, inverse, gain_ref[...])).astype(low_type)


def last_call(tokens, grad_middle, gain, weight, query, keys, values):
    rows, features = tokens.shape
    chunks = len(keys)
    width = features // chunks
    full = full_spec((rows, features))
    return pl.pallas_call(
        functools.partial(last_kernel, chunks, width),
        grid=(3,),
        in_specs=[
            full,
            full,
            full_spec((1, features)),
            pl.BlockSpec((features, features), lambda at: (0, at)),
            full,
        ]
        + [full_spec((rows, width))] * (2 * chunks),
        out_specs=[out_spec((rows, features)), out_spec((8, features))],
        out_shape=[
            jax.ShapeDtypeStruct((rows, features), low_type),
            jax.ShapeDtypeStruct((8, features), jnp.float32),
        ],
        scratch_shapes=[pltpu.VMEM((rows, features), jnp.float32)],
        compiler_params=room(24),
    )(tokens, grad_middle, gain[None], weight, query, *keys, *values)


def columns_kernel(layout, left_count, right_count, split, *refs):
    left_refs, refs = refs[:left_count], refs[left_count:]
    right_refs, refs = refs[:right_count], refs[right_count:]
    for place, (left, right, column) in enumerate(layout):

        @pl.when(pl.program_id(0) == place)
        def _(left=left, right=right, column=column):
            width = refs[-1].shape[1]
            values = right_refs[right][:, column * width : (column + 1) * width]
            result = values if left is None else low_dot(left_refs[left][...], values)
            if split:
                half = result.shape[0] // 2
                result = result + refs[0][...]
                refs[1][...] = result[:half]
                refs[2][...] = result[half:]
            else:
                refs[-1][...] = result


def columns_call(lefts, rights, layout, width, moved=None, kind=jax.ShapeDtypeStruct):
    rows = lefts[0].shape[0]
    total = width * len(layout)
    split = moved is not None
    block = pl.BlockSpec((rows, width), lambda at: (0, at))
    if split:
        out_specs = [pl.BlockSpec((rows // 2, width), lambda at: (0, at))] * 2
        out_shape = [kind((rows // 2, total), jnp.float32)] * 2
    else:
        out_specs, out_shape = block, kind((rows, total), jnp.float32)
    in_specs = [full_spec(left.shape) for left in lefts]
    base = layout[0][2]
    if len(layout) > 1 and layout == [(0, 0, base + at) for at in range(len(layout))]:
        in_specs.append(pl.BlockSpec((rights[0].shape[0], width), lambda at: (0, base + at)))
        layout = [(0, 0, 0)] * len(layout)
    else:
        in_specs += [full_spec(right.shape) for right in rights]
    operands = [*lefts, *rights]
    if split:
        in_specs.append(block)
        operands.append(moved)
    return pl.pallas_call(
        functools.partial(columns_kernel, layout, len(lefts), len(rights), split),
        grid=(len(layout),),
        in_specs=in_specs,
        out_specs=out_specs,
        out_shape=out_shape,
        compiler_params=room(16),
    )(*operands)


def narrow_kernel(count, owner_ref, left_ref, right_ref, *refs):
    result = low_dot(left_ref[...], right_ref[...])
    if len(refs) == 1:
        refs[0][0] = result
        return
    result = result + refs[0][0]
    half = result.shape[0] // 2
    first = pl.program_id(0) < count // 2

    @pl.when(first)
    def _():
        refs[2][0] = result[:half]
        refs[4][0] = result[half:]

    @pl.when(jnp.logical_not(first))
    def _():
        refs[1][0] = result[:half]
        refs[3][0] = result[half:]


def narrow_grad(left, right, order, core, moved=None):
    size = lax.axis_size("seq")
    rows, depth = left.shape
    columns = right.shape[1] // size
    count = size // 2
    held = rows // 2
    if columns % 128:
        chosen = choose(right, 1, order, core).reshape(depth, count, columns)
        result = jnp.einsum("mt,tcp->cmp", left, chosen, preferred_element_type=jnp.float32)
        if moved is None:
            return result
        result = result + moved
        return [part for at in range(2) for part in cut(result[:, at * held : (at + 1) * held], 0)]
    owners = jnp.stack(owner_list(order, core)).astype(jnp.int32)
    half = count // 2

    def turned(at):
        return lax.rem(at + half, count) if moved is not None else at

    in_specs = [
        pl.BlockSpec((rows, depth), lambda at, owner: (0, 0), pipeline_mode=pl.Buffered(1)),
        pl.BlockSpec((depth, columns), lambda at, owner: (0, owner[turned(at)])),
    ]
    if moved is None:
        operands = []
        out_specs = pl.BlockSpec((1, rows, columns), lambda at, owner: (at, 0, 0))
        out_shape = pltpu.HBM((count, rows, columns), jnp.float32)
    else:
        operands = [moved]
        in_specs.append(pl.BlockSpec((1, rows, columns), lambda at, owner: (turned(at), 0, 0)))
        out_specs = [
            pl.BlockSpec((1, held, columns), lambda at, owner: (jnp.maximum(at - half, 0), 0, 0)),
            pl.BlockSpec((1, held, columns), lambda at, owner: (jnp.minimum(at, half - 1), 0, 0)),
        ] * 2
        out_shape = [pltpu.HBM((half, held, columns), jnp.float32)] * 4
    return pl.pallas_call(
        functools.partial(narrow_kernel, count),
        grid_spec=pltpu.PrefetchScalarGridSpec(
            num_scalar_prefetch=1, grid=(count,), in_specs=in_specs, out_specs=out_specs
        ),
        out_shape=out_shape,
        compiler_params=room(16),
    )(owners, left, right, *operands)


def turn_kernel(*refs):
    rows = refs[0].shape[0]
    for at, ref in enumerate(refs[:-1]):
        refs[-1][:, at * rows : (at + 1) * rows] = ref[...].T


def turned_rows(parts):
    rows, columns = parts[0].shape
    shape = (columns, rows * len(parts))
    if columns % 128:
        return jnp.concatenate(parts, axis=0).T
    return pl.pallas_call(
        turn_kernel, out_shape=jax.ShapeDtypeStruct(shape, jnp.float32), compiler_params=room(16)
    )(*parts)


def partner_pairs(size, step):
    return [(place, place ^ step) for place in range(size)]


def swap(values, axis, step):
    return lax.ppermute(values, axis, partner_pairs(lax.axis_size(axis), step))


def start_blocks(own, count, sign):
    size = lax.axis_size("seq")
    blocks = [own]
    for pair in range(1, (count + 1) // 2 + 1):
        step = sign * 2 * pair
        pairs = [(a, a + step) for a in range(size) if 0 <= a + step < size]
        blocks.append(lax.ppermute(own, "seq", pairs))
    return blocks


def fill_blocks(evens, count, sign):
    core = lax.axis_index("seq") & 1
    blocks = [evens[0]]
    for near, far in zip(evens[:-1], evens[1:]):
        sent = jnp.where((core == 0) == (sign > 0), near, far)
        blocks += [swap(sent, "seq", 1), far]
    return blocks[: count + 1]


def core_swap(values):
    size = lax.axis_size("seq")
    groups = [[place, place + 1] for place in range(0, size, 2)]
    return lax.all_to_all(values, "seq", 0, 0, axis_index_groups=groups)


def swap_blocks(evens, count, sign):
    core = lax.axis_index("seq") & 1
    blocks = [evens[0]]
    for near, far in zip(evens[:-1], evens[1:]):
        moved = core_swap(jnp.stack([far, near] if sign > 0 else [near, far]))
        blocks += [lax.dynamic_index_in_dim(moved, 1 - core, 0, keepdims=False), far]
    return blocks[: count + 1]


def later(ready, values):
    first = jax.tree.leaves(ready)[0]
    small = lax.slice(first, (0,) * first.ndim, (1,) * (first.ndim - 2) + (8, 128))
    tied, values, _ = lax.optimization_barrier((ready, values, swap(small, "seq", 1)))
    return tied, values


def region(work, *values):
    shapes = jax.eval_shape(work, *values)

    def idle(*values):
        return jax.tree.map(lambda shape: jnp.zeros(shape.shape, shape.dtype), shapes)

    always = lax.axis_index("seq") < lax.axis_size("seq")
    return lax.cond(always, work, idle, *values)


class Order:
    def __init__(self):
        self.last = None

    def step(self, work, *values):
        if self.last is not None:
            values, _ = lax.optimization_barrier((values, self.last))
        result = work(*values)
        self.last = result
        return result


def owner_list(order, core):
    chip = lax.axis_index("seq") >> 1
    count = len(order)
    owners = []
    for place in range(1 << count):
        relative = sum(((place >> (count - 1 - at)) & 1) << (bit - 1) for at, bit in enumerate(order))
        owners.append(((chip ^ relative) << 1) | core)
    return owners


def choose(values, dim, order, core):
    size = lax.axis_size("seq")
    part = values.shape[dim] // size
    return jnp.concatenate(
        [
            lax.dynamic_slice_in_dim(values, owner * part, part, dim)
            for owner in owner_list(order, core)
        ],
        axis=dim,
    )


def cut(values, dim):
    half = values.shape[dim] // 2
    return lax.slice_in_dim(values, 0, half, axis=dim), lax.slice_in_dim(values, half, 2 * half, axis=dim)


class Piece:
    def __init__(self, kept, moved, dim, order):
        self.kept, self.dim, self.order = kept, dim, order
        self.arriving = swap(moved, "seq", 1 << order[0])
        self.done = 1

    def advance(self, steps):
        bit = self.order[self.done]
        self.done += 1

        def work(kept, arriving):
            keep, move = cut(kept, self.dim)
            arrived_keep, arrived_move = cut(arriving, self.dim)
            return keep + arrived_keep, move + arrived_move

        self.kept, moved = steps.step(work, self.kept, self.arriving)
        self.arriving = swap(moved, "seq", 1 << bit)

    def finish(self, steps):
        while self.done < len(self.order):
            self.advance(steps)
        return steps.step(lambda kept, arriving: kept + arriving, self.kept, self.arriving)


class BatchSum:
    def __init__(self, values):
        self.size = lax.axis_size("batch")
        self.values = values
        self.stage = 0
        if self.size == 4:
            self.arriving = lax.ppermute(values, "batch", [(0, 1), (3, 2)])
        else:
            self.arriving = None

    def advance(self, steps):
        if self.size != 4:
            if self.stage == 0:
                self.values = lax.psum(self.values, "batch")
        elif self.stage < 2:
            self.values = steps.step(lambda values, arriving: values + arriving, self.values, self.arriving)
            pairs = [(1, 2), (2, 1)] if self.stage == 0 else [(1, 0), (2, 3)]
            self.arriving = lax.ppermute(self.values, "batch", pairs)
        else:
            place = lax.axis_index("batch")
            middle = (place == 1) | (place == 2)
            self.values = steps.step(
                lambda values, arriving: jnp.where(middle, values, arriving), self.values, self.arriving
            )
        self.stage += 1


def norm_parts(values):
    centered = values - jnp.mean(values, axis=-1, keepdims=True)
    inverse = lax.rsqrt(jnp.mean(centered * centered, axis=-1, keepdims=True) + norm_epsilon)
    return centered * inverse, inverse


def norm_pull(grad, unit, inverse, gain):
    scaled = grad * gain
    return inverse * (
        scaled
        - jnp.mean(scaled, axis=-1, keepdims=True)
        - unit * jnp.mean(scaled * unit, axis=-1, keepdims=True)
    )


def shape_kernel(raw_kernel):
    shrunk = raw_kernel - shrink_level * jnp.tanh(raw_kernel / shrink_level)
    padded = jnp.pad(shrunk, ((1, 1), (0, 0)))
    return (padded[:-2] + padded[1:-1] + padded[2:]) / 3.0


def tap_rows(values):
    taps, features = values.shape
    return values.reshape(features, taps)


def tap_share(values):
    size = lax.axis_size("seq")
    rows, taps = values.shape
    return values.reshape(taps // size, rows * size)


def wide_dot(left, right):
    return jnp.dot(left, right, preferred_element_type=jnp.float32)


def token_dot(left, right):
    return lax.dot_general(left, right, (((0,), (0,)), ((), ())), preferred_element_type=jnp.float32)


def weight_dot(left, right):
    return lax.dot_general(left, right, (((1,), (1,)), ((), ())), preferred_element_type=jnp.float32)


def on_device(
    tokens,
    first_gain,
    first_shift,
    mixer_input,
    conv_kernel,
    mixer_output,
    second_gain,
    second_shift,
    widen_weight,
    narrow_weight,
    cotangent,
):
    axis_count = lax.axis_size("seq")
    core = lax.axis_index("seq") & 1
    other = 1 - core
    seqs_here, local_len, features = tokens.shape
    row_total = seqs_here * local_len
    tap_count = conv_kernel.shape[0]
    reach = -(-tap_count // local_len)
    block_shape = tokens.shape
    parts = 2 if seqs_here % 2 == 0 else 1
    part_shape = (seqs_here // parts, local_len, features)
    part_rows = row_total // parts
    bits = axis_count.bit_length() - 1
    down_order = list(range(bits - 1, 0, -1))
    up_order = list(range(1, bits))
    steps = Order()

    forward, inverse = half_tables(local_len)
    forward_pair = jnp.asarray(stacked_pair(forward))
    inverse_high, inverse_rest = (jnp.asarray(part) for part in split_low(inverse))
    pull_pair = jnp.asarray(stacked_pair(inverse.T))
    push_high, push_rest = (jnp.asarray(part) for part in split_low(forward.T))

    flat_tokens = tokens.reshape(row_total, features)
    flat_cot = cotangent.reshape(row_total, features)

    normed_low, key_rows, value_rows, *products = steps.step(
        lambda values: first_call(values, first_gain, first_shift, mixer_input, parts), flat_tokens
    )
    key_rows = key_rows.reshape(block_shape)
    value_rows = value_rows.reshape(block_shape)
    product_evens = [start_blocks(products[0].reshape(part_shape), reach, 1)]

    raw_kernel = conv_kernel.astype(jnp.float32)

    def filter_step(raw_kernel):
        kernel_taps = shape_kernel(raw_kernel)
        tap_blocks = jnp.pad(kernel_taps, ((0, reach * local_len - tap_count), (0, 0))).reshape(
            reach, local_len, features
        )
        table = jnp.asarray(forward.astype(np.float32))
        tap_spectra = [jnp.dot(table, tap_blocks[place], precision=highest) for place in range(reach)]
        spectra = []
        for place in range(reach + 1):
            terms = []
            if place > 0:
                terms.append(tap_spectra[place - 1])
            if place < reach:
                terms.append(turn(tap_spectra[place], local_len))
            spectra.append(sum(terms))
        return jnp.stack(spectra)

    cot_columns = steps.step(jnp.transpose, flat_cot)
    normed_columns = steps.step(jnp.transpose, normed_low)
    query_rows = steps.step(
        lambda rows, weight: wide_dot(rows, weight), normed_low, mixer_input[:, :features]
    )
    spectrum = steps.step(filter_step, raw_kernel)
    for part in products[1:]:
        part, _ = lax.optimization_barrier((part, steps.last))
        product_evens.append(start_blocks(part.reshape(part_shape), reach, 1))

    def convolve_part(at, query, spectrum, blocks):
        result = convolve_call(
            convolve_kernel,
            blocks,
            (forward_pair, inverse_high, inverse_rest),
            spectrum,
            (query,),
            (jnp.float32, low_type),
            at,
        )
        return [values.reshape(part_rows, features) for values in result]

    middle_parts, product_blocks, grad_conv, grad_evens, second_sums = None, [], [], [], []
    for at in range(parts):
        fill = swap_blocks if at == 0 else fill_blocks
        blocks = steps.step(lambda evens, fill=fill: fill(evens, reach, 1), product_evens[at])
        convolved, gated = steps.step(
            functools.partial(convolve_part, at), query_rows.reshape(block_shape), spectrum, blocks
        )
        product_blocks.append(blocks)
        *middle_parts, grad, sums = steps.step(
            lambda query, gated, convolved, earlier, at=at: middle_call(
                flat_tokens,
                flat_cot,
                mixer_output,
                second_gain,
                second_shift,
                widen_weight,
                narrow_weight,
                query,
                gated,
                convolved,
                at,
                earlier,
            ),
            query_rows,
            gated,
            convolved,
            middle_parts,
        )
        grad_conv.append(grad.reshape(part_shape))
        grad_evens.append(start_blocks(grad_conv[at], reach, -1))
        second_sums.append(sums)
    (
        second_columns,
        gated_columns,
        active_low,
        grad_hidden,
        block_output,
        grad_middle,
        grad_branch,
        grad_query,
    ) = middle_parts

    tiles = grad_hidden.shape[1] // 2 // features
    half_layouts = [[(0, 0, half * tiles + at) for at in range(tiles)] for half in range(2)]
    output_layout = [(0, 0, 0), (1, 1, 0)]
    both = (other, core)

    def dots(lefts, rights, layout, moved=None, width=features):
        return columns_call(lefts, rights, layout, width, moved, kind=pltpu.HBM)

    def widen_work(second_columns, grad_hidden):
        inner = Order()
        lefts = inner.step(
            lambda v: [choose(v, 0, order, each) for each in both for order in widen_orders], second_columns
        )
        moved = [
            swap(inner.step(lambda *pair, half=half: dots(pair[:1], pair[1:], half), left, grad_hidden), "seq", 1)
            for half, left in zip(half_layouts, lefts[:2])
        ]
        return [
            inner.step(
                lambda left, right, moved, half=half: dots([left], [right], half, moved), left, grad_hidden, part
            )
            for half, left, part in zip(half_layouts, lefts[2:], moved)
        ]

    def narrow_work(cot_columns, active, gated, normed, branch, query):
        inner = Order()
        moved = swap(
            inner.step(lambda *pair: narrow_grad(*pair, down_order, other), cot_columns, active), "seq", 1
        )
        lefts = inner.step(
            lambda *pair: [choose(values, 0, up_order, each) for each in both for values in pair],
            gated,
            normed,
        )
        moved_output = swap(
            inner.step(
                lambda lefts, *rights: dots(lefts, rights, output_layout), lefts[:2], branch, query
            ),
            "seq",
            1,
        )
        narrow = inner.step(
            lambda left, right, moved: narrow_grad(left, right, down_order, core, moved),
            cot_columns,
            active,
            moved,
        )
        output = inner.step(
            lambda lefts, branch, query, moved: dots(lefts, [branch, query], output_layout, moved),
            lefts[2:],
            branch,
            query,
            moved_output,
        )
        return narrow[:2], narrow[2:], output

    starts, flows = {}, {}

    def run(*plan):
        for name in plan:
            if name[0] == "+":
                (kept, moved), order = starts[name[1:]]
                moved, _ = lax.optimization_barrier((moved, steps.last))
                flows[name[1:]] = Piece(kept, moved, 0, order)
                continue
            flow = flows[name]
            if isinstance(flow, BatchSum):
                flow.advance(steps)
            elif flow.done < len(flow.order):
                flow.advance(steps)
            else:
                flows[name] = BatchSum(flow.finish(steps))

    widen_orders = (up_order, down_order)
    second_columns, grad_evens[0] = lax.optimization_barrier((second_columns, grad_evens[0]))
    pairs = steps.step(lambda *values: region(widen_work, *values), second_columns, grad_hidden)
    pairs, grad_evens = lax.optimization_barrier((pairs, grad_evens))
    starts["w0"], starts["w1"] = zip(pairs, widen_orders)
    run("+w0", "+w1")
    grad_evens, cot_columns = later(grad_evens, cot_columns)
    pairs = steps.step(
        lambda *values: region(narrow_work, *values),
        cot_columns,
        active_low,
        gated_columns,
        normed_columns,
        grad_branch,
        grad_query,
    )
    starts["n0"], starts["n1"], starts["o"] = zip(pairs, (down_order, down_order, up_order))
    run("+n0", "+o", "w0", "w1", "+n1")

    grad_spectrum = [
        steps.step(
            lambda grad, blocks, at=at: convolve_call(
                filter_grad_kernel, blocks, (forward_pair, pull_pair), None, (grad,), None, at
            ),
            grad_conv[at],
            product_blocks[at],
        )
        for at in range(parts)
    ]

    def taps_step(raw_kernel, *terms):
        grad_spectrum = sum(terms)
        back_table = jnp.asarray(forward.T.astype(np.float32))
        grad_taps = jnp.concatenate(
            [
                jnp.dot(
                    back_table,
                    grad_spectrum[place + 1] + turn_back(grad_spectrum[place], local_len),
                    precision=highest,
                )
                for place in range(reach)
            ]
        )[:tap_count]
        padded = jnp.pad(grad_taps, ((1, 1), (0, 0)))
        return (
            (padded[:-2] + padded[1:-1] + padded[2:]) / 3.0 * jnp.tanh(raw_kernel / shrink_level) ** 2
        )

    kernel_rows = steps.step(
        lambda *values: tap_rows(taps_step(*values)), raw_kernel, *grad_spectrum
    )

    width = features // 2
    tail_width = -(-(tap_count + 4) // width) * width
    value_layout = [(0, 0, 0)]
    key_layout = [(0, 0, at) for at in range(2)] + [(None, 1, at) for at in range(tail_width // width)]

    def pull_work(evens, spectrum, key, value):
        inner = Order()
        blocks = [fill_blocks(part, reach, -1) for part in evens]
        pulled = None
        for at in range(parts):
            pulled = inner.step(
                lambda spectrum, key, value, blocks, earlier, at=at: convolve_call(
                    pull_kernel,
                    blocks,
                    (pull_pair, push_high, push_rest),
                    spectrum,
                    (key, value),
                    (low_type, low_type),
                    at,
                    seqs_here,
                    earlier,
                ),
                spectrum,
                key,
                value,
                blocks[at],
                pulled,
            )
        return [part.reshape(row_total, features) for part in pulled]

    keys, values = steps.step(
        lambda *values: region(pull_work, *values), grad_evens, spectrum, key_rows, value_rows
    )
    run("w0", "w1", "n0", "o")

    def mixer_work(keys, values, normed, query, grad_middle, kernel_rows, second_sums):
        inner = Order()
        lefts = inner.step(
            lambda v: [choose(v, 0, order, each) for each in both for order in (up_order, down_order)], normed
        )
        grad_tokens, first_sums = inner.step(
            lambda grad_middle, query, keys, values: last_call(
                flat_tokens, grad_middle, first_gain, mixer_input, query, [keys], [values]
            ),
            grad_middle,
            query,
            keys,
            values,
        )

        def tail_step(kernel_rows, first_sums, second_sums):
            rows = jnp.concatenate([first_sums[:2], second_sums[:2]], axis=0)
            tail = jnp.concatenate(
                [kernel_rows, jnp.pad(rows.T, ((0, 0), (0, tail_width - tap_count - 4)))], axis=1
            )
            return [choose(tail, 0, up_order, each) for each in both]

        tails = inner.step(tail_step, kernel_rows, first_sums, second_sums)
        moved_values = swap(
            inner.step(lambda *pair: dots(pair[:1], pair[1:], value_layout), lefts[1], values), "seq", 1
        )
        moved_keys = swap(
            inner.step(
                lambda left, *rights: dots([left], rights, key_layout, None, width), lefts[0], keys, tails[0]
            ),
            "seq",
            1,
        )
        value_pair = inner.step(
            lambda left, values, moved: dots([left], [values], value_layout, moved),
            lefts[3],
            values,
            moved_values,
        )
        key_pair = inner.step(
            lambda left, keys, tail, moved: dots([left], [keys, tail], key_layout, moved, width),
            lefts[2],
            keys,
            tails[1],
            moved_keys,
        )
        return key_pair, value_pair, grad_tokens

    key_pair, value_pair, grad_tokens = steps.step(
        lambda *values: region(mixer_work, *values),
        keys,
        values,
        normed_columns,
        grad_query,
        grad_middle,
        kernel_rows,
        sum(second_sums),
    )
    starts["k"], starts["v"] = (key_pair, up_order), (value_pair, down_order)
    run("w0", "+k", "+v", "n0", "n1", "w0", "w1", "o", "v", "n0", "w0", "w1", "n1", "k")
    run("v", "o", "n0", "w1", "k", "n1", "v", "o", "n0", "k", "n1", "v", "o", "k")
    run("n1", "v", "k")

    output_total, key_total, value_total = (flows[name].values for name in "okv")
    edge = features + tap_count
    return (
        block_output.reshape(block_shape),
        grad_tokens.reshape(block_shape),
        key_total[:, edge],
        key_total[:, edge + 1],
        jnp.concatenate([output_total[:, features:], key_total[:, :features], value_total], axis=1),
        tap_share(key_total[:, features:edge]),
        output_total[:, :features],
        key_total[:, edge + 2],
        key_total[:, edge + 3],
        jnp.concatenate([flows["w0"].values, flows["w1"].values], axis=1),
        turned_rows([flows["n0"].values[0], flows["n1"].values[0]]),
    )


def solution(mesh):
    in_specs = (
        P("batch", "seq", None),
        P(),
        P(),
        P(),
        P(),
        P(),
        P(),
        P(),
        P(),
        P(),
        P("batch", "seq", None),
    )
    out_specs = (
        P("batch", "seq", None),
        P("batch", "seq", None),
        P("seq"),
        P("seq"),
        P("seq", None),
        P("seq", None),
        P("seq", None),
        P("seq"),
        P("seq"),
        P("seq", None),
        P("seq", None),
    )
    return jax.shard_map(
        on_device, mesh=mesh, in_specs=in_specs, out_specs=out_specs, check_vma=False
    )
```

```python
import functools
import math

import jax
import jax.numpy as jnp
import numpy as np
from jax import lax
from jax.experimental import pallas as pl
from jax.experimental.pallas import tpu as pltpu
from jax.sharding import PartitionSpec as P

norm_epsilon = 1e-05
shrink_level = 0.003
highest = lax.Precision.HIGHEST
low_type = jnp.bfloat16


def split_low(table):
    high = table.astype(np.float32).astype(jnp.bfloat16)
    rest = (table - high.astype(np.float64)).astype(np.float32).astype(jnp.bfloat16)
    return high, rest


@functools.lru_cache(maxsize=None)
def half_tables(block):
    order = np.concatenate([np.arange(0, block, 2), np.arange(1, block, 2)])
    theta = np.pi * (2 * order + 1) / (2 * block)
    place = np.arange(block)
    early = theta[:, None] * place[None, :]
    late = theta[None, :] * (block + place[:, None])
    forward = np.concatenate([np.cos(early), -np.sin(early)], axis=0)
    inverse = np.concatenate([np.cos(late), -np.sin(late)], axis=1) / block
    return forward, inverse


def stacked_pair(table):
    high, rest = split_low(table)
    return np.concatenate([high, rest], axis=1)


def turn(spectrum, block):
    half = block // 2
    real, imag = spectrum[:block], spectrum[block:]
    return jnp.concatenate([imag[:half], -imag[half:], -real[:half], real[half:]], axis=0)


def turn_back(spectrum, block):
    half = block // 2
    first, last = spectrum[:block], spectrum[block:]
    return jnp.concatenate([-last[:half], last[half:], first[:half], -first[half:]], axis=0)


def twice(values):
    rounded = values.astype(low_type)
    return jnp.concatenate([rounded, rounded], axis=0)


def low_dot(left, right):
    return jnp.dot(left, right, preferred_element_type=jnp.float32)


def filtered(block_refs, block, table_ref, filter_ref, conjugate):
    real, imag = 0.0, 0.0
    for place, block_ref in enumerate(block_refs):
        spectrum = low_dot(table_ref[...], twice(block_ref[0]))
        own_real, own_imag = spectrum[:block], spectrum[block:]
        filter_real = filter_ref[place, :block, :]
        filter_imag = filter_ref[place, block:, :]
        if conjugate:
            real += own_real * filter_real + own_imag * filter_imag
            imag += own_imag * filter_real - own_real * filter_imag
        else:
            real += own_real * filter_real - own_imag * filter_imag
            imag += own_real * filter_imag + own_imag * filter_real
    return jnp.concatenate([real, imag], axis=0).astype(low_type)


def convolve_kernel(count, block, table_ref, high_ref, rest_ref, filter_ref, query_ref, *refs):
    convolved_ref, gated_ref = refs[-2:]
    total = filtered(refs[:count], block, table_ref, filter_ref, False)
    convolved = low_dot(high_ref[...], total) + low_dot(rest_ref[...], total)
    convolved_ref[0] = convolved
    gated_ref[0] = (query_ref[0] * convolved).astype(low_type)


def pull_kernel(count, block, table_ref, high_ref, rest_ref, filter_ref, key_ref, value_ref, *refs):
    key_out_ref, value_out_ref = refs[-2:]
    total = filtered(refs[:count], block, table_ref, filter_ref, True)
    pulled = low_dot(high_ref[...], total) + low_dot(rest_ref[...], total)
    key_out_ref[0] = (pulled * value_ref[0]).astype(low_type)
    value_out_ref[0] = (pulled * key_ref[0]).astype(low_type)


def filter_grad_kernel(count, block, table_ref, pull_table_ref, grad_ref, *refs):
    out_ref = refs[-1]

    @pl.when(pl.program_id(1) == 0)
    def _():
        out_ref[...] = jnp.zeros_like(out_ref)

    grad = low_dot(pull_table_ref[...], twice(grad_ref[0]))
    grad_real, grad_imag = grad[:block], grad[block:]
    for place in range(count):
        spectrum = low_dot(table_ref[...], twice(refs[place][0]))
        own_real, own_imag = spectrum[:block], spectrum[block:]
        out_ref[place, :block, :] += grad_real * own_real + grad_imag * own_imag
        out_ref[place, block:, :] += grad_imag * own_real - grad_real * own_imag


def full_spec(shape):
    return pl.BlockSpec(shape, lambda *place: (0,) * len(shape), pipeline_mode=pl.Buffered(1))


def out_spec(shape):
    return pl.BlockSpec(shape, lambda *place: (0,) * len(shape))


def room(megabytes):
    return pltpu.CompilerParams(vmem_limit_bytes=megabytes * 2**20)


def convolve_call(body, blocks, tables, spectrum, extras, out_types, part, whole=None, earlier=None):
    seqs, block, features = blocks[0].shape
    count = len(blocks)
    width = features if count < 8 else 256
    base = part * seqs

    def tile(array_seqs):
        first = 0 if array_seqs == seqs else base
        return pl.BlockSpec((1, block, width), lambda column, seq: (first + seq, 0, column))

    in_specs = [full_spec(table.shape) for table in tables]
    operands = list(tables)
    filter_spec = pl.BlockSpec((count, 2 * block, width), lambda column, seq: (0, 0, column))
    if spectrum is not None:
        in_specs.append(filter_spec)
        operands.append(spectrum)
    arrays = list(extras) + list(blocks)
    in_specs += [tile(array.shape[0]) for array in arrays]
    operands += arrays
    aliases = {}
    if earlier is not None:
        aliases = {len(operands) + at: at for at in range(len(earlier))}
        in_specs += [pl.BlockSpec(memory_space=pl.ANY)] * len(earlier)
        operands += list(earlier)
    if out_types is None:
        out_shape = jax.ShapeDtypeStruct((count, 2 * block, features), jnp.float32)
        out_specs = filter_spec
    else:
        held = seqs if whole is None else whole
        out_shape = [jax.ShapeDtypeStruct((held, block, features), kind) for kind in out_types]
        out_specs = [tile(held)] * len(out_types)
    return pl.pallas_call(
        functools.partial(body, count, block),
        grid=(features // width, seqs),
        in_specs=in_specs,
        out_specs=out_specs,
        out_shape=out_shape,
        input_output_aliases=aliases,
        compiler_params=room(24 if count < 8 else 48),
    )(*operands)


def pull_dot(left, right):
    return lax.dot_general(left, right, (((1,), (1,)), ((), ())), preferred_element_type=jnp.float32)


def first_kernel(tokens_ref, gain_ref, shift_ref, key_weight_ref, value_weight_ref, *refs):
    normed_ref, key_ref, value_ref = refs[:3]
    at = pl.program_id(0)

    @pl.when(at == 0)
    def _():
        unit, _ = norm_parts(tokens_ref[...].astype(jnp.float32))
        normed_ref[...] = (unit * gain_ref[...] + shift_ref[...]).astype(low_type)

    normed = normed_ref[...]
    key = low_dot(normed, key_weight_ref[...])
    value = low_dot(normed, value_weight_ref[...])
    key_ref[...] = key
    value_ref[...] = value
    product = key * value
    rows = refs[3].shape[0]
    for part, product_ref in enumerate(refs[3:]):
        product_ref[...] = product[part * rows : (part + 1) * rows]


def first_call(tokens, gain, shift, weight, parts):
    rows, features = tokens.shape
    columns = 2
    width = features // columns
    row = full_spec((1, features))
    wide = jax.ShapeDtypeStruct((rows, features), jnp.float32)
    block = pl.BlockSpec((rows, width), lambda at: (0, at))
    return pl.pallas_call(
        first_kernel,
        grid=(columns,),
        in_specs=[
            full_spec((rows, features)),
            row,
            row,
            pl.BlockSpec((features, width), lambda at: (0, columns + at)),
            pl.BlockSpec((features, width), lambda at: (0, 2 * columns + at)),
        ],
        out_specs=[out_spec((rows, features)), block, block]
        + [pl.BlockSpec((rows // parts, width), lambda at: (0, at))] * parts,
        out_shape=[jax.ShapeDtypeStruct((rows, features), low_type), wide, wide]
        + [jax.ShapeDtypeStruct((rows // parts, features), jnp.float32)] * parts,
        compiler_params=room(24),
    )(tokens, gain[None], shift[None], weight, weight)


def middle_kernel(last, *refs):
    tokens_ref, cot_ref, mixer_ref, gain_ref, shift_ref, widen_ref, narrow_ref, query_ref = refs[:8]
    gated_ref, convolved_ref = refs[8:10]
    second_columns_ref, gated_columns_ref, active_ref, hidden_out_ref, block_ref = refs[-16:-11]
    grad_middle_ref, branch_ref, grad_query_ref, grad_conv_ref, sums_ref = refs[-11:-6]
    second_ref, middle_ref, unit_ref, inverse_ref, grad_ref, feed_ref = refs[-6:]
    at = pl.program_id(0)

    @pl.when(at == 0)
    def _():
        gated = gated_ref[...]
        middle = tokens_ref[...].astype(jnp.float32) + low_dot(gated, mixer_ref[...])
        unit, inverse = norm_parts(middle)
        middle_ref[...] = middle
        unit_ref[...] = unit
        inverse_ref[...] = inverse
        second = (unit * gain_ref[...] + shift_ref[...]).astype(low_type)
        second_ref[...] = second
        second_columns_ref[...] = second.T
        gated_columns_ref[...] = gated.T
        grad_ref[...] = jnp.zeros_like(grad_ref)
        feed_ref[...] = jnp.zeros_like(feed_ref)

    hidden = low_dot(second_ref[...], widen_ref[...])
    grad_active = pull_dot(cot_ref[...], narrow_ref[...])
    spread = 0.5 + 0.5 * lax.erf(hidden * (1.0 / math.sqrt(2.0)))
    active = (hidden * spread).astype(low_type)
    slope = spread + hidden * (jnp.exp(-0.5 * hidden * hidden) * (1.0 / math.sqrt(2.0 * math.pi)))
    grad_hidden = (grad_active * slope).astype(low_type)
    active_ref[...] = active
    hidden_out_ref[...] = grad_hidden
    grad_ref[...] += pull_dot(grad_hidden, widen_ref[...])
    feed_ref[...] += low_dot(active, narrow_ref[...])

    @pl.when(at == last)
    def _():
        grad, unit = grad_ref[...], unit_ref[...]
        sums_ref[0:1, :] = jnp.sum(grad * unit, axis=0, keepdims=True)
        sums_ref[1:2, :] = jnp.sum(grad, axis=0, keepdims=True)
        sums_ref[2:, :] = jnp.zeros_like(sums_ref[2:, :])
        block_ref[...] = (middle_ref[...] + feed_ref[...]).astype(low_type)
        grad_middle = cot_ref[...].astype(jnp.float32) + norm_pull(
            grad, unit, inverse_ref[...], gain_ref[...]
        )
        grad_middle_ref[...] = grad_middle
        branch = grad_middle.astype(low_type)
        branch_ref[...] = branch
        grad_gated = pull_dot(branch, mixer_ref[...])
        grad_conv_ref[...] = grad_gated * query_ref[...]
        grad_query_ref[...] = (grad_gated * convolved_ref[...]).astype(low_type)


def middle_call(tokens, cot, mixer, gain, shift, widen, narrow, query, gated, convolved, part, earlier=None):
    total, features = tokens.shape
    rows = gated.shape[0]
    hidden_size = widen.shape[1]
    tile = 768 if hidden_size % 768 == 0 else hidden_size
    steps = hidden_size // tile
    single = pl.Buffered(1)
    here = pl.BlockSpec((rows, features), lambda at: (part, 0), pipeline_mode=single)
    alone = full_spec((rows, features))
    row = full_spec((1, features))
    out_here = pl.BlockSpec((rows, features), lambda at: (part, 0))
    columns = pl.BlockSpec((features, rows), lambda at: (0, part))
    hidden_tile = pl.BlockSpec((rows, tile), lambda at: (part, at))
    wide, tall = (total, features), (features, total)
    operands = [tokens, cot, mixer, gain[None], shift[None], widen, narrow, query, gated, convolved]
    in_specs = [
        here,
        here,
        full_spec((features, features)),
        row,
        row,
        pl.BlockSpec((features, tile), lambda at: (0, at)),
        pl.BlockSpec((tile, features), lambda at: (at, 0)),
        here,
        alone,
        alone,
    ]
    aliases = {}
    if earlier is not None:
        aliases = {len(operands) + at: at for at in range(len(earlier))}
        in_specs += [pl.BlockSpec(memory_space=pl.ANY)] * len(earlier)
        operands += list(earlier)
    return pl.pallas_call(
        functools.partial(middle_kernel, steps - 1),
        grid=(steps,),
        in_specs=in_specs,
        out_specs=[columns, columns, hidden_tile, hidden_tile, out_here, out_here, out_here, out_here]
        + [out_spec((rows, features)), out_spec((8, features))],
        out_shape=[
            jax.ShapeDtypeStruct(tall, low_type),
            jax.ShapeDtypeStruct(tall, low_type),
            pltpu.HBM((total, hidden_size), low_type),
            pltpu.HBM((total, hidden_size), low_type),
            jax.ShapeDtypeStruct(wide, low_type),
            jax.ShapeDtypeStruct(wide, jnp.float32),
            jax.ShapeDtypeStruct(wide, low_type),
            jax.ShapeDtypeStruct(wide, low_type),
            jax.ShapeDtypeStruct((rows, features), jnp.float32),
            jax.ShapeDtypeStruct((8, features), jnp.float32),
        ],
        scratch_shapes=[
            pltpu.VMEM((rows, features), low_type),
            pltpu.VMEM((rows, features), jnp.float32),
            pltpu.VMEM((rows, features), jnp.float32),
            pltpu.VMEM((rows, 1), jnp.float32),
            pltpu.VMEM((rows, features), jnp.float32),
            pltpu.VMEM((rows, features), jnp.float32),
        ],
        input_output_aliases=aliases,
        compiler_params=room(32),
    )(*operands)


def last_kernel(chunks, width, tokens_ref, grad_middle_ref, gain_ref, weight_ref, query_ref, *refs):
    key_refs, value_refs = refs[:chunks], refs[chunks : 2 * chunks]
    out_ref, sums_ref, grad_ref = refs[2 * chunks :]
    at = pl.program_id(0)

    @pl.when(at == 0)
    def _():
        grad_ref[...] = pull_dot(query_ref[...], weight_ref[...])

    for place, part_refs in ((1, key_refs), (2, value_refs)):

        @pl.when(at == place)
        def _(part_refs=part_refs):
            total = grad_ref[...]
            for chunk, part_ref in enumerate(part_refs):
                total += pull_dot(part_ref[...], weight_ref[:, chunk * width : (chunk + 1) * width])
            grad_ref[...] = total

    @pl.when(at == 2)
    def _():
        grad = grad_ref[...]
        unit, inverse = norm_parts(tokens_ref[...].astype(jnp.float32))
        sums_ref[0:1, :] = jnp.sum(grad * unit, axis=0, keepdims=True)
        sums_ref[1:2, :] = jnp.sum(grad, axis=0, keepdims=True)
        sums_ref[2:, :] = jnp.zeros_like(sums_ref[2:, :])
        out_ref[...] = (grad_middle_ref[...] + norm_pull(grad, unit, inverse, gain_ref[...])).astype(low_type)


def last_call(tokens, grad_middle, gain, weight, query, keys, values):
    rows, features = tokens.shape
    chunks = len(keys)
    width = features // chunks
    full = full_spec((rows, features))
    return pl.pallas_call(
        functools.partial(last_kernel, chunks, width),
        grid=(3,),
        in_specs=[
            full,
            full,
            full_spec((1, features)),
            pl.BlockSpec((features, features), lambda at: (0, at)),
            full,
        ]
        + [full_spec((rows, width))] * (2 * chunks),
        out_specs=[out_spec((rows, features)), out_spec((8, features))],
        out_shape=[
            jax.ShapeDtypeStruct((rows, features), low_type),
            jax.ShapeDtypeStruct((8, features), jnp.float32),
        ],
        scratch_shapes=[pltpu.VMEM((rows, features), jnp.float32)],
        compiler_params=room(24),
    )(tokens, grad_middle, gain[None], weight, query, *keys, *values)


def columns_kernel(layout, left_count, right_count, split, *refs):
    left_refs, refs = refs[:left_count], refs[left_count:]
    right_refs, refs = refs[:right_count], refs[right_count:]
    for place, (left, right, column) in enumerate(layout):

        @pl.when(pl.program_id(0) == place)
        def _(left=left, right=right, column=column):
            width = refs[-1].shape[1]
            values = right_refs[right][:, column * width : (column + 1) * width]
            result = values if left is None else low_dot(left_refs[left][...], values)
            if split:
                half = result.shape[0] // 2
                result = result + refs[0][...]
                refs[1][...] = result[:half]
                refs[2][...] = result[half:]
            else:
                refs[-1][...] = result


def columns_call(lefts, rights, layout, width, moved=None, kind=jax.ShapeDtypeStruct):
    rows = lefts[0].shape[0]
    total = width * len(layout)
    split = moved is not None
    block = pl.BlockSpec((rows, width), lambda at: (0, at))
    if split:
        out_specs = [pl.BlockSpec((rows // 2, width), lambda at: (0, at))] * 2
        out_shape = [kind((rows // 2, total), jnp.float32)] * 2
    else:
        out_specs, out_shape = block, kind((rows, total), jnp.float32)
    in_specs = [full_spec(left.shape) for left in lefts]
    base = layout[0][2]
    if len(layout) > 1 and layout == [(0, 0, base + at) for at in range(len(layout))]:
        in_specs.append(pl.BlockSpec((rights[0].shape[0], width), lambda at: (0, base + at)))
        layout = [(0, 0, 0)] * len(layout)
    else:
        in_specs += [full_spec(right.shape) for right in rights]
    operands = [*lefts, *rights]
    if split:
        in_specs.append(block)
        operands.append(moved)
    return pl.pallas_call(
        functools.partial(columns_kernel, layout, len(lefts), len(rights), split),
        grid=(len(layout),),
        in_specs=in_specs,
        out_specs=out_specs,
        out_shape=out_shape,
        compiler_params=room(16),
    )(*operands)


def narrow_kernel(count, owner_ref, left_ref, right_ref, *refs):
    result = low_dot(left_ref[...], right_ref[...])
    if len(refs) == 1:
        refs[0][0] = result
        return
    result = result + refs[0][0]
    half = result.shape[0] // 2
    first = pl.program_id(0) < count // 2

    @pl.when(first)
    def _():
        refs[2][0] = result[:half]
        refs[4][0] = result[half:]

    @pl.when(jnp.logical_not(first))
    def _():
        refs[1][0] = result[:half]
        refs[3][0] = result[half:]


def narrow_grad(left, right, order, core, moved=None):
    size = lax.axis_size("seq")
    rows, depth = left.shape
    columns = right.shape[1] // size
    count = size // 2
    held = rows // 2
    if columns % 128:
        chosen = choose(right, 1, order, core).reshape(depth, count, columns)
        result = jnp.einsum("mt,tcp->cmp", left, chosen, preferred_element_type=jnp.float32)
        if moved is None:
            return result
        result = result + moved
        return [part for at in range(2) for part in cut(result[:, at * held : (at + 1) * held], 0)]
    owners = jnp.stack(owner_list(order, core)).astype(jnp.int32)
    half = count // 2

    def turned(at):
        return lax.rem(at + half, count) if moved is not None else at

    in_specs = [
        pl.BlockSpec((rows, depth), lambda at, owner: (0, 0), pipeline_mode=pl.Buffered(1)),
        pl.BlockSpec((depth, columns), lambda at, owner: (0, owner[turned(at)])),
    ]
    if moved is None:
        operands = []
        out_specs = pl.BlockSpec((1, rows, columns), lambda at, owner: (at, 0, 0))
        out_shape = pltpu.HBM((count, rows, columns), jnp.float32)
    else:
        operands = [moved]
        in_specs.append(pl.BlockSpec((1, rows, columns), lambda at, owner: (turned(at), 0, 0)))
        out_specs = [
            pl.BlockSpec((1, held, columns), lambda at, owner: (jnp.maximum(at - half, 0), 0, 0)),
            pl.BlockSpec((1, held, columns), lambda at, owner: (jnp.minimum(at, half - 1), 0, 0)),
        ] * 2
        out_shape = [pltpu.HBM((half, held, columns), jnp.float32)] * 4
    return pl.pallas_call(
        functools.partial(narrow_kernel, count),
        grid_spec=pltpu.PrefetchScalarGridSpec(
            num_scalar_prefetch=1, grid=(count,), in_specs=in_specs, out_specs=out_specs
        ),
        out_shape=out_shape,
        compiler_params=room(16),
    )(owners, left, right, *operands)


def turn_kernel(*refs):
    rows = refs[0].shape[0]
    for at, ref in enumerate(refs[:-1]):
        refs[-1][:, at * rows : (at + 1) * rows] = ref[...].T


def turned_rows(parts):
    rows, columns = parts[0].shape
    shape = (columns, rows * len(parts))
    if columns % 128:
        return jnp.concatenate(parts, axis=0).T
    return pl.pallas_call(
        turn_kernel, out_shape=jax.ShapeDtypeStruct(shape, jnp.float32), compiler_params=room(16)
    )(*parts)


def partner_pairs(size, step):
    return [(place, place ^ step) for place in range(size)]


def swap(values, axis, step):
    return lax.ppermute(values, axis, partner_pairs(lax.axis_size(axis), step))


def start_blocks(own, count, sign):
    size = lax.axis_size("seq")
    blocks = [own]
    for pair in range(1, (count + 1) // 2 + 1):
        step = sign * 2 * pair
        pairs = [(a, a + step) for a in range(size) if 0 <= a + step < size]
        blocks.append(lax.ppermute(own, "seq", pairs))
    return blocks


def fill_blocks(evens, count, sign):
    core = lax.axis_index("seq") & 1
    blocks = [evens[0]]
    for near, far in zip(evens[:-1], evens[1:]):
        sent = jnp.where((core == 0) == (sign > 0), near, far)
        blocks += [swap(sent, "seq", 1), far]
    return blocks[: count + 1]


def core_swap(values):
    size = lax.axis_size("seq")
    groups = [[place, place + 1] for place in range(0, size, 2)]
    return lax.all_to_all(values, "seq", 0, 0, axis_index_groups=groups)


def swap_blocks(evens, count, sign):
    core = lax.axis_index("seq") & 1
    blocks = [evens[0]]
    for near, far in zip(evens[:-1], evens[1:]):
        moved = core_swap(jnp.stack([far, near] if sign > 0 else [near, far]))
        blocks += [lax.dynamic_index_in_dim(moved, 1 - core, 0, keepdims=False), far]
    return blocks[: count + 1]


def later(ready, values):
    first = jax.tree.leaves(ready)[0]
    small = lax.slice(first, (0,) * first.ndim, (1,) * (first.ndim - 2) + (8, 128))
    tied, values, _ = lax.optimization_barrier((ready, values, swap(small, "seq", 1)))
    return tied, values


def region(work, *values):
    shapes = jax.eval_shape(work, *values)

    def idle(*values):
        return jax.tree.map(lambda shape: jnp.zeros(shape.shape, shape.dtype), shapes)

    always = lax.axis_index("seq") < lax.axis_size("seq")
    return lax.cond(always, work, idle, *values)


class Order:
    def __init__(self):
        self.last = None

    def step(self, work, *values):
        if self.last is not None:
            values, _ = lax.optimization_barrier((values, self.last))
        result = work(*values)
        self.last = result
        return result


def owner_list(order, core):
    chip = lax.axis_index("seq") >> 1
    count = len(order)
    owners = []
    for place in range(1 << count):
        relative = sum(((place >> (count - 1 - at)) & 1) << (bit - 1) for at, bit in enumerate(order))
        owners.append(((chip ^ relative) << 1) | core)
    return owners


def choose(values, dim, order, core):
    size = lax.axis_size("seq")
    part = values.shape[dim] // size
    return jnp.concatenate(
        [
            lax.dynamic_slice_in_dim(values, owner * part, part, dim)
            for owner in owner_list(order, core)
        ],
        axis=dim,
    )


def cut(values, dim):
    half = values.shape[dim] // 2
    return lax.slice_in_dim(values, 0, half, axis=dim), lax.slice_in_dim(values, half, 2 * half, axis=dim)


class Piece:
    def __init__(self, kept, moved, dim, order):
        self.kept, self.dim, self.order = kept, dim, order
        self.arriving = swap(moved, "seq", 1 << order[0])
        self.done = 1

    def advance(self, steps):
        bit = self.order[self.done]
        self.done += 1

        def work(kept, arriving):
            keep, move = cut(kept, self.dim)
            arrived_keep, arrived_move = cut(arriving, self.dim)
            return keep + arrived_keep, move + arrived_move

        self.kept, moved = steps.step(work, self.kept, self.arriving)
        self.arriving = swap(moved, "seq", 1 << bit)

    def finish(self, steps):
        while self.done < len(self.order):
            self.advance(steps)
        return steps.step(lambda kept, arriving: kept + arriving, self.kept, self.arriving)


class BatchSum:
    def __init__(self, values):
        self.size = lax.axis_size("batch")
        self.values = values
        self.stage = 0
        if self.size == 4:
            self.arriving = lax.ppermute(values, "batch", [(0, 1), (3, 2)])
        else:
            self.arriving = None

    def advance(self, steps):
        if self.size != 4:
            if self.stage == 0:
                self.values = lax.psum(self.values, "batch")
        elif self.stage < 2:
            self.values = steps.step(lambda values, arriving: values + arriving, self.values, self.arriving)
            pairs = [(1, 2), (2, 1)] if self.stage == 0 else [(1, 0), (2, 3)]
            self.arriving = lax.ppermute(self.values, "batch", pairs)
        else:
            place = lax.axis_index("batch")
            middle = (place == 1) | (place == 2)
            self.values = steps.step(
                lambda values, arriving: jnp.where(middle, values, arriving), self.values, self.arriving
            )
        self.stage += 1


def norm_parts(values):
    centered = values - jnp.mean(values, axis=-1, keepdims=True)
    inverse = lax.rsqrt(jnp.mean(centered * centered, axis=-1, keepdims=True) + norm_epsilon)
    return centered * inverse, inverse


def norm_pull(grad, unit, inverse, gain):
    scaled = grad * gain
    return inverse * (
        scaled
        - jnp.mean(scaled, axis=-1, keepdims=True)
        - unit * jnp.mean(scaled * unit, axis=-1, keepdims=True)
    )


def shape_kernel(raw_kernel):
    shrunk = raw_kernel - shrink_level * jnp.tanh(raw_kernel / shrink_level)
    padded = jnp.pad(shrunk, ((1, 1), (0, 0)))
    return (padded[:-2] + padded[1:-1] + padded[2:]) / 3.0


def tap_rows(values):
    taps, features = values.shape
    return values.reshape(features, taps)


def tap_share(values):
    size = lax.axis_size("seq")
    rows, taps = values.shape
    return values.reshape(taps // size, rows * size)


def wide_dot(left, right):
    return jnp.dot(left, right, preferred_element_type=jnp.float32)


def token_dot(left, right):
    return lax.dot_general(left, right, (((0,), (0,)), ((), ())), preferred_element_type=jnp.float32)


def weight_dot(left, right):
    return lax.dot_general(left, right, (((1,), (1,)), ((), ())), preferred_element_type=jnp.float32)


def on_device(
    tokens,
    first_gain,
    first_shift,
    mixer_input,
    conv_kernel,
    mixer_output,
    second_gain,
    second_shift,
    widen_weight,
    narrow_weight,
    cotangent,
):
    axis_count = lax.axis_size("seq")
    core = lax.axis_index("seq") & 1
    other = 1 - core
    seqs_here, local_len, features = tokens.shape
    row_total = seqs_here * local_len
    tap_count = conv_kernel.shape[0]
    reach = -(-tap_count // local_len)
    block_shape = tokens.shape
    parts = 2 if seqs_here % 2 == 0 else 1
    part_shape = (seqs_here // parts, local_len, features)
    part_rows = row_total // parts
    bits = axis_count.bit_length() - 1
    down_order = list(range(bits - 1, 0, -1))
    up_order = list(range(1, bits))
    steps = Order()

    forward, inverse = half_tables(local_len)
    forward_pair = jnp.asarray(stacked_pair(forward))
    inverse_high, inverse_rest = (jnp.asarray(part) for part in split_low(inverse))
    pull_pair = jnp.asarray(stacked_pair(inverse.T))
    push_high, push_rest = (jnp.asarray(part) for part in split_low(forward.T))

    flat_tokens = tokens.reshape(row_total, features)
    flat_cot = cotangent.reshape(row_total, features)

    normed_low, key_rows, value_rows, *products = steps.step(
        lambda values: first_call(values, first_gain, first_shift, mixer_input, parts), flat_tokens
    )
    key_rows = key_rows.reshape(block_shape)
    value_rows = value_rows.reshape(block_shape)
    product_evens = [start_blocks(products[0].reshape(part_shape), reach, 1)]

    raw_kernel = conv_kernel.astype(jnp.float32)

    def filter_step(raw_kernel):
        kernel_taps = shape_kernel(raw_kernel)
        tap_blocks = jnp.pad(kernel_taps, ((0, reach * local_len - tap_count), (0, 0))).reshape(
            reach, local_len, features
        )
        table = jnp.asarray(forward.astype(np.float32))
        tap_spectra = [jnp.dot(table, tap_blocks[place], precision=highest) for place in range(reach)]
        spectra = []
        for place in range(reach + 1):
            terms = []
            if place > 0:
                terms.append(tap_spectra[place - 1])
            if place < reach:
                terms.append(turn(tap_spectra[place], local_len))
            spectra.append(sum(terms))
        return jnp.stack(spectra)

    cot_columns = steps.step(jnp.transpose, flat_cot)
    normed_columns = steps.step(jnp.transpose, normed_low)
    query_rows = steps.step(
        lambda rows, weight: wide_dot(rows, weight), normed_low, mixer_input[:, :features]
    )
    spectrum = steps.step(filter_step, raw_kernel)
    for part in products[1:]:
        part, _ = lax.optimization_barrier((part, steps.last))
        product_evens.append(start_blocks(part.reshape(part_shape), reach, 1))

    def convolve_part(at, query, spectrum, blocks):
        result = convolve_call(
            convolve_kernel,
            blocks,
            (forward_pair, inverse_high, inverse_rest),
            spectrum,
            (query,),
            (jnp.float32, low_type),
            at,
        )
        return [values.reshape(part_rows, features) for values in result]

    middle_parts, product_blocks, grad_conv, grad_evens, second_sums = None, [], [], [], []
    for at in range(parts):
        fill = swap_blocks if at == 0 else fill_blocks
        blocks = steps.step(lambda evens, fill=fill: fill(evens, reach, 1), product_evens[at])
        convolved, gated = steps.step(
            functools.partial(convolve_part, at), query_rows.reshape(block_shape), spectrum, blocks
        )
        product_blocks.append(blocks)
        *middle_parts, grad, sums = steps.step(
            lambda query, gated, convolved, earlier, at=at: middle_call(
                flat_tokens,
                flat_cot,
                mixer_output,
                second_gain,
                second_shift,
                widen_weight,
                narrow_weight,
                query,
                gated,
                convolved,
                at,
                earlier,
            ),
            query_rows,
            gated,
            convolved,
            middle_parts,
        )
        grad_conv.append(grad.reshape(part_shape))
        grad_evens.append(start_blocks(grad_conv[at], reach, -1))
        second_sums.append(sums)
    (
        second_columns,
        gated_columns,
        active_low,
        grad_hidden,
        block_output,
        grad_middle,
        grad_branch,
        grad_query,
    ) = middle_parts

    tiles = grad_hidden.shape[1] // 2 // features
    half_layouts = [[(0, 0, half * tiles + at) for at in range(tiles)] for half in range(2)]
    output_layout = [(0, 0, 0), (1, 1, 0)]
    both = (other, core)

    def dots(lefts, rights, layout, moved=None, width=features):
        return columns_call(lefts, rights, layout, width, moved, kind=pltpu.HBM)

    def widen_work(second_columns, grad_hidden):
        inner = Order()
        lefts = inner.step(
            lambda v: [choose(v, 0, order, each) for each in both for order in widen_orders], second_columns
        )
        moved = [
            swap(inner.step(lambda *pair, half=half: dots(pair[:1], pair[1:], half), left, grad_hidden), "seq", 1)
            for half, left in zip(half_layouts, lefts[:2])
        ]
        return [
            inner.step(
                lambda left, right, moved, half=half: dots([left], [right], half, moved), left, grad_hidden, part
            )
            for half, left, part in zip(half_layouts, lefts[2:], moved)
        ]

    def narrow_work(cot_columns, active, gated, normed, branch, query):
        inner = Order()
        moved = swap(
            inner.step(lambda *pair: narrow_grad(*pair, down_order, other), cot_columns, active), "seq", 1
        )
        lefts = inner.step(
            lambda *pair: [choose(values, 0, up_order, each) for each in both for values in pair],
            gated,
            normed,
        )
        moved_output = swap(
            inner.step(
                lambda lefts, *rights: dots(lefts, rights, output_layout), lefts[:2], branch, query
            ),
            "seq",
            1,
        )
        narrow = inner.step(
            lambda left, right, moved: narrow_grad(left, right, down_order, core, moved),
            cot_columns,
            active,
            moved,
        )
        output = inner.step(
            lambda lefts, branch, query, moved: dots(lefts, [branch, query], output_layout, moved),
            lefts[2:],
            branch,
            query,
            moved_output,
        )
        return narrow[:2], narrow[2:], output

    starts, flows = {}, {}

    def run(*plan):
        for name in plan:
            if name[0] == "+":
                (kept, moved), order = starts[name[1:]]
                moved, _ = lax.optimization_barrier((moved, steps.last))
                flows[name[1:]] = Piece(kept, moved, 0, order)
                continue
            flow = flows[name]
            if isinstance(flow, BatchSum):
                flow.advance(steps)
            elif flow.done < len(flow.order):
                flow.advance(steps)
            else:
                flows[name] = BatchSum(flow.finish(steps))

    widen_orders = (up_order, down_order)
    second_columns, grad_evens[0] = lax.optimization_barrier((second_columns, grad_evens[0]))
    pairs = steps.step(lambda *values: region(widen_work, *values), second_columns, grad_hidden)
    pairs, grad_evens = lax.optimization_barrier((pairs, grad_evens))
    starts["w0"], starts["w1"] = zip(pairs, widen_orders)
    run("+w0", "+w1")
    grad_evens, cot_columns = later(grad_evens, cot_columns)
    pairs = steps.step(
        lambda *values: region(narrow_work, *values),
        cot_columns,
        active_low,
        gated_columns,
        normed_columns,
        grad_branch,
        grad_query,
    )
    starts["n0"], starts["n1"], starts["o"] = zip(pairs, (down_order, down_order, up_order))
    run("w0", "w1", "+n0", "+o", "+n1")

    grad_spectrum = [
        steps.step(
            lambda grad, blocks, at=at: convolve_call(
                filter_grad_kernel, blocks, (forward_pair, pull_pair), None, (grad,), None, at
            ),
            grad_conv[at],
            product_blocks[at],
        )
        for at in range(parts)
    ]

    def taps_step(raw_kernel, *terms):
        grad_spectrum = sum(terms)
        back_table = jnp.asarray(forward.T.astype(np.float32))
        grad_taps = jnp.concatenate(
            [
                jnp.dot(
                    back_table,
                    grad_spectrum[place + 1] + turn_back(grad_spectrum[place], local_len),
                    precision=highest,
                )
                for place in range(reach)
            ]
        )[:tap_count]
        padded = jnp.pad(grad_taps, ((1, 1), (0, 0)))
        return (
            (padded[:-2] + padded[1:-1] + padded[2:]) / 3.0 * jnp.tanh(raw_kernel / shrink_level) ** 2
        )

    kernel_rows = steps.step(
        lambda *values: tap_rows(taps_step(*values)), raw_kernel, *grad_spectrum
    )

    width = features // 2
    tail_width = -(-(tap_count + 4) // width) * width
    value_layout = [(0, 0, 0)]
    key_layout = [(0, 0, at) for at in range(2)] + [(None, 1, at) for at in range(tail_width // width)]

    def pull_work(evens, spectrum, key, value):
        inner = Order()
        blocks = [fill_blocks(part, reach, -1) for part in evens]
        pulled = None
        for at in range(parts):
            pulled = inner.step(
                lambda spectrum, key, value, blocks, earlier, at=at: convolve_call(
                    pull_kernel,
                    blocks,
                    (pull_pair, push_high, push_rest),
                    spectrum,
                    (key, value),
                    (low_type, low_type),
                    at,
                    seqs_here,
                    earlier,
                ),
                spectrum,
                key,
                value,
                blocks[at],
                pulled,
            )
        return [part.reshape(row_total, features) for part in pulled]

    run("w0", "w1")
    keys, values = steps.step(
        lambda *values: region(pull_work, *values), grad_evens, spectrum, key_rows, value_rows
    )
    run("n0", "o")

    def mixer_work(keys, values, normed, query, grad_middle, kernel_rows, second_sums):
        inner = Order()
        lefts = inner.step(
            lambda v: [choose(v, 0, order, each) for each in both for order in (up_order, down_order)], normed
        )
        grad_tokens, first_sums = inner.step(
            lambda grad_middle, query, keys, values: last_call(
                flat_tokens, grad_middle, first_gain, mixer_input, query, [keys], [values]
            ),
            grad_middle,
            query,
            keys,
            values,
        )

        def tail_step(kernel_rows, first_sums, second_sums):
            rows = jnp.concatenate([first_sums[:2], second_sums[:2]], axis=0)
            tail = jnp.concatenate(
                [kernel_rows, jnp.pad(rows.T, ((0, 0), (0, tail_width - tap_count - 4)))], axis=1
            )
            return [choose(tail, 0, up_order, each) for each in both]

        tails = inner.step(tail_step, kernel_rows, first_sums, second_sums)
        moved_values = swap(
            inner.step(lambda *pair: dots(pair[:1], pair[1:], value_layout), lefts[1], values), "seq", 1
        )
        moved_keys = swap(
            inner.step(
                lambda left, *rights: dots([left], rights, key_layout, None, width), lefts[0], keys, tails[0]
            ),
            "seq",
            1,
        )
        value_pair = inner.step(
            lambda left, values, moved: dots([left], [values], value_layout, moved),
            lefts[3],
            values,
            moved_values,
        )
        key_pair = inner.step(
            lambda left, keys, tail, moved: dots([left], [keys, tail], key_layout, moved, width),
            lefts[2],
            keys,
            tails[1],
            moved_keys,
        )
        return key_pair, value_pair, grad_tokens

    key_pair, value_pair, grad_tokens = steps.step(
        lambda *values: region(mixer_work, *values),
        keys,
        values,
        normed_columns,
        grad_query,
        grad_middle,
        kernel_rows,
        sum(second_sums),
    )
    starts["k"], starts["v"] = (key_pair, up_order), (value_pair, down_order)
    run("w0", "+k", "+v", "n0", "n1", "w0", "w1", "o", "v", "n0", "w0", "w1", "n1", "k")
    run("v", "o", "n0", "w1", "k", "n1", "v", "o", "n0", "k", "n1", "v", "o", "k")
    run("n1", "v", "k")

    output_total, key_total, value_total = (flows[name].values for name in "okv")
    edge = features + tap_count
    return (
        block_output.reshape(block_shape),
        grad_tokens.reshape(block_shape),
        key_total[:, edge],
        key_total[:, edge + 1],
        jnp.concatenate([output_total[:, features:], key_total[:, :features], value_total], axis=1),
        tap_share(key_total[:, features:edge]),
        output_total[:, :features],
        key_total[:, edge + 2],
        key_total[:, edge + 3],
        jnp.concatenate([flows["w0"].values, flows["w1"].values], axis=1),
        turned_rows([flows["n0"].values[0], flows["n1"].values[0]]),
    )


def solution(mesh):
    in_specs = (
        P("batch", "seq", None),
        P(),
        P(),
        P(),
        P(),
        P(),
        P(),
        P(),
        P(),
        P(),
        P("batch", "seq", None),
    )
    out_specs = (
        P("batch", "seq", None),
        P("batch", "seq", None),
        P("seq"),
        P("seq"),
        P("seq", None),
        P("seq", None),
        P("seq", None),
        P("seq"),
        P("seq"),
        P("seq", None),
        P("seq", None),
    )
    return jax.shard_map(
        on_device, mesh=mesh, in_specs=in_specs, out_specs=out_specs, check_vma=False
    )
```

```python
import functools
import math

import jax
import jax.numpy as jnp
import numpy as np
from jax import lax
from jax.experimental import pallas as pl
from jax.experimental.pallas import tpu as pltpu
from jax.sharding import PartitionSpec as P

norm_epsilon = 1e-05
shrink_level = 0.003
highest = lax.Precision.HIGHEST
low_type = jnp.bfloat16


def split_low(table):
    high = table.astype(np.float32).astype(jnp.bfloat16)
    rest = (table - high.astype(np.float64)).astype(np.float32).astype(jnp.bfloat16)
    return high, rest


@functools.lru_cache(maxsize=None)
def half_tables(block):
    order = np.concatenate([np.arange(0, block, 2), np.arange(1, block, 2)])
    theta = np.pi * (2 * order + 1) / (2 * block)
    place = np.arange(block)
    early = theta[:, None] * place[None, :]
    late = theta[None, :] * (block + place[:, None])
    forward = np.concatenate([np.cos(early), -np.sin(early)], axis=0)
    inverse = np.concatenate([np.cos(late), -np.sin(late)], axis=1) / block
    return forward, inverse


def stacked_pair(table):
    high, rest = split_low(table)
    return np.concatenate([high, rest], axis=1)


def turn(spectrum, block):
    half = block // 2
    real, imag = spectrum[:block], spectrum[block:]
    return jnp.concatenate([imag[:half], -imag[half:], -real[:half], real[half:]], axis=0)


def turn_back(spectrum, block):
    half = block // 2
    first, last = spectrum[:block], spectrum[block:]
    return jnp.concatenate([-last[:half], last[half:], first[:half], -first[half:]], axis=0)


def twice(values):
    rounded = values.astype(low_type)
    return jnp.concatenate([rounded, rounded], axis=0)


def low_dot(left, right):
    return jnp.dot(left, right, preferred_element_type=jnp.float32)


def filtered(block_refs, block, table_ref, filter_ref, conjugate):
    real, imag = 0.0, 0.0
    for place, block_ref in enumerate(block_refs):
        spectrum = low_dot(table_ref[...], twice(block_ref[0]))
        own_real, own_imag = spectrum[:block], spectrum[block:]
        filter_real = filter_ref[place, :block, :]
        filter_imag = filter_ref[place, block:, :]
        if conjugate:
            real += own_real * filter_real + own_imag * filter_imag
            imag += own_imag * filter_real - own_real * filter_imag
        else:
            real += own_real * filter_real - own_imag * filter_imag
            imag += own_real * filter_imag + own_imag * filter_real
    return jnp.concatenate([real, imag], axis=0).astype(low_type)


def convolve_kernel(count, block, table_ref, high_ref, rest_ref, filter_ref, query_ref, *refs):
    convolved_ref, gated_ref = refs[-2:]
    total = filtered(refs[:count], block, table_ref, filter_ref, False)
    convolved = low_dot(high_ref[...], total) + low_dot(rest_ref[...], total)
    convolved_ref[0] = convolved
    gated_ref[0] = (query_ref[0] * convolved).astype(low_type)


def pull_kernel(count, block, table_ref, high_ref, rest_ref, filter_ref, key_ref, value_ref, *refs):
    key_out_ref, value_out_ref = refs[-2:]
    total = filtered(refs[:count], block, table_ref, filter_ref, True)
    pulled = low_dot(high_ref[...], total) + low_dot(rest_ref[...], total)
    key_out_ref[0] = (pulled * value_ref[0]).astype(low_type)
    value_out_ref[0] = (pulled * key_ref[0]).astype(low_type)


def filter_grad_kernel(count, block, table_ref, pull_table_ref, grad_ref, *refs):
    out_ref = refs[-1]

    @pl.when(pl.program_id(1) == 0)
    def _():
        out_ref[...] = jnp.zeros_like(out_ref)

    grad = low_dot(pull_table_ref[...], twice(grad_ref[0]))
    grad_real, grad_imag = grad[:block], grad[block:]
    for place in range(count):
        spectrum = low_dot(table_ref[...], twice(refs[place][0]))
        own_real, own_imag = spectrum[:block], spectrum[block:]
        out_ref[place, :block, :] += grad_real * own_real + grad_imag * own_imag
        out_ref[place, block:, :] += grad_imag * own_real - grad_real * own_imag


def full_spec(shape):
    return pl.BlockSpec(shape, lambda *place: (0,) * len(shape), pipeline_mode=pl.Buffered(1))


def out_spec(shape):
    return pl.BlockSpec(shape, lambda *place: (0,) * len(shape))


def room(megabytes):
    return pltpu.CompilerParams(vmem_limit_bytes=megabytes * 2**20)


def convolve_call(body, blocks, tables, spectrum, extras, out_types, part, whole=None, earlier=None):
    seqs, block, features = blocks[0].shape
    count = len(blocks)
    width = features if count < 8 else 256
    base = part * seqs

    def tile(array_seqs):
        first = 0 if array_seqs == seqs else base
        return pl.BlockSpec((1, block, width), lambda column, seq: (first + seq, 0, column))

    in_specs = [full_spec(table.shape) for table in tables]
    operands = list(tables)
    filter_spec = pl.BlockSpec((count, 2 * block, width), lambda column, seq: (0, 0, column))
    if spectrum is not None:
        in_specs.append(filter_spec)
        operands.append(spectrum)
    arrays = list(extras) + list(blocks)
    in_specs += [tile(array.shape[0]) for array in arrays]
    operands += arrays
    aliases = {}
    if earlier is not None:
        aliases = {len(operands) + at: at for at in range(len(earlier))}
        in_specs += [pl.BlockSpec(memory_space=pl.ANY)] * len(earlier)
        operands += list(earlier)
    if out_types is None:
        out_shape = jax.ShapeDtypeStruct((count, 2 * block, features), jnp.float32)
        out_specs = filter_spec
    else:
        held = seqs if whole is None else whole
        out_shape = [jax.ShapeDtypeStruct((held, block, features), kind) for kind in out_types]
        out_specs = [tile(held)] * len(out_types)
    return pl.pallas_call(
        functools.partial(body, count, block),
        grid=(features // width, seqs),
        in_specs=in_specs,
        out_specs=out_specs,
        out_shape=out_shape,
        input_output_aliases=aliases,
        compiler_params=room(24 if count < 8 else 48),
    )(*operands)


def pull_dot(left, right):
    return lax.dot_general(left, right, (((1,), (1,)), ((), ())), preferred_element_type=jnp.float32)


def first_kernel(tokens_ref, gain_ref, shift_ref, key_weight_ref, value_weight_ref, *refs):
    normed_ref, key_ref, value_ref = refs[:3]
    at = pl.program_id(0)

    @pl.when(at == 0)
    def _():
        unit, _ = norm_parts(tokens_ref[...].astype(jnp.float32))
        normed_ref[...] = (unit * gain_ref[...] + shift_ref[...]).astype(low_type)

    normed = normed_ref[...]
    key = low_dot(normed, key_weight_ref[...])
    value = low_dot(normed, value_weight_ref[...])
    key_ref[...] = key
    value_ref[...] = value
    product = key * value
    rows = refs[3].shape[0]
    for part, product_ref in enumerate(refs[3:]):
        product_ref[...] = product[part * rows : (part + 1) * rows]


def first_call(tokens, gain, shift, weight, parts):
    rows, features = tokens.shape
    columns = 2
    width = features // columns
    row = full_spec((1, features))
    wide = jax.ShapeDtypeStruct((rows, features), jnp.float32)
    block = pl.BlockSpec((rows, width), lambda at: (0, at))
    return pl.pallas_call(
        first_kernel,
        grid=(columns,),
        in_specs=[
            full_spec((rows, features)),
            row,
            row,
            pl.BlockSpec((features, width), lambda at: (0, columns + at)),
            pl.BlockSpec((features, width), lambda at: (0, 2 * columns + at)),
        ],
        out_specs=[out_spec((rows, features)), block, block]
        + [pl.BlockSpec((rows // parts, width), lambda at: (0, at))] * parts,
        out_shape=[jax.ShapeDtypeStruct((rows, features), low_type), wide, wide]
        + [jax.ShapeDtypeStruct((rows // parts, features), jnp.float32)] * parts,
        compiler_params=room(24),
    )(tokens, gain[None], shift[None], weight, weight)


def middle_kernel(last, *refs):
    tokens_ref, cot_ref, mixer_ref, gain_ref, shift_ref, widen_ref, narrow_ref, query_ref = refs[:8]
    gated_ref, convolved_ref = refs[8:10]
    second_columns_ref, gated_columns_ref, active_ref, hidden_out_ref, block_ref = refs[-16:-11]
    grad_middle_ref, branch_ref, grad_query_ref, grad_conv_ref, sums_ref = refs[-11:-6]
    second_ref, middle_ref, unit_ref, inverse_ref, grad_ref, feed_ref = refs[-6:]
    at = pl.program_id(0)

    @pl.when(at == 0)
    def _():
        gated = gated_ref[...]
        middle = tokens_ref[...].astype(jnp.float32) + low_dot(gated, mixer_ref[...])
        unit, inverse = norm_parts(middle)
        middle_ref[...] = middle
        unit_ref[...] = unit
        inverse_ref[...] = inverse
        second = (unit * gain_ref[...] + shift_ref[...]).astype(low_type)
        second_ref[...] = second
        second_columns_ref[...] = second.T
        gated_columns_ref[...] = gated.T
        grad_ref[...] = jnp.zeros_like(grad_ref)
        feed_ref[...] = jnp.zeros_like(feed_ref)

    hidden = low_dot(second_ref[...], widen_ref[...])
    grad_active = pull_dot(cot_ref[...], narrow_ref[...])
    spread = 0.5 + 0.5 * lax.erf(hidden * (1.0 / math.sqrt(2.0)))
    active = (hidden * spread).astype(low_type)
    slope = spread + hidden * (jnp.exp(-0.5 * hidden * hidden) * (1.0 / math.sqrt(2.0 * math.pi)))
    grad_hidden = (grad_active * slope).astype(low_type)
    active_ref[...] = active
    hidden_out_ref[...] = grad_hidden
    grad_ref[...] += pull_dot(grad_hidden, widen_ref[...])
    feed_ref[...] += low_dot(active, narrow_ref[...])

    @pl.when(at == last)
    def _():
        grad, unit = grad_ref[...], unit_ref[...]
        sums_ref[0:1, :] = jnp.sum(grad * unit, axis=0, keepdims=True)
        sums_ref[1:2, :] = jnp.sum(grad, axis=0, keepdims=True)
        sums_ref[2:, :] = jnp.zeros_like(sums_ref[2:, :])
        block_ref[...] = (middle_ref[...] + feed_ref[...]).astype(low_type)
        grad_middle = cot_ref[...].astype(jnp.float32) + norm_pull(
            grad, unit, inverse_ref[...], gain_ref[...]
        )
        grad_middle_ref[...] = grad_middle
        branch = grad_middle.astype(low_type)
        branch_ref[...] = branch
        grad_gated = pull_dot(branch, mixer_ref[...])
        grad_conv_ref[...] = grad_gated * query_ref[...]
        grad_query_ref[...] = (grad_gated * convolved_ref[...]).astype(low_type)


def middle_call(tokens, cot, mixer, gain, shift, widen, narrow, query, gated, convolved, part, earlier=None):
    total, features = tokens.shape
    rows = gated.shape[0]
    hidden_size = widen.shape[1]
    tile = 768 if hidden_size % 768 == 0 else hidden_size
    steps = hidden_size // tile
    single = pl.Buffered(1)
    here = pl.BlockSpec((rows, features), lambda at: (part, 0), pipeline_mode=single)
    alone = full_spec((rows, features))
    row = full_spec((1, features))
    out_here = pl.BlockSpec((rows, features), lambda at: (part, 0))
    columns = pl.BlockSpec((features, rows), lambda at: (0, part))
    hidden_tile = pl.BlockSpec((rows, tile), lambda at: (part, at))
    wide, tall = (total, features), (features, total)
    operands = [tokens, cot, mixer, gain[None], shift[None], widen, narrow, query, gated, convolved]
    in_specs = [
        here,
        here,
        full_spec((features, features)),
        row,
        row,
        pl.BlockSpec((features, tile), lambda at: (0, at)),
        pl.BlockSpec((tile, features), lambda at: (at, 0)),
        here,
        alone,
        alone,
    ]
    aliases = {}
    if earlier is not None:
        aliases = {len(operands) + at: at for at in range(len(earlier))}
        in_specs += [pl.BlockSpec(memory_space=pl.ANY)] * len(earlier)
        operands += list(earlier)
    return pl.pallas_call(
        functools.partial(middle_kernel, steps - 1),
        grid=(steps,),
        in_specs=in_specs,
        out_specs=[columns, columns, hidden_tile, hidden_tile, out_here, out_here, out_here, out_here]
        + [out_spec((rows, features)), out_spec((8, features))],
        out_shape=[
            jax.ShapeDtypeStruct(tall, low_type),
            jax.ShapeDtypeStruct(tall, low_type),
            pltpu.HBM((total, hidden_size), low_type),
            pltpu.HBM((total, hidden_size), low_type),
            jax.ShapeDtypeStruct(wide, low_type),
            jax.ShapeDtypeStruct(wide, jnp.float32),
            jax.ShapeDtypeStruct(wide, low_type),
            jax.ShapeDtypeStruct(wide, low_type),
            jax.ShapeDtypeStruct((rows, features), jnp.float32),
            jax.ShapeDtypeStruct((8, features), jnp.float32),
        ],
        scratch_shapes=[
            pltpu.VMEM((rows, features), low_type),
            pltpu.VMEM((rows, features), jnp.float32),
            pltpu.VMEM((rows, features), jnp.float32),
            pltpu.VMEM((rows, 1), jnp.float32),
            pltpu.VMEM((rows, features), jnp.float32),
            pltpu.VMEM((rows, features), jnp.float32),
        ],
        input_output_aliases=aliases,
        compiler_params=room(32),
    )(*operands)


def last_kernel(chunks, width, tokens_ref, grad_middle_ref, gain_ref, weight_ref, query_ref, *refs):
    key_refs, value_refs = refs[:chunks], refs[chunks : 2 * chunks]
    out_ref, sums_ref, grad_ref = refs[2 * chunks :]
    at = pl.program_id(0)

    @pl.when(at == 0)
    def _():
        grad_ref[...] = pull_dot(query_ref[...], weight_ref[...])

    for place, part_refs in ((1, key_refs), (2, value_refs)):

        @pl.when(at == place)
        def _(part_refs=part_refs):
            total = grad_ref[...]
            for chunk, part_ref in enumerate(part_refs):
                total += pull_dot(part_ref[...], weight_ref[:, chunk * width : (chunk + 1) * width])
            grad_ref[...] = total

    @pl.when(at == 2)
    def _():
        grad = grad_ref[...]
        unit, inverse = norm_parts(tokens_ref[...].astype(jnp.float32))
        sums_ref[0:1, :] = jnp.sum(grad * unit, axis=0, keepdims=True)
        sums_ref[1:2, :] = jnp.sum(grad, axis=0, keepdims=True)
        sums_ref[2:, :] = jnp.zeros_like(sums_ref[2:, :])
        out_ref[...] = (grad_middle_ref[...] + norm_pull(grad, unit, inverse, gain_ref[...])).astype(low_type)


def last_call(tokens, grad_middle, gain, weight, query, keys, values):
    rows, features = tokens.shape
    chunks = len(keys)
    width = features // chunks
    full = full_spec((rows, features))
    return pl.pallas_call(
        functools.partial(last_kernel, chunks, width),
        grid=(3,),
        in_specs=[
            full,
            full,
            full_spec((1, features)),
            pl.BlockSpec((features, features), lambda at: (0, at)),
            full,
        ]
        + [full_spec((rows, width))] * (2 * chunks),
        out_specs=[out_spec((rows, features)), out_spec((8, features))],
        out_shape=[
            jax.ShapeDtypeStruct((rows, features), low_type),
            jax.ShapeDtypeStruct((8, features), jnp.float32),
        ],
        scratch_shapes=[pltpu.VMEM((rows, features), jnp.float32)],
        compiler_params=room(24),
    )(tokens, grad_middle, gain[None], weight, query, *keys, *values)


def columns_kernel(layout, left_count, right_count, split, *refs):
    left_refs, refs = refs[:left_count], refs[left_count:]
    right_refs, refs = refs[:right_count], refs[right_count:]
    for place, (left, right, column) in enumerate(layout):

        @pl.when(pl.program_id(0) == place)
        def _(left=left, right=right, column=column):
            width = refs[-1].shape[1]
            values = right_refs[right][:, column * width : (column + 1) * width]
            result = values if left is None else low_dot(left_refs[left][...], values)
            if split:
                half = result.shape[0] // 2
                result = result + refs[0][...]
                refs[1][...] = result[:half]
                refs[2][...] = result[half:]
            else:
                refs[-1][...] = result


def columns_call(lefts, rights, layout, width, moved=None, kind=jax.ShapeDtypeStruct):
    rows = lefts[0].shape[0]
    total = width * len(layout)
    split = moved is not None
    block = pl.BlockSpec((rows, width), lambda at: (0, at))
    if split:
        out_specs = [pl.BlockSpec((rows // 2, width), lambda at: (0, at))] * 2
        out_shape = [kind((rows // 2, total), jnp.float32)] * 2
    else:
        out_specs, out_shape = block, kind((rows, total), jnp.float32)
    in_specs = [full_spec(left.shape) for left in lefts]
    base = layout[0][2]
    if len(layout) > 1 and layout == [(0, 0, base + at) for at in range(len(layout))]:
        in_specs.append(pl.BlockSpec((rights[0].shape[0], width), lambda at: (0, base + at)))
        layout = [(0, 0, 0)] * len(layout)
    else:
        in_specs += [full_spec(right.shape) for right in rights]
    operands = [*lefts, *rights]
    if split:
        in_specs.append(block)
        operands.append(moved)
    return pl.pallas_call(
        functools.partial(columns_kernel, layout, len(lefts), len(rights), split),
        grid=(len(layout),),
        in_specs=in_specs,
        out_specs=out_specs,
        out_shape=out_shape,
        compiler_params=room(16),
    )(*operands)


def narrow_kernel(count, owner_ref, left_ref, right_ref, *refs):
    result = low_dot(left_ref[...], right_ref[...])
    if len(refs) == 1:
        refs[0][0] = result
        return
    result = result + refs[0][0]
    half = result.shape[0] // 2
    first = pl.program_id(0) < count // 2

    @pl.when(first)
    def _():
        refs[2][0] = result[:half]
        refs[4][0] = result[half:]

    @pl.when(jnp.logical_not(first))
    def _():
        refs[1][0] = result[:half]
        refs[3][0] = result[half:]


def narrow_grad(left, right, order, core, moved=None):
    size = lax.axis_size("seq")
    rows, depth = left.shape
    columns = right.shape[1] // size
    count = size // 2
    held = rows // 2
    if columns % 128:
        chosen = choose(right, 1, order, core).reshape(depth, count, columns)
        result = jnp.einsum("mt,tcp->cmp", left, chosen, preferred_element_type=jnp.float32)
        if moved is None:
            return result
        result = result + moved
        return [part for at in range(2) for part in cut(result[:, at * held : (at + 1) * held], 0)]
    owners = jnp.stack(owner_list(order, core)).astype(jnp.int32)
    half = count // 2

    def turned(at):
        return lax.rem(at + half, count) if moved is not None else at

    in_specs = [
        pl.BlockSpec((rows, depth), lambda at, owner: (0, 0), pipeline_mode=pl.Buffered(1)),
        pl.BlockSpec((depth, columns), lambda at, owner: (0, owner[turned(at)])),
    ]
    if moved is None:
        operands = []
        out_specs = pl.BlockSpec((1, rows, columns), lambda at, owner: (at, 0, 0))
        out_shape = pltpu.HBM((count, rows, columns), jnp.float32)
    else:
        operands = [moved]
        in_specs.append(pl.BlockSpec((1, rows, columns), lambda at, owner: (turned(at), 0, 0)))
        out_specs = [
            pl.BlockSpec((1, held, columns), lambda at, owner: (jnp.maximum(at - half, 0), 0, 0)),
            pl.BlockSpec((1, held, columns), lambda at, owner: (jnp.minimum(at, half - 1), 0, 0)),
        ] * 2
        out_shape = [pltpu.HBM((half, held, columns), jnp.float32)] * 4
    return pl.pallas_call(
        functools.partial(narrow_kernel, count),
        grid_spec=pltpu.PrefetchScalarGridSpec(
            num_scalar_prefetch=1, grid=(count,), in_specs=in_specs, out_specs=out_specs
        ),
        out_shape=out_shape,
        compiler_params=room(16),
    )(owners, left, right, *operands)


def turn_kernel(*refs):
    rows = refs[0].shape[0]
    for at, ref in enumerate(refs[:-1]):
        refs[-1][:, at * rows : (at + 1) * rows] = ref[...].T


def turned_rows(parts):
    rows, columns = parts[0].shape
    shape = (columns, rows * len(parts))
    if columns % 128:
        return jnp.concatenate(parts, axis=0).T
    return pl.pallas_call(
        turn_kernel, out_shape=jax.ShapeDtypeStruct(shape, parts[0].dtype), compiler_params=room(16)
    )(*parts)


def partner_pairs(size, step):
    return [(place, place ^ step) for place in range(size)]


def swap(values, axis, step):
    return lax.ppermute(values, axis, partner_pairs(lax.axis_size(axis), step))


def start_blocks(own, count, sign):
    size = lax.axis_size("seq")
    blocks = [own]
    for pair in range(1, (count + 1) // 2 + 1):
        step = sign * 2 * pair
        pairs = [(a, a + step) for a in range(size) if 0 <= a + step < size]
        blocks.append(lax.ppermute(own, "seq", pairs))
    return blocks


def fill_blocks(evens, count, sign):
    core = lax.axis_index("seq") & 1
    blocks = [evens[0]]
    for near, far in zip(evens[:-1], evens[1:]):
        sent = jnp.where((core == 0) == (sign > 0), near, far)
        blocks += [swap(sent, "seq", 1), far]
    return blocks[: count + 1]


def core_swap(values):
    size = lax.axis_size("seq")
    groups = [[place, place + 1] for place in range(0, size, 2)]
    return lax.all_to_all(values, "seq", 0, 0, axis_index_groups=groups)


def swap_blocks(evens, count, sign):
    core = lax.axis_index("seq") & 1
    blocks = [evens[0]]
    for near, far in zip(evens[:-1], evens[1:]):
        moved = core_swap(jnp.stack([far, near] if sign > 0 else [near, far]))
        blocks += [lax.dynamic_index_in_dim(moved, 1 - core, 0, keepdims=False), far]
    return blocks[: count + 1]


def later(ready, values):
    first = jax.tree.leaves(ready)[0]
    small = lax.slice(first, (0,) * first.ndim, (1,) * (first.ndim - 2) + (8, 128))
    tied, values, _ = lax.optimization_barrier((ready, values, swap(small, "seq", 1)))
    return tied, values


def region(work, *values):
    shapes = jax.eval_shape(work, *values)

    def idle(*values):
        return jax.tree.map(lambda shape: jnp.zeros(shape.shape, shape.dtype), shapes)

    always = lax.axis_index("seq") < lax.axis_size("seq")
    return lax.cond(always, work, idle, *values)


class Order:
    def __init__(self):
        self.last = None

    def step(self, work, *values):
        if self.last is not None:
            values, _ = lax.optimization_barrier((values, self.last))
        result = work(*values)
        self.last = result
        return result


def owner_list(order, core):
    chip = lax.axis_index("seq") >> 1
    count = len(order)
    owners = []
    for place in range(1 << count):
        relative = sum(((place >> (count - 1 - at)) & 1) << (bit - 1) for at, bit in enumerate(order))
        owners.append(((chip ^ relative) << 1) | core)
    return owners


def choose(values, dim, order, core):
    size = lax.axis_size("seq")
    part = values.shape[dim] // size
    return jnp.concatenate(
        [
            lax.dynamic_slice_in_dim(values, owner * part, part, dim)
            for owner in owner_list(order, core)
        ],
        axis=dim,
    )


def cut(values, dim):
    half = values.shape[dim] // 2
    return lax.slice_in_dim(values, 0, half, axis=dim), lax.slice_in_dim(values, half, 2 * half, axis=dim)


class Piece:
    def __init__(self, kept, moved, dim, order):
        self.kept, self.dim, self.order = kept, dim, order
        self.arriving = swap(moved, "seq", 1 << order[0])
        self.done = 1

    def advance(self, steps):
        bit = self.order[self.done]
        self.done += 1

        def work(kept, arriving):
            keep, move = cut(kept, self.dim)
            arrived_keep, arrived_move = cut(arriving, self.dim)
            return keep + arrived_keep, move + arrived_move

        self.kept, moved = steps.step(work, self.kept, self.arriving)
        self.arriving = swap(moved, "seq", 1 << bit)

    def finish(self, steps):
        while self.done < len(self.order):
            self.advance(steps)
        return steps.step(lambda kept, arriving: kept + arriving, self.kept, self.arriving)


class BatchSum:
    def __init__(self, values):
        self.size = lax.axis_size("batch")
        self.values = values
        self.stage = 0
        if self.size == 4:
            self.arriving = lax.ppermute(values, "batch", [(0, 1), (3, 2)])
        else:
            self.arriving = None

    def advance(self, steps):
        if self.size != 4:
            if self.stage == 0:
                self.values = lax.psum(self.values, "batch")
        elif self.stage < 2:
            self.values = steps.step(lambda values, arriving: values + arriving, self.values, self.arriving)
            pairs = [(1, 2), (2, 1)] if self.stage == 0 else [(1, 0), (2, 3)]
            self.arriving = lax.ppermute(self.values, "batch", pairs)
        else:
            place = lax.axis_index("batch")
            middle = (place == 1) | (place == 2)
            self.values = steps.step(
                lambda values, arriving: jnp.where(middle, values, arriving), self.values, self.arriving
            )
        self.stage += 1


def norm_parts(values):
    centered = values - jnp.mean(values, axis=-1, keepdims=True)
    inverse = lax.rsqrt(jnp.mean(centered * centered, axis=-1, keepdims=True) + norm_epsilon)
    return centered * inverse, inverse


def norm_pull(grad, unit, inverse, gain):
    scaled = grad * gain
    return inverse * (
        scaled
        - jnp.mean(scaled, axis=-1, keepdims=True)
        - unit * jnp.mean(scaled * unit, axis=-1, keepdims=True)
    )


def shape_kernel(raw_kernel):
    shrunk = raw_kernel - shrink_level * jnp.tanh(raw_kernel / shrink_level)
    padded = jnp.pad(shrunk, ((1, 1), (0, 0)))
    return (padded[:-2] + padded[1:-1] + padded[2:]) / 3.0


def tap_rows(values):
    taps, features = values.shape
    return values.reshape(features, taps)


def tap_share(values):
    size = lax.axis_size("seq")
    rows, taps = values.shape
    return values.reshape(taps // size, rows * size)


def wide_dot(left, right):
    return jnp.dot(left, right, preferred_element_type=jnp.float32)


def token_dot(left, right):
    return lax.dot_general(left, right, (((0,), (0,)), ((), ())), preferred_element_type=jnp.float32)


def weight_dot(left, right):
    return lax.dot_general(left, right, (((1,), (1,)), ((), ())), preferred_element_type=jnp.float32)


def on_device(
    tokens,
    first_gain,
    first_shift,
    mixer_input,
    conv_kernel,
    mixer_output,
    second_gain,
    second_shift,
    widen_weight,
    narrow_weight,
    cotangent,
):
    axis_count = lax.axis_size("seq")
    core = lax.axis_index("seq") & 1
    other = 1 - core
    seqs_here, local_len, features = tokens.shape
    row_total = seqs_here * local_len
    tap_count = conv_kernel.shape[0]
    reach = -(-tap_count // local_len)
    block_shape = tokens.shape
    parts = 2 if seqs_here % 2 == 0 else 1
    part_shape = (seqs_here // parts, local_len, features)
    part_rows = row_total // parts
    bits = axis_count.bit_length() - 1
    down_order = list(range(bits - 1, 0, -1))
    up_order = list(range(1, bits))
    steps = Order()

    forward, inverse = half_tables(local_len)
    forward_pair = jnp.asarray(stacked_pair(forward))
    inverse_high, inverse_rest = (jnp.asarray(part) for part in split_low(inverse))
    pull_pair = jnp.asarray(stacked_pair(inverse.T))
    push_high, push_rest = (jnp.asarray(part) for part in split_low(forward.T))

    flat_tokens = tokens.reshape(row_total, features)
    flat_cot = cotangent.reshape(row_total, features)

    normed_low, key_rows, value_rows, *products = steps.step(
        lambda values: first_call(values, first_gain, first_shift, mixer_input, parts), flat_tokens
    )
    key_rows = key_rows.reshape(block_shape)
    value_rows = value_rows.reshape(block_shape)
    product_evens = [start_blocks(products[0].reshape(part_shape), reach, 1)]

    raw_kernel = conv_kernel.astype(jnp.float32)

    def filter_step(raw_kernel):
        kernel_taps = shape_kernel(raw_kernel)
        tap_blocks = jnp.pad(kernel_taps, ((0, reach * local_len - tap_count), (0, 0))).reshape(
            reach, local_len, features
        )
        table = jnp.asarray(forward.astype(np.float32))
        tap_spectra = [jnp.dot(table, tap_blocks[place], precision=highest) for place in range(reach)]
        spectra = []
        for place in range(reach + 1):
            terms = []
            if place > 0:
                terms.append(tap_spectra[place - 1])
            if place < reach:
                terms.append(turn(tap_spectra[place], local_len))
            spectra.append(sum(terms))
        return jnp.stack(spectra)

    cot_columns = steps.step(jnp.transpose, flat_cot)
    normed_columns = steps.step(lambda rows: turned_rows([rows]), normed_low)
    query_rows = steps.step(
        lambda rows, weight: wide_dot(rows, weight), normed_low, mixer_input[:, :features]
    )
    spectrum = steps.step(filter_step, raw_kernel)
    for part in products[1:]:
        part, _ = lax.optimization_barrier((part, steps.last))
        product_evens.append(start_blocks(part.reshape(part_shape), reach, 1))

    def convolve_part(at, query, spectrum, blocks):
        result = convolve_call(
            convolve_kernel,
            blocks,
            (forward_pair, inverse_high, inverse_rest),
            spectrum,
            (query,),
            (jnp.float32, low_type),
            at,
        )
        return [values.reshape(part_rows, features) for values in result]

    middle_parts, product_blocks, grad_conv, grad_evens, second_sums = None, [], [], [], []
    for at in range(parts):
        fill = swap_blocks if at == 0 else fill_blocks
        blocks = steps.step(lambda evens, fill=fill: fill(evens, reach, 1), product_evens[at])
        convolved, gated = steps.step(
            functools.partial(convolve_part, at), query_rows.reshape(block_shape), spectrum, blocks
        )
        product_blocks.append(blocks)
        *middle_parts, grad, sums = steps.step(
            lambda query, gated, convolved, earlier, at=at: middle_call(
                flat_tokens,
                flat_cot,
                mixer_output,
                second_gain,
                second_shift,
                widen_weight,
                narrow_weight,
                query,
                gated,
                convolved,
                at,
                earlier,
            ),
            query_rows,
            gated,
            convolved,
            middle_parts,
        )
        grad_conv.append(grad.reshape(part_shape))
        grad_evens.append(start_blocks(grad_conv[at], reach, -1))
        second_sums.append(sums)
    (
        second_columns,
        gated_columns,
        active_low,
        grad_hidden,
        block_output,
        grad_middle,
        grad_branch,
        grad_query,
    ) = middle_parts

    tiles = grad_hidden.shape[1] // 2 // features
    half_layouts = [[(0, 0, half * tiles + at) for at in range(tiles)] for half in range(2)]
    output_layout = [(0, 0, 0), (1, 1, 0)]
    both = (other, core)

    def dots(lefts, rights, layout, moved=None, width=features):
        return columns_call(lefts, rights, layout, width, moved, kind=pltpu.HBM)

    def widen_work(second_columns, grad_hidden):
        inner = Order()
        lefts = inner.step(
            lambda v: [choose(v, 0, order, each) for each in both for order in widen_orders], second_columns
        )
        moved = [
            swap(inner.step(lambda *pair, half=half: dots(pair[:1], pair[1:], half), left, grad_hidden), "seq", 1)
            for half, left in zip(half_layouts, lefts[:2])
        ]
        return [
            inner.step(
                lambda left, right, moved, half=half: dots([left], [right], half, moved), left, grad_hidden, part
            )
            for half, left, part in zip(half_layouts, lefts[2:], moved)
        ]

    def narrow_work(cot_columns, active, gated, normed, branch, query):
        inner = Order()
        moved = swap(
            inner.step(lambda *pair: narrow_grad(*pair, down_order, other), cot_columns, active), "seq", 1
        )
        lefts = inner.step(
            lambda *pair: [choose(values, 0, up_order, each) for each in both for values in pair],
            gated,
            normed,
        )
        moved_output = swap(
            inner.step(
                lambda lefts, *rights: dots(lefts, rights, output_layout), lefts[:2], branch, query
            ),
            "seq",
            1,
        )
        narrow = inner.step(
            lambda left, right, moved: narrow_grad(left, right, down_order, core, moved),
            cot_columns,
            active,
            moved,
        )
        output = inner.step(
            lambda lefts, branch, query, moved: dots(lefts, [branch, query], output_layout, moved),
            lefts[2:],
            branch,
            query,
            moved_output,
        )
        return narrow[:2], narrow[2:], output

    starts, flows = {}, {}

    def run(*plan):
        for name in plan:
            if name[0] == "+":
                (kept, moved), order = starts[name[1:]]
                moved, _ = lax.optimization_barrier((moved, steps.last))
                flows[name[1:]] = Piece(kept, moved, 0, order)
                continue
            flow = flows[name]
            if isinstance(flow, BatchSum):
                flow.advance(steps)
            elif flow.done < len(flow.order):
                flow.advance(steps)
            else:
                flows[name] = BatchSum(flow.finish(steps))

    widen_orders = (up_order, down_order)
    second_columns, grad_evens[0] = lax.optimization_barrier((second_columns, grad_evens[0]))
    pairs = steps.step(lambda *values: region(widen_work, *values), second_columns, grad_hidden)
    pairs, grad_evens = lax.optimization_barrier((pairs, grad_evens))
    starts["w0"], starts["w1"] = zip(pairs, widen_orders)
    run("+w0", "+w1")
    grad_evens, cot_columns = later(grad_evens, cot_columns)
    pairs = steps.step(
        lambda *values: region(narrow_work, *values),
        cot_columns,
        active_low,
        gated_columns,
        normed_columns,
        grad_branch,
        grad_query,
    )
    starts["n0"], starts["n1"], starts["o"] = zip(pairs, (down_order, down_order, up_order))
    run("w0", "w1", "+n0", "+o", "+n1")

    grad_spectrum = [
        steps.step(
            lambda grad, blocks, at=at: convolve_call(
                filter_grad_kernel, blocks, (forward_pair, pull_pair), None, (grad,), None, at
            ),
            grad_conv[at],
            product_blocks[at],
        )
        for at in range(parts)
    ]

    def taps_step(raw_kernel, *terms):
        grad_spectrum = sum(terms)
        back_table = jnp.asarray(forward.T.astype(np.float32))
        grad_taps = jnp.concatenate(
            [
                jnp.dot(
                    back_table,
                    grad_spectrum[place + 1] + turn_back(grad_spectrum[place], local_len),
                    precision=highest,
                )
                for place in range(reach)
            ]
        )[:tap_count]
        padded = jnp.pad(grad_taps, ((1, 1), (0, 0)))
        return (
            (padded[:-2] + padded[1:-1] + padded[2:]) / 3.0 * jnp.tanh(raw_kernel / shrink_level) ** 2
        )

    kernel_rows = steps.step(
        lambda *values: tap_rows(taps_step(*values)), raw_kernel, *grad_spectrum
    )

    width = features // 2
    tail_width = -(-(tap_count + 4) // width) * width
    value_layout = [(0, 0, 0)]
    key_layout = [(0, 0, at) for at in range(2)] + [(None, 1, at) for at in range(tail_width // width)]

    def pull_work(evens, spectrum, key, value):
        inner = Order()
        blocks = [fill_blocks(part, reach, -1) for part in evens]
        pulled = None
        for at in range(parts):
            pulled = inner.step(
                lambda spectrum, key, value, blocks, earlier, at=at: convolve_call(
                    pull_kernel,
                    blocks,
                    (pull_pair, push_high, push_rest),
                    spectrum,
                    (key, value),
                    (low_type, low_type),
                    at,
                    seqs_here,
                    earlier,
                ),
                spectrum,
                key,
                value,
                blocks[at],
                pulled,
            )
        return [part.reshape(row_total, features) for part in pulled]

    run("w0", "w1")
    keys, values = steps.step(
        lambda *values: region(pull_work, *values), grad_evens, spectrum, key_rows, value_rows
    )
    run("n0", "o")

    def mixer_work(keys, values, normed, query, grad_middle, kernel_rows, second_sums):
        inner = Order()
        lefts = inner.step(
            lambda v: [choose(v, 0, order, each) for each in both for order in (up_order, down_order)], normed
        )
        grad_tokens, first_sums = inner.step(
            lambda grad_middle, query, keys, values: last_call(
                flat_tokens, grad_middle, first_gain, mixer_input, query, [keys], [values]
            ),
            grad_middle,
            query,
            keys,
            values,
        )

        def tail_step(kernel_rows, first_sums, second_sums):
            rows = jnp.concatenate([first_sums[:2], second_sums[:2]], axis=0)
            tail = jnp.concatenate(
                [kernel_rows, jnp.pad(rows.T, ((0, 0), (0, tail_width - tap_count - 4)))], axis=1
            )
            return [choose(tail, 0, up_order, each) for each in both]

        tails = inner.step(tail_step, kernel_rows, first_sums, second_sums)
        moved_values = swap(
            inner.step(lambda *pair: dots(pair[:1], pair[1:], value_layout), lefts[1], values), "seq", 1
        )
        moved_keys = swap(
            inner.step(
                lambda left, *rights: dots([left], rights, key_layout, None, width), lefts[0], keys, tails[0]
            ),
            "seq",
            1,
        )
        value_pair = inner.step(
            lambda left, values, moved: dots([left], [values], value_layout, moved),
            lefts[3],
            values,
            moved_values,
        )
        key_pair = inner.step(
            lambda left, keys, tail, moved: dots([left], [keys, tail], key_layout, moved, width),
            lefts[2],
            keys,
            tails[1],
            moved_keys,
        )
        return key_pair, value_pair, grad_tokens

    key_pair, value_pair, grad_tokens = steps.step(
        lambda *values: region(mixer_work, *values),
        keys,
        values,
        normed_columns,
        grad_query,
        grad_middle,
        kernel_rows,
        sum(second_sums),
    )
    starts["k"], starts["v"] = (key_pair, up_order), (value_pair, down_order)
    run("w0", "+k", "+v", "n0", "n1", "w0", "w1", "o", "v", "n0", "w0", "w1", "n1", "k")
    run("v", "o", "n0", "w1", "k", "n1", "v", "o", "n0", "k", "n1", "v", "o", "k")
    run("n1", "v", "k")

    output_total, key_total, value_total = (flows[name].values for name in "okv")
    edge = features + tap_count
    return (
        block_output.reshape(block_shape),
        grad_tokens.reshape(block_shape),
        key_total[:, edge],
        key_total[:, edge + 1],
        jnp.concatenate([output_total[:, features:], key_total[:, :features], value_total], axis=1),
        tap_share(key_total[:, features:edge]),
        output_total[:, :features],
        key_total[:, edge + 2],
        key_total[:, edge + 3],
        jnp.concatenate([flows["w0"].values, flows["w1"].values], axis=1),
        turned_rows([flows["n0"].values[0], flows["n1"].values[0]]),
    )


def solution(mesh):
    in_specs = (
        P("batch", "seq", None),
        P(),
        P(),
        P(),
        P(),
        P(),
        P(),
        P(),
        P(),
        P(),
        P("batch", "seq", None),
    )
    out_specs = (
        P("batch", "seq", None),
        P("batch", "seq", None),
        P("seq"),
        P("seq"),
        P("seq", None),
        P("seq", None),
        P("seq", None),
        P("seq"),
        P("seq"),
        P("seq", None),
        P("seq", None),
    )
    return jax.shard_map(
        on_device, mesh=mesh, in_specs=in_specs, out_specs=out_specs, check_vma=False
    )
```
